32 devices in a mesh: section: 2 (over core), dp: 16 (over z, y, x).
Axes of the slice: x: 2, y: 2, z: 4, core: 2. Of those that a mesh axis runs over, the one named last changes fastest.
Arguments:
- tokens: bfloat16 [32, 160, 768], P('dp'), may hold values from -6 to 6
- lengths: int32 [32], P('dp'), may hold values from 95 to 160, as said below
- cotangent: bfloat16 [32, 160, 768], P('dp'), may hold values from -6 to 6
- w_qkv: bfloat16 [2, 768, 2304], P('section', 'dp'), may hold values from -0.21875 to 0.21875
- w_out: bfloat16 [2, 768, 768], P('section', 'dp'), may hold values from -0.625 to 0.625
- w_up: bfloat16 [2, 768, 3072], P('section', 'dp'), may hold values from -0.21875 to 0.21875
- w_down: bfloat16 [2, 3072, 768], P('section', 'dp'), may hold values from -0.109375 to 0.109375
- vectors: bfloat16 [2, 9216], P('section', 'dp'), may hold values from -1 to 1.75, as said below
Outputs:
- acts: float32 [2, 32, 160, 768], P('section', 'dp')
- grad_in: float32 [2, 32, 160, 768], P('section', 'dp')
- grad_qkv: float32 [2, 768, 2304], P('section', 'dp')
- grad_out: float32 [2, 768, 768], P('section', 'dp')
- grad_up: float32 [2, 768, 3072], P('section', 'dp')
- grad_down: float32 [2, 3072, 768], P('section', 'dp')
- grad_vectors: float32 [2, 9216], P('section', 'dp')
The draws below stay inside these ranges and needn't reach their ends.
Inputs may be any that keep to these rules, and one draw needn't show every extreme that they name: `lengths`: some chain has exactly 160 residues and some exactly 95. `vectors`: entries 3 * 768 to 3072 and 4608 to 5376 of each layer are norm gains, the others biases.
All inputs are finite; a program needn't handle non-finite values.
Results may differ from the reference program's by a relative error of at most 0.015.
Values may be sent and summed in bfloat16 or wider, within the bound.
No kernel may reach another device: no remote copies, remote signals or barrier semaphores. Data moves between devices by JAX's collectives and lax.ppermute only.
A program may use at most 192 MiB of HBM per device.

```python
import jax
import jax.numpy as jnp
from jax import lax

D = 768
HEADS = 12
HEAD = 64
FF = 3072
L = 160
MIN_LEN = 95
CHAINS_DEV = 2
CHAINS = 32


def draw_lengths(key, part):
    key = jax.random.fold_in(key, 11)
    subkeys = jax.random.split(key, 4)
    devices = CHAINS // CHAINS_DEV
    floors = jax.random.randint(subkeys[0], (devices, 1), MIN_LEN, L + 1)
    spread = jax.random.randint(subkeys[1], (devices, CHAINS_DEV), 0, 1 << 20)
    lengths_all = (floors + spread % (L + 1 - floors)).reshape(CHAINS)
    highest = jax.random.randint(subkeys[2], (), 0, CHAINS)
    offset_draw = jax.random.randint(subkeys[3], (), 1, CHAINS)
    lowest = (highest + offset_draw) % CHAINS
    lengths_all = lengths_all.at[highest].set(L).at[lowest].set(MIN_LEN)
    return lengths_all.astype(jnp.int32)


def draw_vectors(key, part):
    key = jax.random.fold_in(key, 23)
    first_key, second_key = jax.random.split(key)
    total_len = 8 * D + FF
    column = jnp.arange(total_len)
    is_gain = (column >= 3 * D) & (column < 4 * D) | (column >= 6 * D) & (column < 7 * D)
    biases = jnp.clip(0.3 * jax.random.normal(first_key, (2, total_len), jnp.float32), -1.0, 1.0)
    gains = jax.random.uniform(second_key, (2, total_len), jnp.float32, 0.5, 1.5)
    return jnp.where(is_gain[None, :], gains, biases).astype(jnp.bfloat16)


def level_of(rng, extent, shards, smallest, top_value):
    level, own = 1.0, jax.random.fold_in(rng, 6)
    for dim, parts in shards:
        heights = jnp.exp(jax.random.uniform(jax.random.fold_in(own, dim), (parts,), jnp.float32, smallest / len(shards), top_value / len(shards)))
        level = level * jnp.repeat(heights, extent[dim] // parts).reshape([-1 if axis == dim else 1 for axis in range(len(extent))])
    return level


def gaussian(own_key, dims, scale, bound, cuts=(), kind=jnp.bfloat16):
    values = jax.random.normal(own_key, dims, jnp.float32) * scale
    if len(cuts) > 0:
        values = level_of(own_key, dims, cuts, -0.22, 0.18) * values
    return jnp.clip(values, min=-bound, max=bound).astype(kind)


def setup_inputs(seed: int = 0) -> dict:
    keys = jax.random.split(jax.random.key(seed), 9)
    return {
        "tokens": gaussian(keys[0], (CHAINS, L, D), 1.0, 6.0, ((0, 16),)),
        "lengths": draw_lengths(jax.random.fold_in(keys[8], 71), 0),
        "cotangent": gaussian(keys[2], (CHAINS, L, D), 1.0, 6.0, ((0, 16),)),
        "w_qkv": gaussian(keys[3], (2, D, 3 * D), D ** -0.5, 0.21875, ((0, 2), (1, 16))),
        "w_out": gaussian(keys[4], (2, D, D), (D // 8) ** -0.5, 0.625, ((0, 2), (1, 16))),
        "w_up": gaussian(keys[5], (2, D, FF), D ** -0.5, 0.21875, ((0, 2), (1, 16))),
        "w_down": gaussian(keys[6], (2, FF, D), FF ** -0.5, 0.109375, ((0, 2), (1, 16))),
        "vectors": draw_vectors(jax.random.fold_in(keys[8], 71), 0),
    }


@jax.custom_vjp
def low(v):
    return lax.optimization_barrier(v.astype(jnp.bfloat16)).astype(jnp.float32)

@jax.custom_vjp
def low_back(v):
    return v

def low_keep(v):
    return (low(v), None)

def low_pass(kept, grad):
    return (grad,)

def back_keep(v):
    return (v, None)

def back_low(kept, grad):
    return (low(grad),)
low.defvjp(low_keep, low_pass)
low_back.defvjp(back_keep, back_low)
highest = lax.Precision.HIGHEST
eps_norm = 1e-06

def norm_apply(resid, norm_gain, norm_shift):
    row_mean = lax.optimization_barrier(jnp.mean(resid, axis=-1, keepdims=True))
    centered = resid - row_mean
    variance = lax.optimization_barrier(jnp.mean(centered * centered, axis=-1, keepdims=True))
    return centered * lax.rsqrt(variance + eps_norm) * norm_gain + norm_shift

def layer_apply(layer_in, weight_qkv, weight_out, weight_up, weight_down, flat_vec, key_valid):
    model_width = weight_out.shape[0]
    pieces = [flat_vec[position * model_width:(position + 1) * model_width] for position in range(8)]
    bias_q, bias_v, bias_o, gain_one, shift_one, bias_down, gain_two, shift_two = pieces
    bias_up = flat_vec[8 * model_width:]
    chains, length = (layer_in.shape[0], layer_in.shape[1])
    flat_rows = layer_in.reshape(-1, model_width)
    projected = jnp.dot(flat_rows, weight_qkv, precision=highest)
    head_shape = (chains, length, HEADS, HEAD)
    queries = low_back(low(projected[:, :model_width] + bias_q)).reshape(head_shape)
    keys_low = low_back(low(projected[:, model_width:2 * model_width])).reshape(head_shape)
    values = low_back(low(projected[:, 2 * model_width:] + bias_v)).reshape(head_shape)
    dot_scores = jnp.einsum('bqhe,bkhe->bhqk', queries, keys_low, precision=highest) * HEAD ** (-0.5)
    scores = low_back(jnp.where(key_valid[:, None, None, :], dot_scores, -1000000000.0))
    row_max = lax.optimization_barrier(jnp.max(scores, axis=-1, keepdims=True))
    shifted_exp = jnp.exp(scores - row_max)
    soft = low(shifted_exp / lax.optimization_barrier(jnp.sum(shifted_exp, axis=-1, keepdims=True)))
    mixed = jnp.einsum('bhqk,bkhe->bqhe', soft, values, precision=highest).reshape(-1, model_width)
    mixed = low_back(low(mixed))
    branch = low_back(jnp.dot(mixed, weight_out, precision=highest) + bias_o)
    hidden = norm_apply(flat_rows + branch, gain_one, shift_one)
    hidden_low = low(hidden)
    pre_act = low_back(jnp.dot(hidden_low, weight_up, precision=highest) + bias_up)
    act_low = low(jax.nn.gelu(pre_act, approximate=False))
    branch_ff = low_back(jnp.dot(act_low, weight_down, precision=highest) + bias_down)
    return norm_apply(hidden + branch_ff, gain_two, shift_two).reshape(layer_in.shape)

def reference(tokens, lengths, cotangent, w_qkv, w_out, w_up, w_down, vectors):
    params = tuple((item.astype(jnp.float32) for item in (w_qkv, w_out, w_up, w_down, vectors)))
    group_count = CHAINS // CHAINS_DEV
    token_groups = tokens.reshape(group_count, CHAINS_DEV, L, D)
    length_groups = lengths.reshape(group_count, CHAINS_DEV)
    cot_groups = cotangent.reshape(group_count, CHAINS_DEV, L, D)

    def one_group(totals, inputs):
        token_part, length_part, cot_part = inputs
        key_valid = jnp.arange(L)[None, :] < length_part[:, None]
        start = token_part.astype(jnp.float32)
        probe = jnp.zeros_like(start)

        def forward(start_in, probe_in, p_qkv, p_out, p_up, p_down, p_vec):
            first_out = layer_apply(start_in, p_qkv[0], p_out[0], p_up[0], p_down[0], p_vec[0], key_valid)
            passed = low_back(low(first_out)) + probe_in
            final_out = layer_apply(passed, p_qkv[1], p_out[1], p_up[1], p_down[1], p_vec[1], key_valid)
            return (final_out, first_out)
        final_out, pull_back, first_out = jax.vjp(forward, start, probe, params[0], params[1], params[2], params[3], params[4], has_aux=True)
        pulled_grad = jnp.where(key_valid[..., None], cot_part.astype(jnp.float32), 0.0)
        grads = pull_back(pulled_grad)
        new_totals = tuple((total + grad for total, grad in zip(totals, grads[2:])))
        return (new_totals, (jnp.stack([first_out, final_out]), jnp.stack([grads[0], grads[1]])))
    initial = tuple((jnp.zeros(item.shape, jnp.float32) for item in params))
    totals, (act_groups, grad_groups) = lax.scan(one_group, initial, (token_groups, length_groups, cot_groups))
    acts = jnp.moveaxis(act_groups, 1, 0).reshape(2, CHAINS, L, D)
    grad_in = jnp.moveaxis(grad_groups, 1, 0).reshape(2, CHAINS, L, D)
    return (acts, grad_in, totals[0], totals[1], totals[2], totals[3], totals[4])
```

```python
import functools

import jax
import jax.numpy as jnp
from jax import lax
from jax.experimental import pallas as pl
from jax.experimental.pallas import tpu as pltpu
from jax.sharding import PartitionSpec as P

HEADS = 12
BF = jnp.bfloat16
F32 = jnp.float32
EPS = 1e-06
FILL = -1000000000.0
ROOT_HALF = 0.7071067811865476
INV_ROOT_TWO_PI = 0.3989422804014327
VMEM_BYTES = 40 * 1024 * 1024
ALL = ("section", "dp")


def nn(a, b):
    return lax.dot_general(a, b, (((1,), (0,)), ((), ())), preferred_element_type=F32)


def nt(a, b):
    return lax.dot_general(a, b, (((1,), (1,)), ((), ())), preferred_element_type=F32)


def tn(a, b):
    return lax.dot_general(a, b, (((0,), (0,)), ((), ())), preferred_element_type=F32)


def norm(r, gain, shift):
    mean = jnp.mean(r, axis=-1, keepdims=True)
    cent = r - mean
    inv = lax.rsqrt(jnp.mean(cent * cent, axis=-1, keepdims=True) + EPS)
    n = cent * inv
    return n * gain + shift, n, inv


def norm_back(dy, n, inv, gain):
    t = dy * gain
    dr = inv * (
        t - jnp.mean(t, axis=-1, keepdims=True) - n * jnp.mean(t * n, axis=-1, keepdims=True)
    )
    return dr, jnp.sum(dy * n, axis=0, keepdims=True), jnp.sum(dy, axis=0, keepdims=True)


def span(info, side, slot, blocks, stacked, rows):
    half = info[0] if side == 0 else 1 - info[0]
    owner = info[2 + blocks * side + slot]
    if stacked:
        at = pl.multiple_of(owner * rows, 16)
        return (pl.ds(2 * half, 2), pl.ds(at, rows), slice(None))
    at = pl.multiple_of(owner * (2 * rows) + half * rows, 16)
    return (pl.ds(at, rows), slice(None))


def load_weight(info, parts, dst, sem, stacked):
    if len(parts) == 1:
        copy = pltpu.make_async_copy(parts[0], dst, sem)
        copy.start()
        return copy
    blocks = sum(part.shape[0] for part in parts) // 2
    rows = parts[0].shape[-2]
    slot = 0
    for part in parts:
        for s in range(part.shape[0]):
            side, at = divmod(slot, blocks)
            window = span(info, side, at, blocks, stacked, rows)
            pltpu.make_async_copy(part.at[s], dst.at[window], sem).start()
            slot += 1
    return pltpu.make_async_copy(dst, dst, sem)


def store_grad(info, src, outs, sem, stacked):
    if len(outs) == 1:
        copy = pltpu.make_async_copy(src, outs[0], sem)
        copy.start()
        return copy
    blocks = outs[0].shape[0]
    rows = outs[0].shape[-2]
    for side in (1, 0):
        for s in range(blocks):
            window = span(info, side, s, blocks, stacked, rows)
            pltpu.make_async_copy(src.at[window], outs[side].at[s], sem).start()
    return pltpu.make_async_copy(src, src, sem)


def attention_forward(n_w, info, x, vec, *refs):
    parts, refs = refs[:n_w], refs[n_w:]
    qkv, soft, mixed, hidden, normed, inv, w, sem = refs
    load_weight(info, parts, w, sem, True).wait()
    xb = x[...]
    length, width = xb.shape
    q = (nn(xb, w[0]) + vec[0:1]).astype(BF)
    k = nn(xb, w[1]).astype(BF)
    v = (nn(xb, w[2]) + vec[1:2]).astype(BF)
    qkv[0] = q
    qkv[1] = k
    qkv[2] = v
    size = width // HEADS
    pair = 2 * size
    low_half = lax.broadcasted_iota(jnp.int32, (length, pair), 1) < size
    valid = lax.broadcasted_iota(jnp.int32, (length, length), 1) < info[1]
    for p in range(HEADS // 2):
        at = slice(p * pair, (p + 1) * pair)
        qp, kp, vp = q[:, at], k[:, at], v[:, at]
        sides = []
        for e in range(2):
            qm = jnp.where(low_half if e == 0 else ~low_half, qp, jnp.zeros_like(qp))
            s = jnp.where(valid, nt(qm, kp) * size ** (-0.5), FILL)
            ex = jnp.exp(s - jnp.max(s, axis=-1, keepdims=True))
            a = ex / jnp.sum(ex, axis=-1, keepdims=True)
            soft[2 * p + e] = a
            sides.append(nn(a.astype(BF), vp))
        mixed[:, at] = jnp.where(low_half, sides[0], sides[1]).astype(BF)
    r = xb.astype(F32) + (nn(mixed[...], w[3]) + vec[2:3])
    hidden[...], normed[...], inv[...] = norm(r, vec[3:4], vec[4:5])


def up_forward(n_w, info, hidden, vec, *refs):
    parts, refs = refs[:n_w], refs[n_w:]
    act, slope, w, sem = refs
    load_weight(info, parts, w, sem, True).wait()
    hb = hidden[...].astype(BF)
    for j in range(4):
        u = nn(hb, w[j]) + vec[8 + j : 9 + j]
        cdf = 0.5 * (1.0 + lax.erf(u * ROOT_HALF))
        act[j] = (u * cdf).astype(BF)
        slope[j] = cdf + u * INV_ROOT_TWO_PI * jnp.exp(-0.5 * u * u)


def down_forward(n_w, info, act, hidden, vec, *refs):
    parts, refs = refs[:n_w], refs[n_w:]
    out, normed, inv, w, sem = refs
    load_weight(info, parts, w, sem, False).wait()
    depth = act.shape[2]
    total = nn(act[0], w[:depth])
    for j in range(1, 4):
        total += nn(act[j], w[j * depth : (j + 1) * depth])
    r = hidden[...] + (total + vec[5:6])
    out[...], normed[...], inv[...] = norm(r, vec[6:7], vec[7:8])


def down_backward(first, n_w, n_g, info, dy, normed, inv, act, slope, vec, *refs):
    parts, refs = refs[:n_w], refs[n_w:]
    outs, refs = refs[:n_g], refs[n_g:]
    dr, du, dvec, w, dw, sems = refs
    load = load_weight(info, parts, w, sems.at[0], False)
    g = dy[...].astype(F32)
    if not first:
        rows = lax.broadcasted_iota(jnp.int32, g.shape, 0)
        g = jnp.where(rows < info[1], g, 0.0)
    grad, dgain, dshift = norm_back(g, normed[...], inv[...], vec[6:7])
    dr[...] = grad
    dz = grad.astype(BF)
    dvec[0:1] = jnp.sum(dz.astype(F32), axis=0, keepdims=True)
    dvec[1:2] = dgain
    dvec[2:3] = dshift
    dvec[7:8] = jnp.zeros_like(dshift)
    depth = act.shape[2]
    for j in range(4):
        dw[j * depth : (j + 1) * depth] = tn(act[j], dz).astype(BF)
    store = store_grad(info, dw, outs, sems.at[1], False)
    load.wait()
    for j in range(4):
        back = nt(dz, w[j * depth : (j + 1) * depth])
        low = (back * slope[j]).astype(BF)
        du[j] = low
        dvec[3 + j : 4 + j] = jnp.sum(low.astype(F32), axis=0, keepdims=True)
    store.wait()


def up_backward(n_w, n_g, info, du, dr, hidden, normed, inv, vec, *refs):
    parts, refs = refs[:n_w], refs[n_w:]
    outs, refs = refs[:n_g], refs[n_g:]
    dr1, dvec, w, dw, sems = refs
    load = load_weight(info, parts, w, sems.at[0], True)
    hb = hidden[...].astype(BF)
    for j in range(4):
        dw[j] = tn(hb, du[j]).astype(BF)
    store = store_grad(info, dw, outs, sems.at[1], True)
    load.wait()
    dh = dr[...]
    for j in range(4):
        dh += nt(du[j], w[j])
    grad, dgain, dshift = norm_back(dh, normed[...], inv[...], vec[3:4])
    dr1[...] = grad
    dvec[0:1] = jnp.sum(grad.astype(BF).astype(F32), axis=0, keepdims=True)
    dvec[1:2] = dgain
    dvec[2:3] = dshift
    dvec[3:8] = jnp.zeros((5, dshift.shape[1]), F32)
    store.wait()


def attention_backward(n_w, n_g, info, dr1, x, qkv, soft, mixed, *refs):
    parts, refs = refs[:n_w], refs[n_w:]
    outs, refs = refs[:n_g], refs[n_g:]
    dx, dvec, w, dw, dp, sems = refs
    load = load_weight(info, parts, w, sems.at[0], True)
    db = dr1[...].astype(BF)
    dw[3] = tn(mixed[...], db).astype(BF)
    load.wait()
    do = nt(db, w[3]).astype(BF)
    length, width = do.shape
    size = width // HEADS
    pair = 2 * size
    scale = size ** (-0.5)
    low_half = lax.broadcasted_iota(jnp.int32, (length, pair), 1) < size
    for p in range(HEADS // 2):
        at = slice(p * pair, (p + 1) * pair)
        qp, kp, vp, dop = qkv[0, :, at], qkv[1, :, at], qkv[2, :, at], do[:, at]
        dqs, dks, dvs = [], [], []
        for e in range(2):
            dom = jnp.where(low_half if e == 0 else ~low_half, dop, jnp.zeros_like(dop))
            a = soft[2 * p + e]
            da = nt(dom, vp)
            ds = (a * (da - jnp.sum(a * da, axis=-1, keepdims=True))).astype(BF)
            dvs.append(tn(a.astype(BF), dop))
            dqs.append(nn(ds, kp))
            dks.append(tn(ds, qp))
        dp[0, :, at] = (jnp.where(low_half, dqs[0], dqs[1]) * scale).astype(BF)
        dp[1, :, at] = (jnp.where(low_half, dks[0], dks[1]) * scale).astype(BF)
        dp[2, :, at] = jnp.where(low_half, dvs[0], dvs[1]).astype(BF)
    xb = x[...]
    for j in range(3):
        dw[j] = tn(xb, dp[j]).astype(BF)
    store = store_grad(info, dw, outs, sems.at[1], True)
    total = dr1[...]
    for j in range(3):
        total += nt(dp[j], w[j])
    dx[...] = total
    dvec[0:1] = jnp.sum(dp[0].astype(F32), axis=0, keepdims=True)
    dvec[1:2] = jnp.sum(dp[2].astype(F32), axis=0, keepdims=True)
    dvec[2:8] = jnp.zeros((6, width), F32)
    store.wait()


def call(kernel, info, small, parts, grads, outs, scratch, flops, nbytes):
    vmem = pl.BlockSpec(memory_space=pltpu.VMEM)
    hbm = pl.BlockSpec(memory_space=pl.ANY)
    shapes = [jax.ShapeDtypeStruct(s, BF) for s in grads]
    shapes += [jax.ShapeDtypeStruct(s, d) for s, d in outs]
    return pl.pallas_call(
        kernel,
        out_shape=shapes,
        in_specs=[pl.BlockSpec(memory_space=pltpu.SMEM)]
        + [vmem] * len(small)
        + [hbm] * len(parts),
        out_specs=[hbm] * len(grads) + [vmem] * len(outs),
        scratch_shapes=scratch,
        compiler_params=pltpu.CompilerParams(vmem_limit_bytes=VMEM_BYTES),
        cost_estimate=pl.CostEstimate(flops=flops, bytes_accessed=nbytes, transcendentals=0),
    )(info, *small, *parts)


class Layer:
    def __init__(self, info, vec, length, width):
        self.info, self.vec = info, vec
        self.length, self.width = length, width
        self.row = ((length, width), F32)
        self.col = ((length, 1), F32)
        self.wide = (4, length, width)
        self.size = 2 * length * width * width
        self.stack = pltpu.VMEM((4, width, width), BF)
        self.tall = pltpu.VMEM((4 * width, width), BF)
        self.bytes = 4 * width * width * 2
        self.sem = pltpu.SemaphoreType.DMA
        self.dvec = ((8, width), F32)

    def attention(self, x, parts):
        self.x = x
        low = ((self.length, self.width), BF)
        outs = [((3,) + low[0], BF), ((HEADS, self.length, self.length), F32), low]
        outs += [self.row, self.row, self.col]
        self.qkv, self.soft, self.mixed, self.hidden, self.n1, self.s1 = call(
            functools.partial(attention_forward, len(parts)), self.info, [x, self.vec], parts,
            [], outs, [self.stack, self.sem], 5 * self.size, self.bytes,
        )

    def up(self, parts):
        self.act, self.slope = call(
            functools.partial(up_forward, len(parts)), self.info, [self.hidden, self.vec], parts,
            [], [(self.wide, BF), (self.wide, F32)], [self.stack, self.sem],
            4 * self.size, self.bytes,
        )

    def down(self, parts):
        out, self.n2, self.s2 = call(
            functools.partial(down_forward, len(parts)), self.info,
            [self.act, self.hidden, self.vec], parts,
            [], [self.row, self.row, self.col], [self.tall, self.sem], 4 * self.size, self.bytes,
        )
        return out

    def down_back(self, first, dy, parts, grads):
        got = call(
            functools.partial(down_backward, first, len(parts), len(grads)), self.info,
            [dy, self.n2, self.s2, self.act, self.slope, self.vec], parts, grads,
            [self.row, (self.wide, BF), self.dvec],
            [self.tall, self.tall, self.sem((2,))], 8 * self.size, 2 * self.bytes,
        )
        self.dr, self.du, self.dvec_down = got[len(grads) :]
        return got[: len(grads)]

    def up_back(self, parts, grads):
        got = call(
            functools.partial(up_backward, len(parts), len(grads)), self.info,
            [self.du, self.dr, self.hidden, self.n1, self.s1, self.vec], parts, grads,
            [self.row, self.dvec],
            [self.stack, self.stack, self.sem((2,))], 8 * self.size, 2 * self.bytes,
        )
        self.dr1, self.dvec_up = got[len(grads) :]
        return got[: len(grads)]

    def attention_back(self, parts, grads):
        got = call(
            functools.partial(attention_backward, len(parts), len(grads)), self.info,
            [self.dr1, self.x, self.qkv, self.soft, self.mixed], parts, grads,
            [self.row, self.dvec],
            [self.stack, self.stack, pltpu.VMEM((3, self.length, self.width), BF), self.sem((2,))],
            11 * self.size, 2 * self.bytes,
        )
        self.dx, self.dvec_att = got[len(grads) :]
        return got[: len(grads)]

    def grad_vec(self):
        d, u, a = self.dvec_down, self.dvec_up, self.dvec_att
        return jnp.concatenate([a[0:2], u[0:3], d[0:7]], axis=0)


def route(move):
    size = lax.axis_size("dp")
    pairs = []
    for s in range(2):
        for d in range(size):
            to_s, to_d = move(s, d)
            pairs.append((s * size + d, to_s * size + to_d))
    return pairs


def send(v, pairs):
    return lax.ppermute(v, ALL, pairs)


def after(v, *others):
    return lax.optimization_barrier((v,) + others)[0]


def cube_routes():
    return (
        route(lambda s, d: (s, d ^ 4)),
        route(lambda s, d: (s, d ^ 8)),
        route(lambda s, d: (s, d ^ (1 if s == 0 else 2))),
        route(lambda s, d: (s, d ^ (2 if s == 0 else 1))),
    )


def cube_owners(core, me):
    slot = jnp.arange(16)
    third = jnp.where(core == 0, 1, 2)

    def table(a, b):
        bits = [(slot >> i) & 1 for i in range(4)]
        return me ^ (bits[0] * 4 + bits[1] * 8 + bits[2] * a + bits[3] * b)

    return jnp.concatenate([table(third, 3 - third), table(3 - third, third)]).astype(jnp.int32)


def swap_route():
    return route(lambda s, d: (1 - s, d))


def cube_body(tokens, lengths, cotangent, w_qkv, w_out, w_up, w_down, vectors):
    core = lax.axis_index("section")
    me = lax.axis_index("dp")
    first = core == 0
    _, length, width = tokens.shape
    rows = w_out.shape[1]
    z_low, z_high, third, last = cube_routes()
    swap = swap_route()

    def chunks(w):
        return jnp.stack([w[:, j * width : (j + 1) * width] for j in range(w.shape[1] // width)])

    own = jnp.stack(
        [
            jnp.concatenate([chunks(w_qkv[0]), w_out]),
            chunks(w_up[0]),
            w_down[0].reshape(4, rows, width),
        ]
    )
    mine = lax.dynamic_slice_in_dim(own, 2 * core, 2, 1)
    other = lax.dynamic_slice_in_dim(own, 2 * (1 - core), 2, 1)
    other = send(other, swap)
    zero = jnp.where(first, mine, other)
    one = jnp.where(first, other, mine)
    blocks = [half[p] for half in (zero, one) for p in range(3)]

    vec = jnp.stack([vectors[0], send(vectors[0], swap)])
    vec = jnp.where(first, vec, vec[::-1])[None]
    for bit, pairs in ((0, route(lambda s, d: (s, d ^ 1))), (1, route(lambda s, d: (s, d ^ 2))),
                       (2, z_low), (3, z_high)):
        got = send(vec, pairs)
        upper = (me >> bit) & 1 == 1
        vec = jnp.where(upper, jnp.concatenate([got, vec]), jnp.concatenate([vec, got]))
    vec = vec.transpose(1, 0, 2).reshape(2, -1, width).astype(F32)

    info = jnp.concatenate([core[None], lengths[core][None], cube_owners(core, me)])
    info = info.astype(jnp.int32)
    layers = [Layer(info, vec[l], length, width) for l in range(2)]

    count = len(blocks)
    low, pairs2, high, quads, cross, eights, rest = {}, {}, {}, {}, {}, {}, {}
    swapped, late = {}, {}
    low[0] = send(blocks[0], z_low)
    low[1] = send(blocks[1], z_low)
    pairs2[0] = jnp.stack([blocks[0], low[0]])
    high[0] = send(pairs2[0], z_high)
    for p in range(count):
        quads[p] = jnp.concatenate([pairs2[p], high[p]])
        cross[p] = send(quads[p], third)
        if p + 1 < count:
            pairs2[p + 1] = jnp.stack([blocks[p + 1], low[p + 1]])
            high[p + 1] = send(after(pairs2[p + 1], quads[p]), z_high)
        if p + 2 < count:
            low[p + 2] = send(after(blocks[p + 2], quads[p]), z_low)
        eights[p] = jnp.concatenate([quads[p], cross[p]])
        rest[p] = send(eights[p], last)
        swapped[p] = send(eights[p], swap)
        late[p] = send(rest[p], swap)

    def parts(p):
        got = [eights[p], rest[p], swapped[p], late[p]]
        if p % 3 == 2:
            got = [a.reshape(8, 2 * rows, width) for a in got]
        return got

    x = lax.dynamic_index_in_dim(tokens, core, 0, keepdims=False)
    cot = lax.dynamic_index_in_dim(cotangent, core, 0, keepdims=False)
    results = []
    for l in range(2):
        layer = layers[l]
        layer.attention(x, parts(3 * l))
        layer.up(parts(3 * l + 1))
        y = layer.down(parts(3 * l + 2))
        results.append(y)
        x = y.astype(BF)

    stacked = [(16, 2, rows, width)] * 2
    tall = [(16, 2 * rows, width)] * 2

    def add(a, b):
        return (a.astype(F32) + b.astype(F32)).astype(BF)

    def reduce(keep, give):
        keep = keep.reshape(16, 2, rows, width)
        got = send(give.reshape(16, 2, rows, width), swap)
        for n, pairs in ((8, last), (4, third), (2, z_high), (1, z_low)):
            out = add(keep[n:], got[n:])
            keep = add(keep[:n], got[:n])
            got = send(out, pairs)
        return keep[0].astype(F32) + got[0].astype(F32)

    sums = {}
    dy = cot
    dxs = {}
    for l in (1, 0):
        layer = layers[l]
        sums[l, 2] = reduce(*layer.down_back(l == 0, dy, parts(3 * l + 2), tall))
        sums[l, 1] = reduce(*layer.up_back(parts(3 * l + 1), stacked))
        sums[l, 0] = reduce(*layer.attention_back(parts(3 * l), stacked))
        dxs[l] = layer.dx
        dy = layer.dx.astype(BF)

    def by_layer(a, b):
        keep = jnp.where(first, a, b)
        got = send(jnp.where(first, b, a), swap)
        return keep, got

    def chains(a, b):
        keep, got = by_layer(a, b)
        return jnp.where(first, jnp.stack([keep, got]), jnp.stack([got, keep]))[None]

    acts = chains(*results)
    grads_in = chains(dxs[0], dxs[1])
    whole = []
    for p in range(3):
        keep, got = by_layer(sums[0, p], sums[1, p])
        whole.append(jnp.where(first, jnp.concatenate([keep, got]), jnp.concatenate([got, keep])))

    def side_by_side(stack):
        return jnp.concatenate([stack[j] for j in range(stack.shape[0])], axis=1)[None]

    keep, got = by_layer(layers[0].grad_vec(), layers[1].grad_vec())
    total = (keep + got).reshape(16, -1)
    for bit, pairs in ((3, z_high), (2, z_low), (1, route(lambda s, d: (s, d ^ 2))),
                       (0, route(lambda s, d: (s, d ^ 1)))):
        n = 1 << bit
        mine_at = ((me >> bit) & 1) * n
        give = lax.dynamic_slice_in_dim(total, n - mine_at, n, 0)
        total = lax.dynamic_slice_in_dim(total, mine_at, n, 0) + send(give, pairs)
    return (
        acts,
        grads_in,
        side_by_side(whole[0][:3]),
        whole[0][3][None],
        side_by_side(whole[1]),
        whole[2].reshape(1, 4 * rows, width),
        total,
    )


def plain_body(tokens, lengths, cotangent, w_qkv, w_out, w_up, w_down, vectors):
    core = lax.axis_index("section")
    first = core == 0
    chains_dev, length, width = tokens.shape
    swap = swap_route()
    size = lax.axis_size("dp")
    rows = w_out.shape[1]

    def gathered(w):
        return lax.all_gather(w, "dp", axis=0, tiled=True)

    def both(v):
        got = send(v, swap)
        return jnp.where(first, v, got), jnp.where(first, got, v)

    def chunks(w):
        return jnp.stack([w[:, j * width : (j + 1) * width] for j in range(w.shape[1] // width)])

    att = jnp.concatenate([chunks(gathered(w_qkv[0])), gathered(w_out[0])[None]])
    up = chunks(gathered(w_up[0]))
    down = gathered(w_down[0])
    vec = gathered(vectors[0]).reshape(-1, width).astype(F32)
    att, up, down, vec = both(att), both(up), both(down), both(vec)
    info = jnp.stack([core, lengths[core]]).astype(jnp.int32)
    layers = [Layer(info, vec[l], length, width) for l in range(2)]
    x = lax.dynamic_index_in_dim(tokens, core, 0, keepdims=False)
    dy = lax.dynamic_index_in_dim(cotangent, core, 0, keepdims=False)
    results = []
    for l in range(2):
        layers[l].attention(x, [att[l]])
        layers[l].up([up[l]])
        y = layers[l].down([down[l]])
        results.append(y)
        x = y.astype(BF)
    stacked, tall = [(4, width, width)], [(4 * width, width)]
    grads = {}
    dxs = {}
    for l in (1, 0):
        layer = layers[l]
        (grads[l, 2],) = layer.down_back(l == 0, dy, [down[l]], tall)
        (grads[l, 1],) = layer.up_back([up[l]], stacked)
        (grads[l, 0],) = layer.attention_back([att[l]], stacked)
        dxs[l] = layer.dx
        dy = layer.dx.astype(BF)

    def by_layer(a, b):
        return jnp.where(first, a, b), send(jnp.where(first, b, a), swap)

    def chains(a, b):
        keep, got = by_layer(a, b)
        return jnp.where(first, jnp.stack([keep, got]), jnp.stack([got, keep]))[None]

    def summed(a, b):
        keep, got = by_layer(a, b)
        total = (keep.astype(F32) + got.astype(F32)).astype(keep.dtype)
        dim = total.ndim - 2 if total.ndim > 1 else 0
        got = lax.psum_scatter(total, "dp", scatter_dimension=dim, tiled=True)
        return got.astype(F32)

    def side_by_side(stack):
        return jnp.concatenate([stack[j] for j in range(stack.shape[0])], axis=1)[None]

    g_att = summed(grads[0, 0], grads[1, 0])
    g_up = summed(grads[0, 1], grads[1, 1])
    g_down = summed(grads[0, 2], grads[1, 2])
    g_vec = summed(layers[0].grad_vec().reshape(-1), layers[1].grad_vec().reshape(-1))
    return (
        chains(*results),
        chains(dxs[0], dxs[1]),
        side_by_side(g_att[:3]),
        g_att[3][None],
        side_by_side(g_up),
        g_down[None],
        g_vec[None],
    )


def solution(mesh):
    placed = (
        P("dp", None, None),
        P("dp"),
        P("dp", None, None),
        P("section", "dp", None),
        P("section", "dp", None),
        P("section", "dp", None),
        P("section", "dp", None),
        P("section", "dp"),
    )
    return jax.shard_map(
        cube_body if mesh.shape["dp"] == 16 else plain_body,
        mesh=mesh,
        in_specs=placed,
        out_specs=(
            P("section", "dp", None, None),
            P("section", "dp", None, None),
            P("section", "dp", None),
            P("section", "dp", None),
            P("section", "dp", None),
            P("section", "dp", None),
            P("section", "dp"),
        ),
        check_vma=False,
    )
```

```python
import functools

import jax
import jax.numpy as jnp
from jax import lax
from jax.experimental import pallas as pl
from jax.experimental.pallas import tpu as pltpu
from jax.sharding import PartitionSpec as P

HEADS = 12
BF = jnp.bfloat16
F32 = jnp.float32
EPS = 1e-06
FILL = -1000000000.0
ROOT_HALF = 0.7071067811865476
INV_ROOT_TWO_PI = 0.3989422804014327
VMEM_BYTES = 24 * 1024 * 1024
ALL = ("section", "dp")
WINDOW = 1


def nn(a, b):
    return lax.dot_general(a, b, (((1,), (0,)), ((), ())), preferred_element_type=F32)


def nt(a, b):
    return lax.dot_general(a, b, (((1,), (1,)), ((), ())), preferred_element_type=F32)


def tn(a, b):
    return lax.dot_general(a, b, (((0,), (0,)), ((), ())), preferred_element_type=F32)


def norm(r, gain, shift):
    mean = jnp.mean(r, axis=-1, keepdims=True)
    cent = r - mean
    inv = lax.rsqrt(jnp.mean(cent * cent, axis=-1, keepdims=True) + EPS)
    n = cent * inv
    return n * gain + shift, n, inv


def norm_back(dy, n, inv, gain):
    t = dy * gain
    dr = inv * (
        t - jnp.mean(t, axis=-1, keepdims=True) - n * jnp.mean(t * n, axis=-1, keepdims=True)
    )
    return dr, jnp.sum(dy * n, axis=0, keepdims=True), jnp.sum(dy, axis=0, keepdims=True)


def load_weight(info, parts, dst, sem, stacked):
    if len(parts) == 1:
        copy = pltpu.make_async_copy(parts[0], dst, sem)
        copy.start()
        return copy
    blocks = sum(part.shape[0] for part in parts) // 2
    rows = parts[0].shape[-2]
    slot = 0
    for part in parts:
        for s in range(part.shape[0]):
            half = info[0] if slot < blocks else 1 - info[0]
            at = pl.ds(pl.multiple_of(info[2 + slot] * rows, 16), rows)
            window = (pl.ds(2 * half, 2) if stacked else half, at)
            pltpu.make_async_copy(part.at[s], dst.at[window], sem).start()
            slot += 1
    return pltpu.make_async_copy(dst, dst, sem)


def store_grad(info, src, outs, sem, stacked):
    if len(outs) == 1:
        copy = pltpu.make_async_copy(src, outs[0], sem)
        copy.start()
        return copy
    near = outs[1].shape[0]
    rows = outs[0].shape[-2]
    for out, base in ((outs[0], near), (outs[1], 0)):
        for s in range(out.shape[0]):
            at = pl.ds(pl.multiple_of(info[2 + base + s] * rows, 16), rows)
            window = (slice(None), at) if stacked else (at,)
            pltpu.make_async_copy(src.at[window], out.at[s], sem).start()
    return pltpu.make_async_copy(src, src, sem)


def attention_forward(n_w, info, x, vec, *refs):
    parts, refs = refs[:n_w], refs[n_w:]
    qkv, soft, mixed, hidden, hidden_low, normed, inv, w, sem = refs
    load_weight(info, parts, w, sem, True).wait()
    xb = x[...]
    length, width = xb.shape
    q = (nn(xb, w[0]) + vec[0:1]).astype(BF)
    k = nn(xb, w[1]).astype(BF)
    v = (nn(xb, w[2]) + vec[1:2]).astype(BF)
    qkv[0] = q
    qkv[1] = k
    qkv[2] = v
    size = width // HEADS
    pair = 2 * size
    low_half = lax.broadcasted_iota(jnp.int32, (length, pair), 1) < size
    valid = lax.broadcasted_iota(jnp.int32, (length, length), 1) < info[1]
    for p in range(HEADS // 2):
        at = slice(p * pair, (p + 1) * pair)
        qp, kp, vp = q[:, at], k[:, at], v[:, at]
        sides = []
        for e in range(2):
            qm = jnp.where(low_half if e == 0 else ~low_half, qp, jnp.zeros_like(qp))
            s = jnp.where(valid, nt(qm, kp) * size ** (-0.5), FILL)
            ex = jnp.exp(s - jnp.max(s, axis=-1, keepdims=True))
            a = ex / jnp.sum(ex, axis=-1, keepdims=True)
            soft[2 * p + e] = a
            sides.append(nn(a.astype(BF), vp))
        mixed[:, at] = jnp.where(low_half, sides[0], sides[1]).astype(BF)
    r = xb.astype(F32) + (nn(mixed[...], w[3]) + vec[2:3])
    h, normed[...], inv[...] = norm(r, vec[3:4], vec[4:5])
    hidden[...] = h
    hidden_low[...] = h.astype(BF)


def up_forward(n_w, info, hidden_low, vec, *refs):
    parts, refs = refs[:n_w], refs[n_w:]
    act, slope, w, sem = refs
    load_weight(info, parts, w, sem, True).wait()
    hb = hidden_low[...]
    for j in range(4):
        u = nn(hb, w[j]) + vec[8 + j : 9 + j]
        cdf = 0.5 * (1.0 + lax.erf(u * ROOT_HALF))
        act[j] = (u * cdf).astype(BF)
        slope[j] = cdf + u * INV_ROOT_TWO_PI * jnp.exp(-0.5 * u * u)


def down_forward(n_w, info, act, hidden, vec, *refs):
    parts, refs = refs[:n_w], refs[n_w:]
    out, normed, inv, w, sem = refs
    load_weight(info, parts, w, sem, False).wait()
    depth = act.shape[2]
    halves = []
    for h in range(2):
        total = nn(act[0], w[h, :depth])
        for j in range(1, 4):
            total += nn(act[j], w[h, j * depth : (j + 1) * depth])
        halves.append(total)
    r = hidden[...] + (jnp.concatenate(halves, axis=1) + vec[5:6])
    out[...], normed[...], inv[...] = norm(r, vec[6:7], vec[7:8])


def down_backward(first, n_w, info, dy, normed, inv, slope, vec, *refs):
    parts, refs = refs[:n_w], refs[n_w:]
    dr, dz_keep, dz_give, du, du_give, dvec, w, sem = refs
    load = load_weight(info, parts, w, sem, False)
    g = dy[...].astype(F32)
    if not first:
        rows = lax.broadcasted_iota(jnp.int32, g.shape, 0)
        g = jnp.where(rows < info[1], g, 0.0)
    grad, dgain, dshift = norm_back(g, normed[...], inv[...], vec[6:7])
    dr[...] = grad
    dz = grad.astype(BF)
    dvec[0:1] = jnp.sum(dz.astype(F32), axis=0, keepdims=True)
    dvec[1:2] = dgain
    dvec[2:3] = dshift
    dvec[7:8] = jnp.zeros_like(dshift)
    half = dz.shape[1] // 2
    left, right = dz[:, :half], dz[:, half:]
    on_left = info[0] == 0
    dz_keep[...] = jnp.where(on_left, left, right)
    dz_give[...] = jnp.where(on_left, right, left)
    depth = dz.shape[1]
    load.wait()
    for j in range(4):
        at = slice(j * depth, (j + 1) * depth)
        low = ((nt(left, w[0, at]) + nt(right, w[1, at])) * slope[j]).astype(BF)
        du[j] = low
        dvec[3 + j : 4 + j] = jnp.sum(low.astype(F32), axis=0, keepdims=True)
    for j in range(2):
        du_give[j] = du[2 * (1 - info[0]) + j]


def up_backward(n_w, info, du, dr, normed, inv, vec, *refs):
    parts, refs = refs[:n_w], refs[n_w:]
    dr1, dvec, w, sem = refs
    load_weight(info, parts, w, sem, True).wait()
    dh = dr[...]
    for j in range(4):
        dh += nt(du[j], w[j])
    grad, dgain, dshift = norm_back(dh, normed[...], inv[...], vec[3:4])
    dr1[...] = grad
    dvec[0:1] = jnp.sum(grad.astype(BF).astype(F32), axis=0, keepdims=True)
    dvec[1:2] = dgain
    dvec[2:3] = dshift
    dvec[3:8] = jnp.zeros((5, dshift.shape[1]), F32)


def attention_backward(n_w, info, dr1, qkv, soft, *refs):
    parts, refs = refs[:n_w], refs[n_w:]
    dx, side, side_give, dvec, w, sem = refs
    load = load_weight(info, parts, w, sem, True)
    db = dr1[...].astype(BF)
    load.wait()
    do = nt(db, w[3]).astype(BF)
    length, width = do.shape
    size = width // HEADS
    pair = 2 * size
    scale = size ** (-0.5)
    low_half = lax.broadcasted_iota(jnp.int32, (length, pair), 1) < size
    for p in range(HEADS // 2):
        at = slice(p * pair, (p + 1) * pair)
        qp, kp, vp, dop = qkv[0, :, at], qkv[1, :, at], qkv[2, :, at], do[:, at]
        dqs, dks, dvs = [], [], []
        for e in range(2):
            dom = jnp.where(low_half if e == 0 else ~low_half, dop, jnp.zeros_like(dop))
            a = soft[2 * p + e]
            da = nt(dom, vp)
            ds = (a * (da - jnp.sum(a * da, axis=-1, keepdims=True))).astype(BF)
            dvs.append(tn(a.astype(BF), dop))
            dqs.append(nn(ds, kp))
            dks.append(tn(ds, qp))
        side[0, :, at] = (jnp.where(low_half, dqs[0], dqs[1]) * scale).astype(BF)
        side[1, :, at] = (jnp.where(low_half, dks[0], dks[1]) * scale).astype(BF)
        side[2, :, at] = jnp.where(low_half, dvs[0], dvs[1]).astype(BF)
    side[3] = db
    total = dr1[...]
    for j in range(3):
        total += nt(side[j], w[j])
    dx[...] = total
    dvec[0:1] = jnp.sum(side[0].astype(F32), axis=0, keepdims=True)
    dvec[1:2] = jnp.sum(side[2].astype(F32), axis=0, keepdims=True)
    dvec[2:8] = jnp.zeros((6, width), F32)
    for j in range(2):
        side_give[j] = side[2 * (1 - info[0]) + j]


def down_weight(info, act, act_other, dz, dz_other, *refs):
    outs, (dw, sem) = refs[:-2], refs[-2:]
    right = jnp.concatenate([dz[...], dz_other[...]], axis=0)
    depth = act.shape[2]
    for j in range(4):
        left = jnp.concatenate([act[j], act_other[j]], axis=0)
        dw[j * depth : (j + 1) * depth] = tn(left, right).astype(BF)
    store_grad(info, dw, outs, sem, False).wait()


def up_weight(info, hidden, hidden_other, du, du_other, *refs):
    outs, (dw, sem) = refs[:-2], refs[-2:]
    left = jnp.concatenate([hidden[...], hidden_other[...]], axis=0)
    for j in range(2):
        right = jnp.concatenate([du[2 * info[0] + j], du_other[j]], axis=0)
        dw[j] = tn(left, right).astype(BF)
    store_grad(info, dw, outs, sem, True).wait()


def attention_weight(info, x, x_other, mixed, mixed_other, side, side_other, *refs):
    outs, (dw, sem) = refs[:-2], refs[-2:]
    left = jnp.concatenate([x[...], x_other[...]], axis=0)
    last = jnp.concatenate([mixed[...], mixed_other[...]], axis=0)
    for j in range(2):
        right = jnp.concatenate([side[2 * info[0] + j], side_other[j]], axis=0)
        if j == 1:
            left = jnp.where(info[0] == 0, left, last)
        dw[j] = tn(left, right).astype(BF)
    store_grad(info, dw, outs, sem, True).wait()


def call(kernel, info, small, parts, grads, outs, scratch, flops, nbytes):
    vmem = pl.BlockSpec(memory_space=pltpu.VMEM)
    hbm = pl.BlockSpec(memory_space=pl.ANY)
    shapes = [jax.ShapeDtypeStruct(s, BF) for s in grads]
    shapes += [jax.ShapeDtypeStruct(s, d) for s, d in outs]
    return pl.pallas_call(
        kernel,
        out_shape=shapes,
        in_specs=[pl.BlockSpec(memory_space=pltpu.SMEM)]
        + [vmem] * len(small)
        + [hbm] * len(parts),
        out_specs=[hbm] * len(grads) + [vmem] * len(outs),
        scratch_shapes=scratch,
        compiler_params=pltpu.CompilerParams(vmem_limit_bytes=VMEM_BYTES),
        cost_estimate=pl.CostEstimate(flops=1, bytes_accessed=1, transcendentals=0),
    )(info, *small, *parts)


class Layer:
    def __init__(self, info, vec, length, width):
        self.info, self.vec = info, vec
        self.length, self.width = length, width
        self.row = ((length, width), F32)
        self.low = ((length, width), BF)
        self.col = ((length, 1), F32)
        self.wide = (4, length, width)
        self.two = ((2, length, width), BF)
        self.half = ((length, width // 2), BF)
        self.size = 2 * length * width * width
        self.stack = pltpu.VMEM((4, width, width), BF)
        self.tall = pltpu.VMEM((2, 4 * width, width // 2), BF)
        self.bytes = 4 * width * width * 2
        self.sem = pltpu.SemaphoreType.DMA
        self.dvec = ((8, width), F32)
        self.other = {}

    def run(self, kernel, parts, small, outs, scratch, mults, grads=()):
        if parts:
            kernel = functools.partial(kernel, len(parts))
        return call(
            kernel, self.info, small, parts, grads, outs, scratch + [self.sem],
            mults * self.size, self.bytes,
        )

    def attention(self, x, parts):
        self.x = x
        outs = [((3,) + self.low[0], BF), ((HEADS, self.length, self.length), F32), self.low]
        outs += [self.row, self.low, self.row, self.col]
        got = self.run(attention_forward, parts, [x, self.vec], outs, [self.stack], 5)
        self.qkv, self.soft, self.mixed, self.hidden, self.hidden_low, self.n1, self.s1 = got
        return self.hidden_low

    def up(self, hidden_low, parts):
        self.act, self.slope = self.run(
            up_forward, parts, [hidden_low, self.vec], [(self.wide, BF), (self.wide, F32)],
            [self.stack], 4,
        )
        return self.act

    def down(self, act, parts):
        out, self.n2, self.s2 = self.run(
            down_forward, parts, [act, self.hidden, self.vec], [self.row, self.row, self.col],
            [self.tall], 4,
        )
        return out

    def down_back(self, first, dy, parts):
        got = self.run(
            functools.partial(down_backward, first), parts,
            [dy, self.n2, self.s2, self.slope, self.vec],
            [self.row, self.half, self.half, (self.wide, BF), self.two, self.dvec],
            [self.tall], 4,
        )
        self.dr, self.dz, dz_give, self.du, du_give, self.dvec_down = got
        return dz_give, du_give

    def up_back(self, parts):
        self.dr1, self.dvec_up = self.run(
            up_backward, parts, [self.du, self.dr, self.n1, self.s1, self.vec],
            [self.row, self.dvec], [self.stack], 4,
        )

    def attention_back(self, dr1, parts):
        self.dx, self.side, give, self.dvec_att = self.run(
            attention_backward, parts, [dr1, self.qkv, self.soft],
            [self.row, (self.wide, BF), self.two, self.dvec], [self.stack], 7,
        )
        return give

    def weight(self, kind, grads):
        o = self.other
        stack = pltpu.VMEM((2, self.width, self.width), BF)
        if kind == 2:
            stack = pltpu.VMEM((4 * self.width, self.width // 2), BF)
            small, kernel = [self.act, o["act"], self.dz, o["dz"]], down_weight
        elif kind == 1:
            small = [self.hidden_low, o["hidden"], self.du, o["du"]]
            kernel = up_weight
        else:
            small = [self.x, o["x"], self.mixed, o["mixed"], self.side, o["side"]]
            kernel = attention_weight
        return self.run(kernel, [], small, [], [stack], 4, grads)

    def grad_vec(self):
        d, u, a = self.dvec_down, self.dvec_up, self.dvec_att
        return jnp.concatenate([a[0:2], u[0:3], d[0:7]], axis=0)


def route(move):
    size = lax.axis_size("dp")
    pairs = []
    for s in range(2):
        for d in range(size):
            to_s, to_d = move(s, d)
            pairs.append((s * size + d, to_s * size + to_d))
    return pairs


def send(v, pairs):
    return lax.ppermute(v, ALL, pairs)


def after(v, *others):
    return lax.optimization_barrier((v,) + others)[0]


def cube_routes():
    return (
        route(lambda s, d: (s, d ^ (1 if s == 0 else 2))),
        route(lambda s, d: (s, d ^ (2 if s == 0 else 1))),
    )


def cube_owners(core, me):
    slot = jnp.arange(16)
    third = jnp.where(core == 0, 1, 2)

    def table(a, b):
        bits = [(slot >> i) & 1 for i in range(4)]
        return me ^ (bits[0] * 8 + bits[1] * 4 + bits[2] * a + bits[3] * b)

    return jnp.concatenate([table(third, 3 - third), table(3 - third, third)]).astype(jnp.int32)


def swap_route():
    return route(lambda s, d: (1 - s, d))


def cube_body(tokens, lengths, cotangent, w_qkv, w_out, w_up, w_down, vectors):
    core = lax.axis_index("section")
    me = lax.axis_index("dp")
    first = core == 0
    _, length, width = tokens.shape
    rows = w_out.shape[1]
    third, last = cube_routes()
    swap = swap_route()
    z_routes = {
        j: route(lambda s, d, m=m: (s, d ^ m)) for j, m in ((1, 8), (2, 4), (3, 12))
    }
    vec_sum_routes = [route(lambda s, d, i=i: (s, d ^ (1 << i))) for i in range(4)]

    def chunks(w):
        return jnp.stack([w[:, j * width : (j + 1) * width] for j in range(w.shape[1] // width)])

    own = (
        jnp.concatenate([chunks(w_qkv[0]), w_out]),
        chunks(w_up[0]),
        jnp.stack([w_down[0][:, : width // 2], w_down[0][:, width // 2 :]]),
    )
    blocks = [None] * 6

    def split(p):
        n = own[p].shape[0] // 2
        mine = lax.dynamic_slice_in_dim(own[p], n * core, n, 0)
        other = lax.dynamic_slice_in_dim(own[p], n * (1 - core), n, 0)
        return (mine, other) if n > 1 else (mine[0], other[0])

    def place(p, mine, other):
        blocks[p] = jnp.where(first, mine, other)
        blocks[p + 3] = jnp.where(first, other, mine)

    info = jnp.concatenate([core[None], lengths[core][None], cube_owners(core, me)])
    info = info.astype(jnp.int32)
    layers = [Layer(info, None, length, width) for l in range(2)]

    x = lax.dynamic_index_in_dim(tokens, core, 0, keepdims=False)
    layers[0].other["x"] = lax.dynamic_index_in_dim(tokens, 1 - core, 0, keepdims=False)
    cot = lax.dynamic_index_in_dim(cotangent, core, 0, keepdims=False)

    history = [[], []]
    now = []

    def tie(*values, extra=()):
        deps = history[WINDOW] + list(extra)
        return lax.optimization_barrier(tuple(values) + tuple(deps))[: len(values)]

    def sends(items, extra=()):
        values = tie(*[v for v, _ in items], extra=extra)
        got = [send(v, pairs) for v, (_, pairs) in zip(values, items)]
        now.extend(got)
        return got

    def step_end():
        history[:] = [history[1], list(now)]
        now[:] = []

    parts = {}
    results = []
    exchange = []

    def forward(p, v):
        l, kind = divmod(p, 3)
        layer = layers[l]
        (v,) = tie(v)
        if kind == 0:
            if l == 1:
                exchange.append((l, "x", v))
            v = layer.attention(v, parts[p])
            exchange.append((l, "mixed", layer.mixed))
            exchange.append((l, "hidden", layer.hidden_low))
        elif kind == 1:
            v = layer.up(v, parts[p])
            exchange.append((l, "act", v))
        else:
            v = layer.down(v, parts[p])
            results.append(v)
            v = v.astype(BF)
        now.append(v)
        return v

    twos, quads, eights, rest, swapped = {}, {}, {}, {}, {}
    n = len(blocks)
    vec = jnp.stack([vectors[0], send(vectors[0], swap)])
    vec = jnp.where(first, vec, vec[::-1])
    third_bit = jnp.where(first, 0, 1)
    vec_stages = {
        -1: (3, z_routes[1]),
        0: (2, z_routes[2]),
        1: (third_bit, third),
        2: (1 - third_bit, last),
    }
    mine, other = split(0)
    place(0, mine, send(other, swap))
    for t in range(-1, n + 3):
        todo = []
        if 0 <= t - 2 < n:
            todo.append(("rest", t - 2, eights[t - 2], last))
        if 0 <= t - 1 < n:
            todo.append(("cross", t - 1, quads[t - 1], third))
        if 0 <= t < n:
            todo.append(("low", t, twos[t], z_routes[2]))
        if t + 1 < n:
            todo.append(("high", t + 1, blocks[t + 1], z_routes[1]))
        if 0 <= t - 3 < n:
            todo.append(("late", t - 3, rest[t - 3], swap))
        if 0 <= t - 2 < n:
            todo.append(("swapped", t - 2, eights[t - 2], swap))
        if t == -1:
            halves = [split(1), split(2)]
            todo += [("own", p, halves[p - 1][1], swap) for p in (1, 2)]
        if t in vec_stages:
            todo.append(("vec", t, vec, vec_stages[t][1]))
        for l, name, v in exchange:
            todo.append((name, l, v, swap))
        exchange.clear()
        early = [i for i, item in enumerate(todo) if item[0] not in ("low", "high") or t < 3]
        late = [i for i in range(len(todo)) if i not in early]
        got = [None] * len(todo)
        for i, v in zip(early, sends([todo[i][2:] for i in early])):
            got[i] = v
            if todo[i][0] == "late":
                q = todo[i][1]
                parts[q] = [eights[q], rest[q], swapped[q], v]
        if t >= 3:
            x = forward(t - 3, x)
        if late:
            for i, v in zip(late, sends([todo[i][2:] for i in late], [x])):
                got[i] = v
        new = {}
        for (name, q, _, _), v in zip(todo, got):
            if name == "rest":
                rest[q] = v
            elif name in ("cross", "low", "high"):
                new[name] = v
            elif name == "late":
                pass
            elif name == "swapped":
                swapped[q] = v
            elif name == "own":
                place(q, halves[q - 1][0], v)
            elif name == "vec":
                upper = (me >> vec_stages[q][0]) & 1 == 1
                vec = jnp.where(upper, jnp.stack([v, vec]), jnp.stack([vec, v]))
                if q == 2:
                    a, b = (vec.transpose(4, 3, 2, i, 1 - i, 5) for i in (0, 1))
                    vec = jnp.where(first, a, b).reshape(2, -1, width).astype(F32)
                    layers[0].vec, layers[1].vec = vec[0], vec[1]
            else:
                layers[q].other[name] = v
        step_end()
        if "high" in new:
            twos[t + 1] = jnp.stack([blocks[t + 1], new["high"]])
        if "low" in new:
            quads[t] = jnp.concatenate([twos[t], new["low"]])
        if "cross" in new:
            eights[t - 1] = jnp.concatenate([quads[t - 1], new["cross"]])

    order = [(l, kind) for l in (1, 0) for kind in (2, 1, 0)]
    dxs = {}

    def chain(l, kind):
        layer = layers[l]
        if kind == 2:
            dy = cot if l == 1 else dxs[1].astype(BF)
            (dy,) = tie(dy)
            dz, du = layer.down_back(l == 0, dy, parts[3 * l + 2])
            layer.other["dz"], layer.other["du"] = send(dz, swap), send(du, swap)
            now.append(layer.dr)
        elif kind == 1:
            layer.up_back(parts[3 * l + 1])
            now.append(layer.dr1)
        else:
            (dr1,) = tie(layer.dr1)
            layer.other["side"] = send(layer.attention_back(dr1, parts[3 * l]), swap)
            dxs[l] = layer.dx
            now.append(layer.dx)

    def weight(l, kind):
        shape = (8,) + blocks[kind].shape
        give, keep = layers[l].weight(kind, [shape, shape])
        terms.append([keep])
        gives.append(give)
        now.extend([give, keep])

    terms, gives = [], []
    work = [
        [(chain, 1, 2), (chain, 1, 1), (weight, 1, 2)],
        [(chain, 1, 0), (weight, 1, 1)],
        [(weight, 1, 0), (chain, 0, 2)],
        [(chain, 0, 1), (weight, 0, 2)],
        [(chain, 0, 0), (weight, 0, 1)],
        [(weight, 0, 0)],
    ]

    def part(q, lo, hi, kind):
        total = terms[q][0][lo:hi].astype(F32)
        for v in terms[q][1:]:
            total = total + v[lo:hi].astype(F32)
        return total.astype(kind)

    def by_layer(a, b):
        return jnp.where(first, a, b), jnp.where(first, b, a)

    sums, out_keep, out_got = {}, {}, {}
    pending = []
    vec_sum = None
    acts_keep, acts_give = by_layer(*results)
    extra = [("acts", acts_give)]
    kept = {"acts": acts_keep}
    got_extra = {}
    t = 0
    while t < len(order) + 4:
        todo = []
        if 0 <= t - 1 < 6:
            todo.append(("last", t - 1, gives[t - 1], last))
        if 0 <= t - 2 < 6:
            todo.append(("third", t - 2, part(t - 2, 4, 8, BF), third))
        if 0 <= t - 3 < 6:
            for j in (1, 2, 3):
                todo.append(("z", t - 3, part(t - 3, j, j + 1, BF), z_routes[j]))
        for name, v in extra:
            todo.append((name, 0, v, swap))
        extra = []
        if vec_sum is not None and vec_sum[0] >= 0:
            bit, vec_give = vec_sum[0], vec_sum[2]
            todo.append(("vec", 0, vec_give, swap if bit == 4 else vec_sum_routes[bit]))
        early = [item for item in todo if item[0] != "z" or t >= len(work)]
        late = [item for item in todo if item[0] == "z" and t < len(work)]
        todo = early + late
        got = sends([item[2:] for item in early])
        if t < len(work):
            for f, l, kind in work[t]:
                f(l, kind)
        if late:
            got = got + sends([item[2:] for item in late], now[-1:])
        step_end()
        final = None
        for (name, q, _, _), v in zip(todo, got):
            if name in ("last", "third"):
                terms[q].append(v)
            elif name == "z":
                if final is None:
                    final = part(q, 0, 1, F32)[0]
                final = final + v[0].astype(F32)
                sums[order[q]] = final
            elif name == "vec":
                bit, keep_v = vec_sum[0], vec_sum[1]
                total = keep_v + v
                if bit == 4:
                    total = total.reshape(16, -1)
                if bit > 0:
                    m = 1 << (bit - 1)
                    at = ((me >> (bit - 1)) & 1) * m
                    vec_sum = (
                        bit - 1,
                        lax.dynamic_slice_in_dim(total, at, m, 0),
                        lax.dynamic_slice_in_dim(total, m - at, m, 0),
                    )
                else:
                    vec_sum = (-1, None, None)
                    total_vec = total
            else:
                got_extra[name] = v
        if t == 4:
            keep_v, give_v = by_layer(layers[0].grad_vec(), layers[1].grad_vec())
            vec_sum = (4, keep_v, give_v)
            kept["dx"], give_v = by_layer(dxs[0], dxs[1])
            extra.append(("dx", give_v))
        if 0 <= t - 3 < 6 and order[t - 3][0] == 0:
            kind = order[t - 3][1]
            kept[kind], give_v = by_layer(sums[0, kind], sums[1, kind])
            extra.append((kind, give_v))
        t += 1

    def joined(name, axis):
        a, b = kept[name], got_extra[name]
        if axis is None:
            return jnp.where(first, jnp.stack([a, b]), jnp.stack([b, a]))
        return jnp.where(first, jnp.concatenate([a, b], axis), jnp.concatenate([b, a], axis))

    acts = joined("acts", None)[None]
    grads_in = joined("dx", None)[None]
    whole = [joined(0, 0), joined(1, 0), joined(2, 1)]

    def side_by_side(stack):
        return jnp.concatenate([stack[j] for j in range(stack.shape[0])], axis=1)[None]

    return (
        acts,
        grads_in,
        side_by_side(whole[0][:3]),
        whole[0][3][None],
        side_by_side(whole[1]),
        whole[2][None],
        total_vec,
    )


def plain_body(tokens, lengths, cotangent, w_qkv, w_out, w_up, w_down, vectors):
    core = lax.axis_index("section")
    first = core == 0
    chains_dev, length, width = tokens.shape
    swap = swap_route()
    size = lax.axis_size("dp")
    rows = w_out.shape[1]

    def gathered(w):
        return lax.all_gather(w, "dp", axis=0, tiled=True)

    def both(v):
        got = send(v, swap)
        return jnp.where(first, v, got), jnp.where(first, got, v)

    def chunks(w):
        return jnp.stack([w[:, j * width : (j + 1) * width] for j in range(w.shape[1] // width)])

    att = jnp.concatenate([chunks(gathered(w_qkv[0])), gathered(w_out[0])[None]])
    up = chunks(gathered(w_up[0]))
    down = gathered(w_down[0])
    down = jnp.stack([down[:, : width // 2], down[:, width // 2 :]])
    vec = gathered(vectors[0]).reshape(-1, width).astype(F32)
    att, up, down, vec = both(att), both(up), both(down), both(vec)
    info = jnp.stack([core, lengths[core]]).astype(jnp.int32)
    layers = [Layer(info, vec[l], length, width) for l in range(2)]
    x = lax.dynamic_index_in_dim(tokens, core, 0, keepdims=False)
    dy = lax.dynamic_index_in_dim(cotangent, core, 0, keepdims=False)
    results = []
    for l in range(2):
        layer = layers[l]
        layer.other["x"] = send(x, swap)
        hidden = layer.attention(x, [att[l]])
        act = layer.up(hidden, [up[l]])
        layer.other["mixed"], layer.other["hidden"] = send(layer.mixed, swap), send(hidden, swap)
        layer.other["act"] = send(act, swap)
        y = layer.down(act, [down[l]])
        results.append(y)
        x = y.astype(BF)
    stacked, tall = [(2, width, width)], [(4 * width, width // 2)]
    grads = {}
    dxs = {}
    for l in (1, 0):
        layer = layers[l]
        dz, du = layer.down_back(l == 0, dy, [down[l]])
        layer.other["dz"], layer.other["du"] = send(dz, swap), send(du, swap)
        layer.up_back([up[l]])
        layer.other["side"] = send(layer.attention_back(layer.dr1, [att[l]]), swap)
        for kind in range(3):
            (grads[l, kind],) = layer.weight(kind, tall if kind == 2 else stacked)
        dxs[l] = layer.dx
        dy = layer.dx.astype(BF)

    def by_layer(a, b):
        return jnp.where(first, a, b), send(jnp.where(first, b, a), swap)

    def chains(a, b):
        keep, got = by_layer(a, b)
        return jnp.where(first, jnp.stack([keep, got]), jnp.stack([got, keep]))[None]

    def scattered(total):
        dim = total.ndim - 2 if total.ndim > 1 else 0
        return lax.psum_scatter(total, "dp", scatter_dimension=dim, tiled=True).astype(F32)

    def summed(kind, axis):
        keep, got = by_layer(scattered(grads[0, kind]), scattered(grads[1, kind]))
        left, right = jnp.where(first, keep, got), jnp.where(first, got, keep)
        return jnp.concatenate([left, right], axis)

    def side_by_side(stack):
        return jnp.concatenate([stack[j] for j in range(stack.shape[0])], axis=1)[None]

    g_att, g_up, g_down = summed(0, 0), summed(1, 0), summed(2, 1)
    keep, got = by_layer(layers[0].grad_vec(), layers[1].grad_vec())
    g_vec = scattered((keep + got).reshape(-1))
    return (
        chains(*results),
        chains(dxs[0], dxs[1]),
        side_by_side(g_att[:3]),
        g_att[3][None],
        side_by_side(g_up),
        g_down[None],
        g_vec[None],
    )


def solution(mesh):
    placed = (
        P("dp", None, None),
        P("dp"),
        P("dp", None, None),
        P("section", "dp", None),
        P("section", "dp", None),
        P("section", "dp", None),
        P("section", "dp", None),
        P("section", "dp"),
    )
    return jax.shard_map(
        cube_body if mesh.shape["dp"] == 16 else plain_body,
        mesh=mesh,
        in_specs=placed,
        out_specs=(
            P("section", "dp", None, None),
            P("section", "dp", None, None),
            P("section", "dp", None),
            P("section", "dp", None),
            P("section", "dp", None),
            P("section", "dp", None),
            P("section", "dp"),
        ),
        check_vma=False,
    )
```

```python
import functools

import jax
import jax.numpy as jnp
from jax import lax
from jax.experimental import pallas as pl
from jax.experimental.pallas import tpu as pltpu
from jax.sharding import PartitionSpec as P

HEADS = 12
BF = jnp.bfloat16
F32 = jnp.float32
EPS = 1e-06
FILL = -1000000000.0
ROOT_HALF = 0.7071067811865476
INV_ROOT_TWO_PI = 0.3989422804014327
VMEM_BYTES = 24 * 1024 * 1024
ALL = ("section", "dp")
WINDOW = 1
DIRECT = 2
FLAT_GATHER = {3: 0, 5: 3}
FLAT_SUM = {0: 4, 1: 7}


def nn(a, b):
    return lax.dot_general(a, b, (((1,), (0,)), ((), ())), preferred_element_type=F32)


def nt(a, b):
    return lax.dot_general(a, b, (((1,), (1,)), ((), ())), preferred_element_type=F32)


def tn(a, b):
    return lax.dot_general(a, b, (((0,), (0,)), ((), ())), preferred_element_type=F32)


def norm(r, gain, shift):
    mean = jnp.mean(r, axis=-1, keepdims=True)
    cent = r - mean
    inv = lax.rsqrt(jnp.mean(cent * cent, axis=-1, keepdims=True) + EPS)
    n = cent * inv
    return n * gain + shift, n, inv


def norm_back(dy, n, inv, gain):
    t = dy * gain
    dr = inv * (
        t - jnp.mean(t, axis=-1, keepdims=True) - n * jnp.mean(t * n, axis=-1, keepdims=True)
    )
    return dr, jnp.sum(dy * n, axis=0, keepdims=True), jnp.sum(dy, axis=0, keepdims=True)


def load_weight(info, parts, dst, sem, stacked):
    if len(parts) == 1:
        copy = pltpu.make_async_copy(parts[0], dst, sem)
        copy.start()
        return copy
    blocks = sum(part.shape[0] for part in parts) // 2
    rows = parts[0].shape[-2]
    slot = 0
    for part in parts:
        for s in range(part.shape[0]):
            half = info[0] if slot < blocks else 1 - info[0]
            at = pl.ds(pl.multiple_of(info[2 + slot] * rows, 16), rows)
            if stacked:
                window = (pl.ds(2 * half, 2), at)
            else:
                cols = part.shape[-1]
                window = (at, pl.ds(pl.multiple_of(half * cols, 128), cols))
            pltpu.make_async_copy(part.at[s], dst.at[window], sem).start()
            slot += 1
    return pltpu.make_async_copy(dst, dst, sem)


def store_grad(info, src, outs, sem, stacked):
    if len(outs) == 1:
        copy = pltpu.make_async_copy(src, outs[0], sem)
        copy.start()
        return copy
    near = outs[1].shape[0]
    rows = outs[0].shape[-2]
    for out, base in ((outs[0], near), (outs[1], 0)):
        for s in range(out.shape[0]):
            at = pl.ds(pl.multiple_of(info[2 + base + s] * rows, 16), rows)
            window = (slice(None), at) if stacked else (at,)
            pltpu.make_async_copy(src.at[window], out.at[s], sem).start()
    return pltpu.make_async_copy(src, src, sem)


def attention_forward(n_w, info, x, vec, *refs):
    parts, refs = refs[:n_w], refs[n_w:]
    qkv, soft, mixed, hidden, hidden_low, normed, inv, w, sem = refs
    load_weight(info, parts, w, sem, True).wait()
    xb = x[...]
    length, width = xb.shape
    q = (nn(xb, w[0]) + vec[0:1]).astype(BF)
    k = nn(xb, w[1]).astype(BF)
    v = (nn(xb, w[2]) + vec[1:2]).astype(BF)
    qkv[0] = q
    qkv[1] = k
    qkv[2] = v
    size = width // HEADS
    pair = 2 * size
    low_half = lax.broadcasted_iota(jnp.int32, (length, pair), 1) < size
    valid = lax.broadcasted_iota(jnp.int32, (length, length), 1) < info[1]
    for p in range(HEADS // 2):
        at = slice(p * pair, (p + 1) * pair)
        qp, kp, vp = q[:, at], k[:, at], v[:, at]
        sides = []
        for e in range(2):
            qm = jnp.where(low_half if e == 0 else ~low_half, qp, jnp.zeros_like(qp))
            s = jnp.where(valid, nt(qm, kp) * size ** (-0.5), FILL)
            ex = jnp.exp(s - jnp.max(s, axis=-1, keepdims=True))
            a = ex / jnp.sum(ex, axis=-1, keepdims=True)
            soft[2 * p + e] = a
            sides.append(nn(a.astype(BF), vp))
        mixed[:, at] = jnp.where(low_half, sides[0], sides[1]).astype(BF)
    r = xb.astype(F32) + (nn(mixed[...], w[3]) + vec[2:3])
    h, normed[...], inv[...] = norm(r, vec[3:4], vec[4:5])
    hidden[...] = h
    hidden_low[...] = h.astype(BF)


def up_forward(n_w, info, hidden_low, vec, *refs):
    parts, refs = refs[:n_w], refs[n_w:]
    act, slope, w, sem = refs
    load_weight(info, parts, w, sem, True).wait()
    hb = hidden_low[...]
    for j in range(4):
        u = nn(hb, w[j]) + vec[8 + j : 9 + j]
        cdf = 0.5 * (1.0 + lax.erf(u * ROOT_HALF))
        act[:, j * u.shape[1] : (j + 1) * u.shape[1]] = (u * cdf).astype(BF)
        slope[j] = cdf + u * INV_ROOT_TWO_PI * jnp.exp(-0.5 * u * u)


def down_forward(n_w, info, act, hidden, vec, *refs):
    parts, refs = refs[:n_w], refs[n_w:]
    out, normed, inv, w, sem = refs
    load_weight(info, parts, w, sem, False).wait()
    r = hidden[...] + (nn(act[...], w[...]) + vec[5:6])
    out[...], normed[...], inv[...] = norm(r, vec[6:7], vec[7:8])


def down_backward(first, n_w, info, dy, normed, inv, slope, vec, *refs):
    parts, refs = refs[:n_w], refs[n_w:]
    dr, dz_keep, dz_give, du, du_give, dvec, w, sem = refs
    load = load_weight(info, parts, w, sem, False)
    g = dy[...].astype(F32)
    if not first:
        rows = lax.broadcasted_iota(jnp.int32, g.shape, 0)
        g = jnp.where(rows < info[1], g, 0.0)
    grad, dgain, dshift = norm_back(g, normed[...], inv[...], vec[6:7])
    dr[...] = grad
    dz = grad.astype(BF)
    dvec[0:1] = jnp.sum(dz.astype(F32), axis=0, keepdims=True)
    dvec[1:2] = dgain
    dvec[2:3] = dshift
    dvec[7:8] = jnp.zeros_like(dshift)
    half = dz.shape[1] // 2
    left, right = dz[:, :half], dz[:, half:]
    on_left = info[0] == 0
    dz_keep[...] = jnp.where(on_left, left, right)
    dz_give[...] = jnp.where(on_left, right, left)
    depth = dz.shape[1]
    load.wait()
    for j in range(4):
        at = slice(j * depth, (j + 1) * depth)
        low = (nt(dz, w[at]) * slope[j]).astype(BF)
        du[j] = low
        dvec[3 + j : 4 + j] = jnp.sum(low.astype(F32), axis=0, keepdims=True)
    for j in range(2):
        du_give[j] = du[2 * (1 - info[0]) + j]


def up_backward(n_w, info, du, dr, normed, inv, vec, *refs):
    parts, refs = refs[:n_w], refs[n_w:]
    dr1, dvec, w, sem = refs
    load_weight(info, parts, w, sem, True).wait()
    dh = dr[...]
    for j in range(4):
        dh += nt(du[j], w[j])
    grad, dgain, dshift = norm_back(dh, normed[...], inv[...], vec[3:4])
    dr1[...] = grad
    dvec[0:1] = jnp.sum(grad.astype(BF).astype(F32), axis=0, keepdims=True)
    dvec[1:2] = dgain
    dvec[2:3] = dshift
    dvec[3:8] = jnp.zeros((5, dshift.shape[1]), F32)


def attention_backward(n_w, info, dr1, qkv, soft, *refs):
    parts, refs = refs[:n_w], refs[n_w:]
    dx, side, side_give, dvec, w, sem = refs
    load = load_weight(info, parts, w, sem, True)
    db = dr1[...].astype(BF)
    load.wait()
    do = nt(db, w[3]).astype(BF)
    length, width = do.shape
    size = width // HEADS
    pair = 2 * size
    scale = size ** (-0.5)
    low_half = lax.broadcasted_iota(jnp.int32, (length, pair), 1) < size
    for p in range(HEADS // 2):
        at = slice(p * pair, (p + 1) * pair)
        qp, kp, vp, dop = qkv[0, :, at], qkv[1, :, at], qkv[2, :, at], do[:, at]
        dqs, dks, dvs = [], [], []
        for e in range(2):
            dom = jnp.where(low_half if e == 0 else ~low_half, dop, jnp.zeros_like(dop))
            a = soft[2 * p + e]
            da = nt(dom, vp)
            ds = (a * (da - jnp.sum(a * da, axis=-1, keepdims=True))).astype(BF)
            dvs.append(tn(a.astype(BF), dop))
            dqs.append(nn(ds, kp))
            dks.append(tn(ds, qp))
        side[0, :, at] = (jnp.where(low_half, dqs[0], dqs[1]) * scale).astype(BF)
        side[1, :, at] = (jnp.where(low_half, dks[0], dks[1]) * scale).astype(BF)
        side[2, :, at] = jnp.where(low_half, dvs[0], dvs[1]).astype(BF)
    side[3] = db
    total = dr1[...]
    for j in range(3):
        total += nt(side[j], w[j])
    dx[...] = total
    dvec[0:1] = jnp.sum(side[0].astype(F32), axis=0, keepdims=True)
    dvec[1:2] = jnp.sum(side[2].astype(F32), axis=0, keepdims=True)
    dvec[2:8] = jnp.zeros((6, width), F32)
    for j in range(2):
        side_give[j] = side[2 * (1 - info[0]) + j]


def down_weight(rows_too, info, act, act_other, dz, dz_other, *refs):
    if rows_too:
        extra, refs = refs[0], refs[1:]
    outs, (dw, sem) = refs[:-2], refs[-2:]
    right = jnp.concatenate([dz[...], dz_other[...]], axis=0)
    depth = dw.shape[0] // 4
    for j in range(4):
        at = slice(j * depth, (j + 1) * depth)
        left = jnp.concatenate([act[:, at], act_other[:, at]], axis=0)
        dw[at] = tn(left, right).astype(BF)
    if not rows_too:
        store_grad(info, dw, outs, sem, False).wait()
        return
    near = outs[1].shape[0]
    rows = dw.shape[0] // (2 * near)
    more = outs[0].shape[-2] - rows
    for out, base in ((outs[0], near), (outs[1], 0)):
        for s in range(out.shape[0]):
            owner = info[2 + base + s]
            at = pl.ds(pl.multiple_of(owner * rows, 16), rows)
            pltpu.make_async_copy(dw.at[at], out.at[s, pl.ds(0, rows)], sem).start()
            pltpu.make_async_copy(extra.at[owner], out.at[s, pl.ds(rows, more)], sem).start()
    pltpu.make_async_copy(dw, dw, sem).wait()
    pltpu.make_async_copy(extra, extra, sem).wait()


def up_weight(info, hidden, hidden_other, du, du_other, *refs):
    outs, (dw, sem) = refs[:-2], refs[-2:]
    left = jnp.concatenate([hidden[...], hidden_other[...]], axis=0)
    for j in range(2):
        right = jnp.concatenate([du[2 * info[0] + j], du_other[j]], axis=0)
        dw[j] = tn(left, right).astype(BF)
    store_grad(info, dw, outs, sem, True).wait()


def attention_weight(info, x, x_other, mixed, mixed_other, side, side_other, *refs):
    outs, (dw, sem) = refs[:-2], refs[-2:]
    left = jnp.concatenate([x[...], x_other[...]], axis=0)
    last = jnp.concatenate([mixed[...], mixed_other[...]], axis=0)
    for j in range(2):
        right = jnp.concatenate([side[2 * info[0] + j], side_other[j]], axis=0)
        if j == 1:
            left = jnp.where(info[0] == 0, left, last)
        dw[j] = tn(left, right).astype(BF)
    store_grad(info, dw, outs, sem, True).wait()


def call(kernel, info, small, parts, grads, outs, scratch, flops, nbytes):
    vmem = pl.BlockSpec(memory_space=pltpu.VMEM)
    hbm = pl.BlockSpec(memory_space=pl.ANY)
    shapes = [jax.ShapeDtypeStruct(s, BF) for s in grads]
    shapes += [jax.ShapeDtypeStruct(s, d) for s, d in outs]
    return pl.pallas_call(
        kernel,
        out_shape=shapes,
        in_specs=[pl.BlockSpec(memory_space=pltpu.SMEM)]
        + [vmem] * len(small)
        + [hbm] * len(parts),
        out_specs=[hbm] * len(grads) + [vmem] * len(outs),
        scratch_shapes=scratch,
        compiler_params=pltpu.CompilerParams(vmem_limit_bytes=VMEM_BYTES),
        cost_estimate=pl.CostEstimate(flops=1, bytes_accessed=1, transcendentals=0),
    )(info, *small, *parts)


class Layer:
    def __init__(self, info, vec, length, width):
        self.info, self.vec = info, vec
        self.length, self.width = length, width
        self.row = ((length, width), F32)
        self.low = ((length, width), BF)
        self.col = ((length, 1), F32)
        self.wide = (4, length, width)
        self.two = ((2, length, width), BF)
        self.half = ((length, width // 2), BF)
        self.size = 2 * length * width * width
        self.stack = pltpu.VMEM((4, width, width), BF)
        self.tall = pltpu.VMEM((4 * width, width), BF)
        self.bytes = 4 * width * width * 2
        self.sem = pltpu.SemaphoreType.DMA
        self.dvec = ((8, width), F32)
        self.other = {}

    def run(self, kernel, parts, small, outs, scratch, mults, grads=()):
        if parts:
            kernel = functools.partial(kernel, len(parts))
        return call(
            kernel, self.info, small, parts, grads, outs, scratch + [self.sem],
            mults * self.size, self.bytes,
        )

    def attention(self, x, parts):
        self.x = x
        outs = [((3,) + self.low[0], BF), ((HEADS, self.length, self.length), F32), self.low]
        outs += [self.row, self.low, self.row, self.col]
        got = self.run(attention_forward, parts, [x, self.vec], outs, [self.stack], 5)
        self.qkv, self.soft, self.mixed, self.hidden, self.hidden_low, self.n1, self.s1 = got
        return self.hidden_low

    def up(self, hidden_low, parts):
        self.act, self.slope = self.run(
            up_forward, parts, [hidden_low, self.vec],
            [((self.length, 4 * self.width), BF), (self.wide, F32)],
            [self.stack], 4,
        )
        return self.act

    def down(self, act, parts):
        out, self.n2, self.s2 = self.run(
            down_forward, parts, [act, self.hidden, self.vec], [self.row, self.row, self.col],
            [self.tall], 4,
        )
        return out

    def down_back(self, first, dy, parts):
        got = self.run(
            functools.partial(down_backward, first), parts,
            [dy, self.n2, self.s2, self.slope, self.vec],
            [self.row, self.half, self.half, (self.wide, BF), self.two, self.dvec],
            [self.tall], 4,
        )
        self.dr, self.dz, dz_give, self.du, du_give, self.dvec_down = got
        return dz_give, du_give

    def up_back(self, parts):
        self.dr1, self.dvec_up = self.run(
            up_backward, parts, [self.du, self.dr, self.n1, self.s1, self.vec],
            [self.row, self.dvec], [self.stack], 4,
        )

    def attention_back(self, dr1, parts):
        self.dx, self.side, give, self.dvec_att = self.run(
            attention_backward, parts, [dr1, self.qkv, self.soft],
            [self.row, (self.wide, BF), self.two, self.dvec], [self.stack], 7,
        )
        return give

    def weight(self, kind, grads, extra=()):
        o = self.other
        stack = pltpu.VMEM((2, self.width, self.width), BF)
        if kind == 2:
            stack = pltpu.VMEM((4 * self.width, self.width // 2), BF)
            small = [self.act, o["act"], self.dz, o["dz"], *extra]
            kernel = functools.partial(down_weight, len(extra) > 0)
        elif kind == 1:
            small = [self.hidden_low, o["hidden"], self.du, o["du"]]
            kernel = up_weight
        else:
            small = [self.x, o["x"], self.mixed, o["mixed"], self.side, o["side"]]
            kernel = attention_weight
        return self.run(kernel, [], small, [], [stack], 4, grads)

    def grad_vec(self):
        d, u, a = self.dvec_down, self.dvec_up, self.dvec_att
        return jnp.concatenate([a[0:2], u[0:3], d[0:7]], axis=0)


def route(move):
    size = lax.axis_size("dp")
    pairs = []
    for s in range(2):
        for d in range(size):
            to_s, to_d = move(s, d)
            pairs.append((s * size + d, to_s * size + to_d))
    return pairs


def send(v, pairs):
    return lax.ppermute(v, ALL, pairs)


def after(v, *others):
    return lax.optimization_barrier((v,) + others)[0]


def cube_routes():
    return (
        route(lambda s, d: (s, d ^ (1 if s == 0 else 2))),
        route(lambda s, d: (s, d ^ (2 if s == 0 else 1))),
    )


def cube_owners(core, me, flat_first):
    slot = jnp.arange(16)
    third = jnp.where(core == 0, 1, 2)

    def table(a, b):
        masks = (a, 8, 4, b) if flat_first else (8, 4, a, b)
        return me ^ sum(((slot >> i) & 1) * m for i, m in enumerate(masks))

    return jnp.concatenate([table(third, 3 - third), table(3 - third, third)]).astype(jnp.int32)


def swap_route():
    return route(lambda s, d: (1 - s, d))


def cube_body(tokens, lengths, cotangent, w_qkv, w_out, w_up, w_down, vectors):
    core = lax.axis_index("section")
    me = lax.axis_index("dp")
    first = core == 0
    _, length, width = tokens.shape
    rows = w_out.shape[1]
    third, last = cube_routes()
    swap = swap_route()
    z_routes = {
        j: route(lambda s, d, m=m: (s, d ^ m)) for j, m in ((1, 8), (2, 4), (3, 12))
    }
    vec_sum_routes = [route(lambda s, d, i=i: (s, d ^ (1 << i))) for i in range(4)]

    def chunks(w):
        return jnp.stack([w[:, j * width : (j + 1) * width] for j in range(w.shape[1] // width)])

    blocks = [None] * 6
    own = [jnp.concatenate([chunks(w_qkv[0]), w_out])]

    def split(p):
        n = own[p].shape[0] // 2
        mine = lax.dynamic_slice_in_dim(own[p], n * core, n, 0)
        other = lax.dynamic_slice_in_dim(own[p], n * (1 - core), n, 0)
        return (mine, other) if n > 1 else (mine[0], other[0])

    def place(p, mine, other):
        blocks[p] = jnp.where(first, mine, other)
        blocks[p + 3] = jnp.where(first, other, mine)

    infos = [
        jnp.concatenate([core[None], lengths[core][None], cube_owners(core, me, flat)])
        for flat in (False, True)
    ]
    infos = [info.astype(jnp.int32) for info in infos]
    layers = [Layer(infos[0], None, length, width) for l in range(2)]

    history = [[], []]
    now = []

    def tie(*values, extra=()):
        deps = history[WINDOW] + list(extra)
        return lax.optimization_barrier(tuple(values) + tuple(deps))[: len(values)]

    def sends(items, extra=()):
        values = tie(*[v for v, _ in items], extra=extra)
        got = [send(v, pairs) for v, (_, pairs) in zip(values, items)]
        now.extend(got)
        return got

    def step_end():
        history[:] = [history[1], list(now)]
        now[:] = []

    parts = {}
    results = []
    exchange = []

    def forward(p, v):
        l, kind = divmod(p, 3)
        layer = layers[l]
        layer.info = infos[p in FLAT_GATHER]
        (v,) = tie(v)
        if kind == 0:
            if l == 1:
                exchange.append((l, "x", v))
            v = layer.attention(v, parts[p])
            exchange.append((l, "mixed", layer.mixed))
            exchange.append((l, "hidden", layer.hidden_low))
        elif kind == 1:
            v = layer.up(v, parts[p])
            exchange.append((l, "act", v))
        else:
            v = layer.down(v, parts[p])
            results.append(v)
            v = v.astype(BF)
        now.append(v)
        return v

    rest, swapped = {}, {}
    n = len(blocks)
    halves = [split(0)]
    w_up, w_down, vectors, tokens, cotangent = lax.optimization_barrier(
        (w_up, w_down, vectors, tokens, cotangent, halves[0][1])
    )[:5]
    own.append(chunks(w_up[0]))
    own.append(jnp.stack([w_down[0][:, : width // 2], w_down[0][:, width // 2 :]]))
    halves += [split(1), split(2)]
    x = lax.dynamic_index_in_dim(tokens, core, 0, keepdims=False)
    layers[0].other["x"] = lax.dynamic_index_in_dim(tokens, 1 - core, 0, keepdims=False)
    cot = lax.dynamic_index_in_dim(cotangent, core, 0, keepdims=False)
    vec = jnp.stack([vectors[0], send(vectors[0], swap)])
    vec = jnp.where(first, vec, vec[::-1])
    vec_stages = {
        -1: [(3, z_routes[1]), (2, z_routes[2])],
        0: [(0, vec_sum_routes[0]), (1, vec_sum_routes[1])],
    }
    plan = {}

    def at_step(t, *item):
        plan.setdefault(t, []).append(item)

    for p in range(n):
        at_step(p + 1, "last", p, last)
        if p < DIRECT:
            for j in (1, 2, 3):
                at_step(p - 1, "z", p, z_routes[j])
            at_step(p, "flat", p, third)
        elif p in FLAT_GATHER:
            at_step(FLAT_GATHER[p], "flat", p, third)
            at_step(p - 1, "tall", p, z_routes[1])
            at_step(p, "tall", p, z_routes[2])
        else:
            early = p - 2 if p < 4 else p - 3
            at_step(early, "tall", p, z_routes[1])
            at_step(early + 1, "tall", p, z_routes[2])
            at_step(p, "flat", p, third)
        at_step(p + 2, "late", p, swap)
        at_step(p + 1, "swapped", p, swap)

    for p in range(2):
        place(p, halves[p][0], send(halves[p][1], swap))
    here = dict(enumerate(blocks))
    joins = []
    for t in range(-1, n + 2):
        flat = [v for _, _, arrays, _ in joins for v in arrays]
        tied = list(tie(*flat)) if flat else []
        for where, q, arrays, join in joins:
            where[q] = join([tied.pop(0) for _ in arrays])
        joins = []
        todo = []
        for name, p, pairs in plan.get(t, []):
            todo.append((name, p, rest[p] if name == "late" else here[p], pairs))
        if t == -1:
            todo.append(("own", 2, halves[2][1], swap))
        for l, name, v in exchange:
            todo.append((name, l, v, swap))
        exchange.clear()
        got = sends([item[2:] for item in todo])
        for (name, q, _, _), v in zip(todo, got):
            if name == "late":
                parts[q] = [here[q], rest[q], swapped[q], v]
        for bit, pairs in vec_stages.get(t, []):
            (v,) = sends([(vec, pairs)], [blocks[0]])
            upper = (me >> bit) & 1 == 1
            vec = jnp.where(upper, jnp.stack([v, vec]), jnp.stack([vec, v]))
        if t == 0:
            vec = vec.transpose(4, 3, 2, 0, 1, 5).reshape(2, -1, width).astype(F32)
            layers[0].vec, layers[1].vec = vec[0], vec[1]
        if t >= 2:
            x = forward(t - 2, x)
        straight = {}
        for (name, q, _, _), v in zip(todo, got):
            if name == "last":
                rest[q] = v
            elif name == "z":
                straight.setdefault(q, [blocks[q]]).append(v)
            elif name == "swapped":
                swapped[q] = v
            elif name == "own":
                place(q, halves[q][0], v)
                here[q], here[q + 3] = blocks[q], blocks[q + 3]
            elif name in ("flat", "tall"):
                one = here[q].shape == blocks[q].shape
                joins.append((here, q, [here[q], v], jnp.stack if one else jnp.concatenate))
            elif name != "late":
                layers[q].other[name] = v
        for q, arrays in straight.items():
            joins.append((here, q, arrays, jnp.stack))
        step_end()

    order = [(1, 2), (1, 1), (1, 0), (0, 1), (0, 0), (0, 2)]
    dxs = {}

    def chain(l, kind):
        layer = layers[l]
        layer.info = infos[3 * l + kind in FLAT_GATHER]
        if kind == 2:
            dy = cot if l == 1 else dxs[1].astype(BF)
            (dy,) = tie(dy)
            dz, du = layer.down_back(l == 0, dy, parts[3 * l + 2])
            layer.other["dz"], layer.other["du"] = send(dz, swap), send(du, swap)
            now.append(layer.dr)
        elif kind == 1:
            layer.up_back(parts[3 * l + 1])
            now.append(layer.dr1)
        else:
            (dr1,) = tie(layer.dr1)
            layer.other["side"] = send(layer.attention_back(dr1, parts[3 * l]), swap)
            dxs[l] = layer.dx
            now.append(layer.dx)

    def weight(l, kind):
        shape = (8,) + blocks[kind].shape
        extra = ()
        if (l, kind) == order[-1]:
            keep, give = by_layer(layers[0].grad_vec(), layers[1].grad_vec())
            (got,) = sends([(give, swap)])
            entries = (keep + got).reshape(16, 2, -1).astype(BF)
            pad = shape[-1] - entries.shape[-1]
            extra = (jnp.pad(entries, ((0, 0), (0, 14), (0, pad))),)
            shape = (8, shape[1] + 16, shape[2])
        layers[l].info = infos[order.index((l, kind)) in FLAT_SUM]
        give, keep = layers[l].weight(kind, [shape, shape], extra)
        terms.append([keep])
        gives.append(give)
        now.extend([give, keep])

    def by_layer(a, b):
        return jnp.where(first, a, b), jnp.where(first, b, a)

    terms, gives = [], []
    work = [
        [(chain, 1, 2), (chain, 1, 1), (weight, 1, 2)],
        [(chain, 1, 0), (weight, 1, 1)],
        [(weight, 1, 0), (chain, 0, 2)],
        [(chain, 0, 1), (weight, 0, 1)],
        [(chain, 0, 0), (weight, 0, 0)],
        [(weight, 0, 2)],
    ]

    def part(arrays, lo, hi, kind):
        total = arrays[0][lo:hi].astype(F32)
        for v in arrays[1:]:
            total = total + v[lo:hi].astype(F32)
        return total.astype(kind)

    z_low, z_high = z_routes[2], z_routes[1]
    plan = {}
    for q in range(len(order)):
        steps = [(q + 1, last)]
        if q in FLAT_SUM:
            steps += [(q + 2, z_low), (q + 3, z_high), (FLAT_SUM[q], third)]
        else:
            steps += [(q + 2, third), (q + 3, None)]
        left = 16
        for t, pairs in steps:
            plan.setdefault(t, []).append((q, left, pairs))
            left //= 2

    sums = {}
    acts_keep, acts_give = by_layer(*results)
    extra = [("acts", acts_give)]
    kept = {"acts": acts_keep}
    got_extra = {}
    total_vec = None
    for t in range(len(order) + 4):
        todo = []
        for q, left, pairs in plan.get(t, []):
            if left == 16:
                todo.append(("flat", q, gives[q], pairs))
                continue
            arrays = tie(*terms[q])
            if pairs is None:
                for j in (1, 2, 3):
                    todo.append(("tall", q, part(arrays, j, j + 1, BF), z_routes[j]))
            else:
                name = "flat" if pairs is third else "tall"
                todo.append((name, q, part(arrays, left // 2, left, BF), pairs))
        for name, v in extra:
            todo.append((name, 0, v, swap))
        extra = []
        got = sends([item[2:] for item in todo]) if todo else []
        for f, l, kind in work[t] if t < len(work) else []:
            f(l, kind)
        step_end()
        for (name, q, _, _), v in zip(todo, got):
            if name in ("flat", "tall"):
                terms[q].append(v)
            else:
                got_extra[name] = v
        if t == 4:
            kept["dx"], give_v = by_layer(dxs[0], dxs[1])
            extra.append(("dx", give_v))
        for q, left, pairs in plan.get(t, []):
            if left > 2 and pairs is not None:
                continue
            sums[order[q]] = part(terms[q], 0, 1, F32)[0]
            l, kind = order[q]
            if (1 - l, kind) not in sums:
                continue
            mine = sums[0, kind]
            if order[-1] == (0, kind):
                n_rows = blocks[kind].shape[0]
                total_vec = mine[n_rows : n_rows + 2, : vectors.shape[1] // 2].reshape(1, -1)
                mine = mine[:n_rows]
            kept[kind], give_v = by_layer(mine, sums[1, kind])
            extra.append((kind, give_v))
        if t == len(order) + 1:
            for name in ("acts", "dx"):
                kept[name], got_extra[name] = tie(kept[name], got_extra[name])

    def joined(name, axis):
        a, b = kept[name], got_extra[name]
        if axis is None:
            return jnp.where(first, jnp.stack([a, b]), jnp.stack([b, a]))
        return jnp.where(first, jnp.concatenate([a, b], axis), jnp.concatenate([b, a], axis))

    acts = joined("acts", None)[None]
    grads_in = joined("dx", None)[None]
    whole = [joined(0, 0), joined(1, 0), joined(2, 1)]

    def side_by_side(stack):
        return jnp.concatenate([stack[j] for j in range(stack.shape[0])], axis=1)[None]

    return (
        acts,
        grads_in,
        side_by_side(whole[0][:3]),
        whole[0][3][None],
        side_by_side(whole[1]),
        whole[2][None],
        total_vec,
    )


def plain_body(tokens, lengths, cotangent, w_qkv, w_out, w_up, w_down, vectors):
    core = lax.axis_index("section")
    first = core == 0
    chains_dev, length, width = tokens.shape
    swap = swap_route()
    size = lax.axis_size("dp")
    rows = w_out.shape[1]

    def gathered(w):
        return lax.all_gather(w, "dp", axis=0, tiled=True)

    def both(v):
        got = send(v, swap)
        return jnp.where(first, v, got), jnp.where(first, got, v)

    def chunks(w):
        return jnp.stack([w[:, j * width : (j + 1) * width] for j in range(w.shape[1] // width)])

    att = jnp.concatenate([chunks(gathered(w_qkv[0])), gathered(w_out[0])[None]])
    up = chunks(gathered(w_up[0]))
    down = gathered(w_down[0])
    vec = gathered(vectors[0]).reshape(-1, width).astype(F32)
    att, up, down, vec = both(att), both(up), both(down), both(vec)
    info = jnp.stack([core, lengths[core]]).astype(jnp.int32)
    layers = [Layer(info, vec[l], length, width) for l in range(2)]
    x = lax.dynamic_index_in_dim(tokens, core, 0, keepdims=False)
    dy = lax.dynamic_index_in_dim(cotangent, core, 0, keepdims=False)
    results = []
    for l in range(2):
        layer = layers[l]
        layer.other["x"] = send(x, swap)
        hidden = layer.attention(x, [att[l]])
        act = layer.up(hidden, [up[l]])
        layer.other["mixed"], layer.other["hidden"] = send(layer.mixed, swap), send(hidden, swap)
        layer.other["act"] = send(act, swap)
        y = layer.down(act, [down[l]])
        results.append(y)
        x = y.astype(BF)
    stacked, tall = [(2, width, width)], [(4 * width, width // 2)]
    grads = {}
    dxs = {}
    for l in (1, 0):
        layer = layers[l]
        dz, du = layer.down_back(l == 0, dy, [down[l]])
        layer.other["dz"], layer.other["du"] = send(dz, swap), send(du, swap)
        layer.up_back([up[l]])
        layer.other["side"] = send(layer.attention_back(layer.dr1, [att[l]]), swap)
        for kind in range(3):
            (grads[l, kind],) = layer.weight(kind, tall if kind == 2 else stacked)
        dxs[l] = layer.dx
        dy = layer.dx.astype(BF)

    def by_layer(a, b):
        return jnp.where(first, a, b), send(jnp.where(first, b, a), swap)

    def chains(a, b):
        keep, got = by_layer(a, b)
        return jnp.where(first, jnp.stack([keep, got]), jnp.stack([got, keep]))[None]

    def scattered(total):
        dim = total.ndim - 2 if total.ndim > 1 else 0
        return lax.psum_scatter(total, "dp", scatter_dimension=dim, tiled=True).astype(F32)

    def summed(kind, axis):
        keep, got = by_layer(scattered(grads[0, kind]), scattered(grads[1, kind]))
        left, right = jnp.where(first, keep, got), jnp.where(first, got, keep)
        return jnp.concatenate([left, right], axis)

    def side_by_side(stack):
        return jnp.concatenate([stack[j] for j in range(stack.shape[0])], axis=1)[None]

    g_att, g_up, g_down = summed(0, 0), summed(1, 0), summed(2, 1)
    keep, got = by_layer(layers[0].grad_vec(), layers[1].grad_vec())
    g_vec = scattered((keep + got).reshape(-1))
    return (
        chains(*results),
        chains(dxs[0], dxs[1]),
        side_by_side(g_att[:3]),
        g_att[3][None],
        side_by_side(g_up),
        g_down[None],
        g_vec[None],
    )


def solution(mesh):
    placed = (
        P("dp", None, None),
        P("dp"),
        P("dp", None, None),
        P("section", "dp", None),
        P("section", "dp", None),
        P("section", "dp", None),
        P("section", "dp", None),
        P("section", "dp"),
    )
    return jax.shard_map(
        cube_body if mesh.shape["dp"] == 16 else plain_body,
        mesh=mesh,
        in_specs=placed,
        out_specs=(
            P("section", "dp", None, None),
            P("section", "dp", None, None),
            P("section", "dp", None),
            P("section", "dp", None),
            P("section", "dp", None),
            P("section", "dp", None),
            P("section", "dp"),
        ),
        check_vma=False,
    )
```

```python
import functools

import jax
import jax.numpy as jnp
from jax import lax
from jax.experimental import pallas as pl
from jax.experimental.pallas import tpu as pltpu
from jax.sharding import PartitionSpec as P

HEADS = 12
BF = jnp.bfloat16
F32 = jnp.float32
EPS = 1e-06
FILL = -1000000000.0
ROOT_HALF = 0.7071067811865476
INV_ROOT_TWO_PI = 0.3989422804014327
VMEM_BYTES = 24 * 1024 * 1024
ALL = ("section", "dp")
WINDOW = 1
DIRECT = 2
FLAT_GATHER = {3: 0, 5: 3}
FLAT_SUM = {0: 4, 1: 7}


def nn(a, b):
    return lax.dot_general(a, b, (((1,), (0,)), ((), ())), preferred_element_type=F32)


def nt(a, b):
    return lax.dot_general(a, b, (((1,), (1,)), ((), ())), preferred_element_type=F32)


def tn(a, b):
    return lax.dot_general(a, b, (((0,), (0,)), ((), ())), preferred_element_type=F32)


def norm(r, gain, shift):
    mean = jnp.mean(r, axis=-1, keepdims=True)
    cent = r - mean
    inv = lax.rsqrt(jnp.mean(cent * cent, axis=-1, keepdims=True) + EPS)
    n = cent * inv
    return n * gain + shift, n, inv


def norm_back(dy, n, inv, gain):
    t = dy * gain
    dr = inv * (
        t - jnp.mean(t, axis=-1, keepdims=True) - n * jnp.mean(t * n, axis=-1, keepdims=True)
    )
    return dr, jnp.sum(dy * n, axis=0, keepdims=True), jnp.sum(dy, axis=0, keepdims=True)


def load_weight(info, parts, dst, sem, stacked):
    if len(parts) == 1:
        copy = pltpu.make_async_copy(parts[0], dst, sem)
        copy.start()
        return copy
    blocks = sum(part.shape[0] for part in parts) // 2
    rows = parts[0].shape[-2]
    slot = 0
    for part in parts:
        for s in range(part.shape[0]):
            half = info[0] if slot < blocks else 1 - info[0]
            at = pl.ds(pl.multiple_of(info[2 + slot] * rows, 16), rows)
            if stacked:
                window = (pl.ds(2 * half, 2), at)
            else:
                cols = part.shape[-1]
                window = (at, pl.ds(pl.multiple_of(half * cols, 128), cols))
            pltpu.make_async_copy(part.at[s], dst.at[window], sem).start()
            slot += 1
    return pltpu.make_async_copy(dst, dst, sem)


def store_grad(info, src, outs, sem, stacked):
    if len(outs) == 1:
        copy = pltpu.make_async_copy(src, outs[0], sem)
        copy.start()
        return copy
    near = outs[1].shape[0]
    rows = outs[0].shape[-2]
    for out, base in ((outs[0], near), (outs[1], 0)):
        for s in range(out.shape[0]):
            at = pl.ds(pl.multiple_of(info[2 + base + s] * rows, 16), rows)
            window = (slice(None), at) if stacked else (at,)
            pltpu.make_async_copy(src.at[window], out.at[s], sem).start()
    return pltpu.make_async_copy(src, src, sem)


def attention_forward(n_w, info, x, vec, *refs):
    parts, refs = refs[:n_w], refs[n_w:]
    qkv, soft, pack, hidden, normed, inv, w, sem = refs
    load_weight(info, parts, w, sem, True).wait()
    xb = x[...]
    length, width = xb.shape
    q = (nn(xb, w[0]) + vec[0:1]).astype(BF)
    k = nn(xb, w[1]).astype(BF)
    v = (nn(xb, w[2]) + vec[1:2]).astype(BF)
    qkv[0] = q
    qkv[1] = k
    qkv[2] = v
    size = width // HEADS
    pair = 2 * size
    low_half = lax.broadcasted_iota(jnp.int32, (length, pair), 1) < size
    valid = lax.broadcasted_iota(jnp.int32, (length, length), 1) < info[1]
    for p in range(HEADS // 2):
        at = slice(p * pair, (p + 1) * pair)
        qp, kp, vp = q[:, at], k[:, at], v[:, at]
        sides = []
        for e in range(2):
            qm = jnp.where(low_half if e == 0 else ~low_half, qp, jnp.zeros_like(qp))
            s = jnp.where(valid, nt(qm, kp) * size ** (-0.5), FILL)
            ex = jnp.exp(s - jnp.max(s, axis=-1, keepdims=True))
            a = ex / jnp.sum(ex, axis=-1, keepdims=True)
            soft[2 * p + e] = a
            sides.append(nn(a.astype(BF), vp))
        pack[1, :, at] = jnp.where(low_half, sides[0], sides[1]).astype(BF)
    pack[0] = xb
    r = xb.astype(F32) + (nn(pack[1], w[3]) + vec[2:3])
    h, normed[...], inv[...] = norm(r, vec[3:4], vec[4:5])
    hidden[...] = h
    pack[2] = h.astype(BF)


def up_forward(n_w, info, pack, vec, *refs):
    parts, refs = refs[:n_w], refs[n_w:]
    act, slope, w, sem = refs
    load_weight(info, parts, w, sem, True).wait()
    hb = pack[2]
    for j in range(4):
        u = nn(hb, w[j]) + vec[8 + j : 9 + j]
        cdf = 0.5 * (1.0 + lax.erf(u * ROOT_HALF))
        act[:, j * u.shape[1] : (j + 1) * u.shape[1]] = (u * cdf).astype(BF)
        slope[j] = cdf + u * INV_ROOT_TWO_PI * jnp.exp(-0.5 * u * u)


def down_forward(n_w, info, act, hidden, vec, *refs):
    parts, refs = refs[:n_w], refs[n_w:]
    out, normed, inv, w, sem = refs
    load_weight(info, parts, w, sem, False).wait()
    r = hidden[...] + (nn(act[...], w[...]) + vec[5:6])
    out[...], normed[...], inv[...] = norm(r, vec[6:7], vec[7:8])


def down_backward(first, n_w, info, dy, normed, inv, slope, vec, *refs):
    parts, refs = refs[:n_w], refs[n_w:]
    dr, dz_keep, dz_give, du, du_give, dvec, w, sem = refs
    load = load_weight(info, parts, w, sem, False)
    g = dy[...].astype(F32)
    if not first:
        rows = lax.broadcasted_iota(jnp.int32, g.shape, 0)
        g = jnp.where(rows < info[1], g, 0.0)
    grad, dgain, dshift = norm_back(g, normed[...], inv[...], vec[6:7])
    dr[...] = grad
    dz = grad.astype(BF)
    dvec[0:1] = jnp.sum(dz.astype(F32), axis=0, keepdims=True)
    dvec[1:2] = dgain
    dvec[2:3] = dshift
    dvec[7:8] = jnp.zeros_like(dshift)
    half = dz.shape[1] // 2
    left, right = dz[:, :half], dz[:, half:]
    on_left = info[0] == 0
    dz_keep[...] = jnp.where(on_left, left, right)
    dz_give[...] = jnp.where(on_left, right, left)
    depth = dz.shape[1]
    load.wait()
    for j in range(4):
        at = slice(j * depth, (j + 1) * depth)
        low = (nt(dz, w[at]) * slope[j]).astype(BF)
        du[j] = low
        dvec[3 + j : 4 + j] = jnp.sum(low.astype(F32), axis=0, keepdims=True)
    for j in range(2):
        du_give[j] = du[2 * (1 - info[0]) + j]


def up_backward(n_w, info, du, dr, normed, inv, vec, *refs):
    parts, refs = refs[:n_w], refs[n_w:]
    dr1, dvec, w, sem = refs
    load_weight(info, parts, w, sem, True).wait()
    dh = dr[...]
    for j in range(4):
        dh += nt(du[j], w[j])
    grad, dgain, dshift = norm_back(dh, normed[...], inv[...], vec[3:4])
    dr1[...] = grad
    dvec[0:1] = jnp.sum(grad.astype(BF).astype(F32), axis=0, keepdims=True)
    dvec[1:2] = dgain
    dvec[2:3] = dshift
    dvec[3:8] = jnp.zeros((5, dshift.shape[1]), F32)


def attention_backward(n_w, info, dr1, qkv, soft, *refs):
    parts, refs = refs[:n_w], refs[n_w:]
    dx, side, side_give, dvec, w, sem = refs
    load = load_weight(info, parts, w, sem, True)
    db = dr1[...].astype(BF)
    load.wait()
    do = nt(db, w[3]).astype(BF)
    length, width = do.shape
    size = width // HEADS
    pair = 2 * size
    scale = size ** (-0.5)
    low_half = lax.broadcasted_iota(jnp.int32, (length, pair), 1) < size
    for p in range(HEADS // 2):
        at = slice(p * pair, (p + 1) * pair)
        qp, kp, vp, dop = qkv[0, :, at], qkv[1, :, at], qkv[2, :, at], do[:, at]
        dqs, dks, dvs = [], [], []
        for e in range(2):
            dom = jnp.where(low_half if e == 0 else ~low_half, dop, jnp.zeros_like(dop))
            a = soft[2 * p + e]
            da = nt(dom, vp)
            ds = (a * (da - jnp.sum(a * da, axis=-1, keepdims=True))).astype(BF)
            dvs.append(tn(a.astype(BF), dop))
            dqs.append(nn(ds, kp))
            dks.append(tn(ds, qp))
        side[0, :, at] = (jnp.where(low_half, dqs[0], dqs[1]) * scale).astype(BF)
        side[1, :, at] = (jnp.where(low_half, dks[0], dks[1]) * scale).astype(BF)
        side[2, :, at] = jnp.where(low_half, dvs[0], dvs[1]).astype(BF)
    side[3] = db
    total = dr1[...]
    for j in range(3):
        total += nt(side[j], w[j])
    dx[...] = total
    dvec[0:1] = jnp.sum(side[0].astype(F32), axis=0, keepdims=True)
    dvec[1:2] = jnp.sum(side[2].astype(F32), axis=0, keepdims=True)
    dvec[2:8] = jnp.zeros((6, width), F32)
    for j in range(2):
        side_give[j] = side[2 * (1 - info[0]) + j]


def down_weight(rows_too, info, act, act_other, dz, dz_other, *refs):
    if rows_too:
        extra, refs = refs[0], refs[1:]
    outs, (dw, sem) = refs[:-2], refs[-2:]
    right = jnp.concatenate([dz[...], dz_other[...]], axis=0)
    depth = dw.shape[0] // 4
    for j in range(4):
        at = slice(j * depth, (j + 1) * depth)
        left = jnp.concatenate([act[:, at], act_other[:, at]], axis=0)
        dw[at] = tn(left, right).astype(BF)
    if not rows_too:
        store_grad(info, dw, outs, sem, False).wait()
        return
    near = outs[1].shape[0]
    rows = dw.shape[0] // (2 * near)
    more = outs[0].shape[-2] - rows
    for out, base in ((outs[0], near), (outs[1], 0)):
        for s in range(out.shape[0]):
            owner = info[2 + base + s]
            at = pl.ds(pl.multiple_of(owner * rows, 16), rows)
            pltpu.make_async_copy(dw.at[at], out.at[s, pl.ds(0, rows)], sem).start()
            pltpu.make_async_copy(extra.at[owner], out.at[s, pl.ds(rows, more)], sem).start()
    pltpu.make_async_copy(dw, dw, sem).wait()
    pltpu.make_async_copy(extra, extra, sem).wait()


def up_weight(info, pack, pack_other, du, du_other, *refs):
    outs, (dw, sem) = refs[:-2], refs[-2:]
    left = jnp.concatenate([pack[2], pack_other[2]], axis=0)
    for j in range(2):
        right = jnp.concatenate([du[2 * info[0] + j], du_other[j]], axis=0)
        dw[j] = tn(left, right).astype(BF)
    store_grad(info, dw, outs, sem, True).wait()


def attention_weight(info, pack, pack_other, side, side_other, *refs):
    outs, (dw, sem) = refs[:-2], refs[-2:]
    left = jnp.concatenate([pack[0], pack_other[0]], axis=0)
    last = jnp.concatenate([pack[1], pack_other[1]], axis=0)
    for j in range(2):
        right = jnp.concatenate([side[2 * info[0] + j], side_other[j]], axis=0)
        if j == 1:
            left = jnp.where(info[0] == 0, left, last)
        dw[j] = tn(left, right).astype(BF)
    store_grad(info, dw, outs, sem, True).wait()


def call(kernel, info, small, parts, grads, outs, scratch, flops, nbytes):
    vmem = pl.BlockSpec(memory_space=pltpu.VMEM)
    hbm = pl.BlockSpec(memory_space=pl.ANY)
    shapes = [jax.ShapeDtypeStruct(s, BF) for s in grads]
    shapes += [jax.ShapeDtypeStruct(s, d) for s, d in outs]
    return pl.pallas_call(
        kernel,
        out_shape=shapes,
        in_specs=[pl.BlockSpec(memory_space=pltpu.SMEM)]
        + [vmem] * len(small)
        + [hbm] * len(parts),
        out_specs=[hbm] * len(grads) + [vmem] * len(outs),
        scratch_shapes=scratch,
        compiler_params=pltpu.CompilerParams(vmem_limit_bytes=VMEM_BYTES),
        cost_estimate=pl.CostEstimate(flops=1, bytes_accessed=1, transcendentals=0),
    )(info, *small, *parts)


class Layer:
    def __init__(self, info, vec, length, width):
        self.info, self.vec = info, vec
        self.length, self.width = length, width
        self.row = ((length, width), F32)
        self.low = ((length, width), BF)
        self.col = ((length, 1), F32)
        self.wide = (4, length, width)
        self.two = ((2, length, width), BF)
        self.half = ((length, width // 2), BF)
        self.size = 2 * length * width * width
        self.stack = pltpu.VMEM((4, width, width), BF)
        self.tall = pltpu.VMEM((4 * width, width), BF)
        self.bytes = 4 * width * width * 2
        self.sem = pltpu.SemaphoreType.DMA
        self.dvec = ((8, width), F32)
        self.other = {}

    def run(self, kernel, parts, small, outs, scratch, mults, grads=()):
        if parts:
            kernel = functools.partial(kernel, len(parts))
        return call(
            kernel, self.info, small, parts, grads, outs, scratch + [self.sem],
            mults * self.size, self.bytes,
        )

    def attention(self, x, parts):
        outs = [((3,) + self.low[0], BF), ((HEADS, self.length, self.length), F32)]
        outs += [((3,) + self.low[0], BF), self.row, self.row, self.col]
        got = self.run(attention_forward, parts, [x, self.vec], outs, [self.stack], 5)
        self.qkv, self.soft, self.pack, self.hidden, self.n1, self.s1 = got
        return self.pack

    def up(self, pack, parts):
        self.act, self.slope = self.run(
            up_forward, parts, [pack, self.vec],
            [((self.length, 4 * self.width), BF), (self.wide, F32)],
            [self.stack], 4,
        )
        return self.act

    def down(self, act, parts):
        out, self.n2, self.s2 = self.run(
            down_forward, parts, [act, self.hidden, self.vec], [self.row, self.row, self.col],
            [self.tall], 4,
        )
        return out

    def down_back(self, first, dy, parts):
        got = self.run(
            functools.partial(down_backward, first), parts,
            [dy, self.n2, self.s2, self.slope, self.vec],
            [self.row, self.half, self.half, (self.wide, BF), self.two, self.dvec],
            [self.tall], 4,
        )
        self.dr, self.dz, dz_give, self.du, du_give, self.dvec_down = got
        return dz_give, du_give

    def up_back(self, parts):
        self.dr1, self.dvec_up = self.run(
            up_backward, parts, [self.du, self.dr, self.n1, self.s1, self.vec],
            [self.row, self.dvec], [self.stack], 4,
        )

    def attention_back(self, dr1, parts):
        self.dx, self.side, give, self.dvec_att = self.run(
            attention_backward, parts, [dr1, self.qkv, self.soft],
            [self.row, (self.wide, BF), self.two, self.dvec], [self.stack], 7,
        )
        return give

    def weight(self, kind, grads, extra=()):
        o = self.other
        stack = pltpu.VMEM((2, self.width, self.width), BF)
        if kind == 2:
            stack = pltpu.VMEM((4 * self.width, self.width // 2), BF)
            small = [self.act, o["act"], self.dz, o["dz"], *extra]
            kernel = functools.partial(down_weight, len(extra) > 0)
        elif kind == 1:
            small = [self.pack, o["pack"], self.du, o["du"]]
            kernel = up_weight
        else:
            small = [self.pack, o["pack"], self.side, o["side"]]
            kernel = attention_weight
        return self.run(kernel, [], small, [], [stack], 4, grads)

    def grad_vec(self):
        d, u, a = self.dvec_down, self.dvec_up, self.dvec_att
        return jnp.concatenate([a[0:2], u[0:3], d[0:7]], axis=0)


def route(move):
    size = lax.axis_size("dp")
    pairs = []
    for s in range(2):
        for d in range(size):
            to_s, to_d = move(s, d)
            pairs.append((s * size + d, to_s * size + to_d))
    return pairs


def send(v, pairs):
    return lax.ppermute(v, ALL, pairs)


def after(v, *others):
    return lax.optimization_barrier((v,) + others)[0]


def cube_routes():
    return (
        route(lambda s, d: (s, d ^ (1 if s == 0 else 2))),
        route(lambda s, d: (s, d ^ (2 if s == 0 else 1))),
    )


def cube_owners(core, me, flat_first):
    slot = jnp.arange(16)
    third = jnp.where(core == 0, 1, 2)

    def table(a, b):
        masks = (a, 8, 4, b) if flat_first else (8, 4, a, b)
        return me ^ sum(((slot >> i) & 1) * m for i, m in enumerate(masks))

    return jnp.concatenate([table(third, 3 - third), table(3 - third, third)]).astype(jnp.int32)


def swap_route():
    return route(lambda s, d: (1 - s, d))


def cube_body(tokens, lengths, cotangent, w_qkv, w_out, w_up, w_down, vectors):
    core = lax.axis_index("section")
    me = lax.axis_index("dp")
    first = core == 0
    _, length, width = tokens.shape
    rows = w_out.shape[1]
    third, last = cube_routes()
    swap = swap_route()
    z_routes = {
        j: route(lambda s, d, m=m: (s, d ^ m)) for j, m in ((1, 8), (2, 4), (3, 12))
    }
    vec_sum_routes = [route(lambda s, d, i=i: (s, d ^ (1 << i))) for i in range(4)]

    def chunks(w):
        return jnp.stack([w[:, j * width : (j + 1) * width] for j in range(w.shape[1] // width)])

    blocks = [None] * 6
    own = [jnp.concatenate([chunks(w_qkv[0]), w_out])]

    def split(p):
        n = own[p].shape[0] // 2
        mine = lax.dynamic_slice_in_dim(own[p], n * core, n, 0)
        other = lax.dynamic_slice_in_dim(own[p], n * (1 - core), n, 0)
        return (mine, other) if n > 1 else (mine[0], other[0])

    def place(p, mine, other):
        blocks[p] = jnp.where(first, mine, other)
        blocks[p + 3] = jnp.where(first, other, mine)

    infos = [
        jnp.concatenate([core[None], lengths[core][None], cube_owners(core, me, flat)])
        for flat in (False, True)
    ]
    infos = [info.astype(jnp.int32) for info in infos]
    layers = [Layer(infos[0], None, length, width) for l in range(2)]

    history = [[], []]
    now = []

    def tie(*values, extra=()):
        deps = history[WINDOW] + list(extra)
        return lax.optimization_barrier(tuple(values) + tuple(deps))[: len(values)]

    gate = []

    slow, older = [[], []], []

    def sends(items, extra=(), long=False, over=False):
        more = [] if long else older if over else slow[0]
        values = tie(*[v for v, _ in items], extra=list(extra) + more)
        gate.extend(values)
        got = [send(v, pairs) for v, (_, pairs) in zip(values, items)]
        (slow[1] if long else now).extend(got)
        return got

    def step_end():
        history[:] = [history[1], list(now)]
        now[:] = []
        gate[:] = []
        older[:] = slow[0]
        slow[:] = [slow[1], []]

    parts = {}
    results = []
    exchange = []

    def forward(p, v):
        l, kind = divmod(p, 3)
        layer = layers[l]
        layer.info = infos[p in FLAT_GATHER]
        (v,) = tie(v, extra=gate)
        if kind == 0:
            v = layer.attention(v, parts[p])
            exchange.append((l, "pack", v))
        elif kind == 1:
            v = layer.up(v, parts[p])
            exchange.append((l, "act", v))
        else:
            v = layer.down(v, parts[p])
            results.append(v)
            v = v.astype(BF)
        now.append(v)
        return v

    rest, swapped = {}, {}
    n = len(blocks)
    halves = [split(0)]
    w_up, w_down, vectors, tokens, cotangent = lax.optimization_barrier(
        (w_up, w_down, vectors, tokens, cotangent, halves[0][1])
    )[:5]
    own.append(chunks(w_up[0]))
    own.append(jnp.stack([w_down[0][:, : width // 2], w_down[0][:, width // 2 :]]))
    halves += [split(1), split(2)]
    x = lax.dynamic_index_in_dim(tokens, core, 0, keepdims=False)
    cot = lax.dynamic_index_in_dim(cotangent, core, 0, keepdims=False)
    vec = jnp.stack([vectors[0], send(vectors[0], swap)])
    vec = jnp.where(first, vec, vec[::-1])
    vec_stages = {
        -1: [(3, z_routes[1]), (2, z_routes[2])],
        0: [(0, vec_sum_routes[0]), (1, vec_sum_routes[1])],
    }
    plan = {}

    def at_step(t, *item):
        plan.setdefault(t, []).append(item)

    for p in range(n):
        at_step(p + 1, "last", p, last)
        if p < DIRECT:
            for j in (1, 2, 3):
                at_step(p - 1, "z", p, z_routes[j])
            at_step(p, "flat", p, third)
        elif p in FLAT_GATHER:
            at_step(FLAT_GATHER[p], "flat", p, third)
            at_step(p - 1, "tall", p, z_routes[1])
            at_step(p, "tall", p, z_routes[2])
        else:
            early = p - 2 if p < 4 else p - 3
            at_step(early, "tall", p, z_routes[1])
            at_step(early + 1, "tall", p, z_routes[2])
            at_step(p, "flat", p, third)
        at_step(min(p + 3, n + 1), "late", p, swap)
        at_step(p + 1, "swapped", p, swap)

    for p in range(2):
        place(p, halves[p][0], send(halves[p][1], swap))
    here = dict(enumerate(blocks))
    joins = []
    for t in range(-1, n + 3):
        flat = [v for _, _, arrays, _ in joins for v in arrays]
        tied = list(tie(*flat)) if flat else []
        for where, q, arrays, join in joins:
            where[q] = join([tied.pop(0) for _ in arrays])
        joins = []
        todo = []
        for name, p, pairs in plan.get(t, []):
            todo.append((name, p, rest[p] if name == "late" else here[p], pairs))
        if t == -1:
            todo.append(("own", 2, halves[2][1], swap))
        for l, name, v in exchange:
            todo.append((name, l, v, swap))
        exchange.clear()
        long = [item for item in todo if item[0] == "last"]
        todo = [item for item in todo if item[0] != "last"]
        got = sends([item[2:] for item in long], long=True) if long else []
        got = got + (sends([item[2:] for item in todo], over=True) if todo else [])
        todo = long + todo
        for (name, q, _, _), v in zip(todo, got):
            if name == "late":
                parts[q] = [here[q], rest[q], swapped[q], v]
        for bit, pairs in vec_stages.get(t, []):
            (v,) = sends([(vec, pairs)], [blocks[0]])
            upper = (me >> bit) & 1 == 1
            vec = jnp.where(upper, jnp.stack([v, vec]), jnp.stack([vec, v]))
        if t == 0:
            vec = vec.transpose(4, 3, 2, 0, 1, 5).reshape(2, -1, width).astype(F32)
            layers[0].vec, layers[1].vec = vec[0], vec[1]
        if t >= 3:
            x = forward(t - 3, x)
        straight = {}
        for (name, q, _, _), v in zip(todo, got):
            if name == "last":
                rest[q] = v
            elif name == "z":
                straight.setdefault(q, [blocks[q]]).append(v)
            elif name == "swapped":
                swapped[q] = v
            elif name == "own":
                place(q, halves[q][0], v)
                here[q], here[q + 3] = blocks[q], blocks[q + 3]
            elif name in ("flat", "tall"):
                one = here[q].shape == blocks[q].shape
                joins.append((here, q, [here[q], v], jnp.stack if one else jnp.concatenate))
            elif name != "late":
                layers[q].other[name] = v
        for q, arrays in straight.items():
            joins.append((here, q, arrays, jnp.stack))
        step_end()

    order = [(1, 2), (1, 1), (1, 0), (0, 1), (0, 0), (0, 2)]
    dxs = {}

    def chain(l, kind):
        layer = layers[l]
        layer.info = infos[3 * l + kind in FLAT_GATHER]
        if kind == 2:
            dy = cot if l == 1 else dxs[1].astype(BF)
            (dy,) = tie(dy, extra=gate)
            dz, du = layer.down_back(l == 0, dy, parts[3 * l + 2])
            layer.other["dz"], layer.other["du"] = send(dz, swap), send(du, swap)
            now.append(layer.dr)
        elif kind == 1:
            (layer.dr,) = tie(layer.dr, extra=gate if l == 0 else ())
            layer.up_back(parts[3 * l + 1])
            now.append(layer.dr1)
        else:
            (dr1,) = tie(layer.dr1, extra=gate)
            layer.other["side"] = send(layer.attention_back(dr1, parts[3 * l]), swap)
            dxs[l] = layer.dx
            now.append(layer.dx)

    def weight(l, kind):
        shape = (8,) + blocks[kind].shape
        extra = ()
        if (l, kind) == order[-1]:
            keep, give = by_layer(layers[0].grad_vec(), layers[1].grad_vec())
            (got,) = sends([(give, swap)])
            entries = (keep + got).reshape(16, 2, -1).astype(BF)
            pad = shape[-1] - entries.shape[-1]
            extra = (jnp.pad(entries, ((0, 0), (0, 14), (0, pad))),)
            shape = (8, shape[1] + 16, shape[2])
        layers[l].info = infos[order.index((l, kind)) in FLAT_SUM]
        give, keep = layers[l].weight(kind, [shape, shape], extra)
        terms.append([keep])
        gives.append(give)
        now.extend([give, keep])

    def by_layer(a, b):
        return jnp.where(first, a, b), jnp.where(first, b, a)

    terms, gives = [], []
    work = [
        [(chain, 1, 2), (chain, 1, 1), (weight, 1, 2)],
        [(chain, 1, 0), (weight, 1, 1)],
        [(weight, 1, 0), (chain, 0, 2)],
        [(chain, 0, 1), (weight, 0, 1)],
        [(chain, 0, 0), (weight, 0, 0)],
        [(weight, 0, 2)],
    ]

    def part(arrays, lo, hi, kind):
        total = arrays[0][lo:hi].astype(F32)
        for v in arrays[1:]:
            total = total + v[lo:hi].astype(F32)
        return total.astype(kind)

    z_low, z_high = z_routes[2], z_routes[1]
    plan = {}
    for q in range(len(order)):
        steps = [(q + 1, last)]
        if q in FLAT_SUM:
            steps += [(q + 2, z_low), (q + 3, z_high), (FLAT_SUM[q], third)]
        else:
            steps += [(q + 2, third), (q + 3, None)]
        left = 16
        for t, pairs in steps:
            plan.setdefault(t, []).append((q, left, pairs))
            left //= 2

    sums = {}
    acts_keep, acts_give = by_layer(*results)
    extra = [("acts", acts_give)]
    kept = {"acts": acts_keep}
    got_extra = {}
    total_vec = None
    for t in range(len(order) + 4):
        todo = []
        for q, left, pairs in plan.get(t, []):
            if left == 16:
                todo.append(("long", q, gives[q], pairs))
                continue
            arrays = tie(*terms[q])
            if pairs is None:
                for j in (1, 2, 3):
                    todo.append(("tall", q, part(arrays, j, j + 1, BF), z_routes[j]))
            else:
                name = "flat" if pairs is third else "tall"
                todo.append((name, q, part(arrays, left // 2, left, BF), pairs))
        for name, v in extra:
            todo.append((name, 0, v, swap))
        extra = []
        long = [item for item in todo if item[0] == "long"]
        todo = [item for item in todo if item[0] != "long"]
        got = sends([item[2:] for item in long], long=True) if long else []
        got = got + (sends([item[2:] for item in todo]) if todo else [])
        todo = long + todo
        for f, l, kind in work[t] if t < len(work) else []:
            f(l, kind)
        step_end()
        for (name, q, _, _), v in zip(todo, got):
            if name in ("flat", "tall", "long"):
                terms[q].append(v)
            else:
                got_extra[name] = v
        if t == 4:
            kept["dx"], give_v = by_layer(dxs[0], dxs[1])
            extra.append(("dx", give_v))
        for q, left, pairs in plan.get(t, []):
            if left > 2 and pairs is not None:
                continue
            sums[order[q]] = part(terms[q], 0, 1, F32)[0]
            l, kind = order[q]
            if (1 - l, kind) not in sums:
                continue
            mine = sums[0, kind]
            if order[-1] == (0, kind):
                n_rows = blocks[kind].shape[0]
                total_vec = mine[n_rows : n_rows + 2, : vectors.shape[1] // 2].reshape(1, -1)
                mine = mine[:n_rows]
            kept[kind], give_v = by_layer(mine, sums[1, kind])
            extra.append((kind, give_v))
        if t == len(order) + 1:
            for name in ("acts", "dx"):
                kept[name], got_extra[name] = tie(kept[name], got_extra[name])

    def joined(name, axis):
        a, b = kept[name], got_extra[name]
        if axis is None:
            return jnp.where(first, jnp.stack([a, b]), jnp.stack([b, a]))
        return jnp.where(first, jnp.concatenate([a, b], axis), jnp.concatenate([b, a], axis))

    acts = joined("acts", None)[None]
    grads_in = joined("dx", None)[None]
    whole = [joined(0, 0), joined(1, 0), joined(2, 1)]

    def side_by_side(stack):
        return jnp.concatenate([stack[j] for j in range(stack.shape[0])], axis=1)[None]

    return (
        acts,
        grads_in,
        side_by_side(whole[0][:3]),
        whole[0][3][None],
        side_by_side(whole[1]),
        whole[2][None],
        total_vec,
    )


def plain_body(tokens, lengths, cotangent, w_qkv, w_out, w_up, w_down, vectors):
    core = lax.axis_index("section")
    first = core == 0
    chains_dev, length, width = tokens.shape
    swap = swap_route()
    size = lax.axis_size("dp")
    rows = w_out.shape[1]

    def gathered(w):
        return lax.all_gather(w, "dp", axis=0, tiled=True)

    def both(v):
        got = send(v, swap)
        return jnp.where(first, v, got), jnp.where(first, got, v)

    def chunks(w):
        return jnp.stack([w[:, j * width : (j + 1) * width] for j in range(w.shape[1] // width)])

    att = jnp.concatenate([chunks(gathered(w_qkv[0])), gathered(w_out[0])[None]])
    up = chunks(gathered(w_up[0]))
    down = gathered(w_down[0])
    vec = gathered(vectors[0]).reshape(-1, width).astype(F32)
    att, up, down, vec = both(att), both(up), both(down), both(vec)
    info = jnp.stack([core, lengths[core]]).astype(jnp.int32)
    layers = [Layer(info, vec[l], length, width) for l in range(2)]
    x = lax.dynamic_index_in_dim(tokens, core, 0, keepdims=False)
    dy = lax.dynamic_index_in_dim(cotangent, core, 0, keepdims=False)
    results = []
    for l in range(2):
        layer = layers[l]
        pack = layer.attention(x, [att[l]])
        act = layer.up(pack, [up[l]])
        layer.other["pack"], layer.other["act"] = send(pack, swap), send(act, swap)
        y = layer.down(act, [down[l]])
        results.append(y)
        x = y.astype(BF)
    stacked, tall = [(2, width, width)], [(4 * width, width // 2)]
    grads = {}
    dxs = {}
    for l in (1, 0):
        layer = layers[l]
        dz, du = layer.down_back(l == 0, dy, [down[l]])
        layer.other["dz"], layer.other["du"] = send(dz, swap), send(du, swap)
        layer.up_back([up[l]])
        layer.other["side"] = send(layer.attention_back(layer.dr1, [att[l]]), swap)
        for kind in range(3):
            (grads[l, kind],) = layer.weight(kind, tall if kind == 2 else stacked)
        dxs[l] = layer.dx
        dy = layer.dx.astype(BF)

    def by_layer(a, b):
        return jnp.where(first, a, b), send(jnp.where(first, b, a), swap)

    def chains(a, b):
        keep, got = by_layer(a, b)
        return jnp.where(first, jnp.stack([keep, got]), jnp.stack([got, keep]))[None]

    def scattered(total):
        dim = total.ndim - 2 if total.ndim > 1 else 0
        return lax.psum_scatter(total, "dp", scatter_dimension=dim, tiled=True).astype(F32)

    def summed(kind, axis):
        keep, got = by_layer(scattered(grads[0, kind]), scattered(grads[1, kind]))
        left, right = jnp.where(first, keep, got), jnp.where(first, got, keep)
        return jnp.concatenate([left, right], axis)

    def side_by_side(stack):
        return jnp.concatenate([stack[j] for j in range(stack.shape[0])], axis=1)[None]

    g_att, g_up, g_down = summed(0, 0), summed(1, 0), summed(2, 1)
    keep, got = by_layer(layers[0].grad_vec(), layers[1].grad_vec())
    g_vec = scattered((keep + got).reshape(-1))
    return (
        chains(*results),
        chains(dxs[0], dxs[1]),
        side_by_side(g_att[:3]),
        g_att[3][None],
        side_by_side(g_up),
        g_down[None],
        g_vec[None],
    )


def solution(mesh):
    placed = (
        P("dp", None, None),
        P("dp"),
        P("dp", None, None),
        P("section", "dp", None),
        P("section", "dp", None),
        P("section", "dp", None),
        P("section", "dp", None),
        P("section", "dp"),
    )
    return jax.shard_map(
        cube_body if mesh.shape["dp"] == 16 else plain_body,
        mesh=mesh,
        in_specs=placed,
        out_specs=(
            P("section", "dp", None, None),
            P("section", "dp", None, None),
            P("section", "dp", None),
            P("section", "dp", None),
            P("section", "dp", None),
            P("section", "dp", None),
            P("section", "dp"),
        ),
        check_vma=False,
    )
```

```python
import functools

import jax
import jax.numpy as jnp
from jax import lax
from jax.experimental import pallas as pl
from jax.experimental.pallas import tpu as pltpu
from jax.sharding import PartitionSpec as P

HEADS = 12
BF = jnp.bfloat16
F32 = jnp.float32
EPS = 1e-06
FILL = -1000000000.0
ROOT_HALF = 0.7071067811865476
INV_ROOT_TWO_PI = 0.3989422804014327
VMEM_BYTES = 24 * 1024 * 1024
ALL = ("section", "dp")
WINDOW = 1
DIRECT = 2
FLAT_GATHER = {3: 0, 5: 3}
FLAT_SUM = {}


def nn(a, b):
    return lax.dot_general(a, b, (((1,), (0,)), ((), ())), preferred_element_type=F32)


def nt(a, b):
    return lax.dot_general(a, b, (((1,), (1,)), ((), ())), preferred_element_type=F32)


def tn(a, b):
    return lax.dot_general(a, b, (((0,), (0,)), ((), ())), preferred_element_type=F32)


def norm(r, gain, shift):
    mean = jnp.mean(r, axis=-1, keepdims=True)
    cent = r - mean
    inv = lax.rsqrt(jnp.mean(cent * cent, axis=-1, keepdims=True) + EPS)
    n = cent * inv
    return n * gain + shift, n, inv


def norm_back(dy, n, inv, gain):
    t = dy * gain
    dr = inv * (
        t - jnp.mean(t, axis=-1, keepdims=True) - n * jnp.mean(t * n, axis=-1, keepdims=True)
    )
    return dr, jnp.sum(dy * n, axis=0, keepdims=True), jnp.sum(dy, axis=0, keepdims=True)


def load_weight(info, parts, dst, sem, stacked):
    if len(parts) == 1:
        copy = pltpu.make_async_copy(parts[0], dst, sem)
        copy.start()
        return copy
    blocks = sum(part.shape[0] for part in parts) // 2
    rows = parts[0].shape[-2]
    slot = 0
    for part in parts:
        for s in range(part.shape[0]):
            half = info[0] if slot < blocks else 1 - info[0]
            at = pl.ds(pl.multiple_of(info[2 + slot] * rows, 16), rows)
            if stacked:
                window = (pl.ds(2 * half, 2), at)
            else:
                cols = part.shape[-1]
                window = (at, pl.ds(pl.multiple_of(half * cols, 128), cols))
            pltpu.make_async_copy(part.at[s], dst.at[window], sem).start()
            slot += 1
    return pltpu.make_async_copy(dst, dst, sem)


def store_grad(info, src, outs, sem, stacked):
    if len(outs) == 1:
        copy = pltpu.make_async_copy(src, outs[0], sem)
        copy.start()
        return copy
    near = outs[1].shape[0]
    rows = outs[0].shape[-2]
    for out, base in ((outs[0], near), (outs[1], 0)):
        for s in range(out.shape[0]):
            at = pl.ds(pl.multiple_of(info[2 + base + s] * rows, 16), rows)
            window = (slice(None), at) if stacked else (at,)
            pltpu.make_async_copy(src.at[window], out.at[s], sem).start()
    return pltpu.make_async_copy(src, src, sem)


def attention_forward(n_w, info, x, vec, *refs):
    parts, refs = refs[:n_w], refs[n_w:]
    qkv, soft, pack, hidden, normed, inv, w, sem = refs
    load_weight(info, parts, w, sem, True).wait()
    xb = x[...]
    length, width = xb.shape
    q = (nn(xb, w[0]) + vec[0:1]).astype(BF)
    k = nn(xb, w[1]).astype(BF)
    v = (nn(xb, w[2]) + vec[1:2]).astype(BF)
    qkv[0] = q
    qkv[1] = k
    qkv[2] = v
    size = width // HEADS
    pair = 2 * size
    low_half = lax.broadcasted_iota(jnp.int32, (length, pair), 1) < size
    valid = lax.broadcasted_iota(jnp.int32, (length, length), 1) < info[1]
    for p in range(HEADS // 2):
        at = slice(p * pair, (p + 1) * pair)
        qp, kp, vp = q[:, at], k[:, at], v[:, at]
        sides = []
        for e in range(2):
            qm = jnp.where(low_half if e == 0 else ~low_half, qp, jnp.zeros_like(qp))
            s = jnp.where(valid, nt(qm, kp) * size ** (-0.5), FILL)
            ex = jnp.exp(s - jnp.max(s, axis=-1, keepdims=True))
            a = ex / jnp.sum(ex, axis=-1, keepdims=True)
            soft[2 * p + e] = a
            sides.append(nn(a.astype(BF), vp))
        pack[1, :, at] = jnp.where(low_half, sides[0], sides[1]).astype(BF)
    pack[0] = xb
    r = xb.astype(F32) + (nn(pack[1], w[3]) + vec[2:3])
    h, normed[...], inv[...] = norm(r, vec[3:4], vec[4:5])
    hidden[...] = h
    pack[2] = h.astype(BF)


def up_forward(n_w, info, pack, vec, *refs):
    parts, refs = refs[:n_w], refs[n_w:]
    act, slope, w, sem = refs
    load_weight(info, parts, w, sem, True).wait()
    hb = pack[2]
    for j in range(4):
        u = nn(hb, w[j]) + vec[8 + j : 9 + j]
        cdf = 0.5 * (1.0 + lax.erf(u * ROOT_HALF))
        act[:, j * u.shape[1] : (j + 1) * u.shape[1]] = (u * cdf).astype(BF)
        slope[j] = cdf + u * INV_ROOT_TWO_PI * jnp.exp(-0.5 * u * u)


def down_forward(n_w, info, act, hidden, vec, *refs):
    parts, refs = refs[:n_w], refs[n_w:]
    out, normed, inv, w, sem = refs
    load_weight(info, parts, w, sem, False).wait()
    r = hidden[...] + (nn(act[...], w[...]) + vec[5:6])
    out[...], normed[...], inv[...] = norm(r, vec[6:7], vec[7:8])


def down_backward(first, n_w, info, dy, normed, inv, slope, vec, *refs):
    parts, refs = refs[:n_w], refs[n_w:]
    dr, dz_keep, dz_give, du, du_give, dvec, w, sem = refs
    load = load_weight(info, parts, w, sem, False)
    g = dy[...].astype(F32)
    if not first:
        rows = lax.broadcasted_iota(jnp.int32, g.shape, 0)
        g = jnp.where(rows < info[1], g, 0.0)
    grad, dgain, dshift = norm_back(g, normed[...], inv[...], vec[6:7])
    dr[...] = grad
    dz = grad.astype(BF)
    dvec[0:1] = jnp.sum(dz.astype(F32), axis=0, keepdims=True)
    dvec[1:2] = dgain
    dvec[2:3] = dshift
    dvec[7:8] = jnp.zeros_like(dshift)
    half = dz.shape[1] // 2
    left, right = dz[:, :half], dz[:, half:]
    on_left = info[0] == 0
    dz_keep[...] = jnp.where(on_left, left, right)
    dz_give[...] = jnp.where(on_left, right, left)
    depth = dz.shape[1]
    load.wait()
    for j in range(4):
        at = slice(j * depth, (j + 1) * depth)
        low = (nt(dz, w[at]) * slope[j]).astype(BF)
        du[j] = low
        dvec[3 + j : 4 + j] = jnp.sum(low.astype(F32), axis=0, keepdims=True)
    for j in range(2):
        du_give[j] = du[2 * (1 - info[0]) + j]


def up_backward(n_w, info, du, dr, normed, inv, vec, *refs):
    parts, refs = refs[:n_w], refs[n_w:]
    dr1, dvec, w, sem = refs
    load_weight(info, parts, w, sem, True).wait()
    dh = dr[...]
    for j in range(4):
        dh += nt(du[j], w[j])
    grad, dgain, dshift = norm_back(dh, normed[...], inv[...], vec[3:4])
    dr1[...] = grad
    dvec[0:1] = jnp.sum(grad.astype(BF).astype(F32), axis=0, keepdims=True)
    dvec[1:2] = dgain
    dvec[2:3] = dshift
    dvec[3:8] = jnp.zeros((5, dshift.shape[1]), F32)


def attention_backward(n_w, info, dr1, qkv, soft, *refs):
    parts, refs = refs[:n_w], refs[n_w:]
    dx, side, side_give, dvec, w, sem = refs
    load = load_weight(info, parts, w, sem, True)
    db = dr1[...].astype(BF)
    load.wait()
    do = nt(db, w[3]).astype(BF)
    length, width = do.shape
    size = width // HEADS
    pair = 2 * size
    scale = size ** (-0.5)
    low_half = lax.broadcasted_iota(jnp.int32, (length, pair), 1) < size
    for p in range(HEADS // 2):
        at = slice(p * pair, (p + 1) * pair)
        qp, kp, vp, dop = qkv[0, :, at], qkv[1, :, at], qkv[2, :, at], do[:, at]
        dqs, dks, dvs = [], [], []
        for e in range(2):
            dom = jnp.where(low_half if e == 0 else ~low_half, dop, jnp.zeros_like(dop))
            a = soft[2 * p + e]
            da = nt(dom, vp)
            ds = (a * (da - jnp.sum(a * da, axis=-1, keepdims=True))).astype(BF)
            dvs.append(tn(a.astype(BF), dop))
            dqs.append(nn(ds, kp))
            dks.append(tn(ds, qp))
        side[0, :, at] = (jnp.where(low_half, dqs[0], dqs[1]) * scale).astype(BF)
        side[1, :, at] = (jnp.where(low_half, dks[0], dks[1]) * scale).astype(BF)
        side[2, :, at] = jnp.where(low_half, dvs[0], dvs[1]).astype(BF)
    side[3] = db
    total = dr1[...]
    for j in range(3):
        total += nt(side[j], w[j])
    dx[...] = total
    dvec[0:1] = jnp.sum(side[0].astype(F32), axis=0, keepdims=True)
    dvec[1:2] = jnp.sum(side[2].astype(F32), axis=0, keepdims=True)
    dvec[2:8] = jnp.zeros((6, width), F32)
    for j in range(2):
        side_give[j] = side[2 * (1 - info[0]) + j]


def down_weight(rows_too, info, act, act_other, dz, dz_other, *refs):
    if rows_too:
        extra, refs = refs[0], refs[1:]
    outs, (dw, sem) = refs[:-2], refs[-2:]
    right = jnp.concatenate([dz[...], dz_other[...]], axis=0)
    depth = dw.shape[0] // 4
    for j in range(4):
        at = slice(j * depth, (j + 1) * depth)
        left = jnp.concatenate([act[:, at], act_other[:, at]], axis=0)
        dw[at] = tn(left, right).astype(BF)
    if not rows_too:
        store_grad(info, dw, outs, sem, False).wait()
        return
    near = outs[1].shape[0]
    rows = dw.shape[0] // (2 * near)
    more = outs[0].shape[-2] - rows
    for out, base in ((outs[0], near), (outs[1], 0)):
        for s in range(out.shape[0]):
            owner = info[2 + base + s]
            at = pl.ds(pl.multiple_of(owner * rows, 16), rows)
            pltpu.make_async_copy(dw.at[at], out.at[s, pl.ds(0, rows)], sem).start()
            pltpu.make_async_copy(extra.at[owner], out.at[s, pl.ds(rows, more)], sem).start()
    pltpu.make_async_copy(dw, dw, sem).wait()
    pltpu.make_async_copy(extra, extra, sem).wait()


def up_weight(info, pack, pack_other, du, du_other, *refs):
    outs, (dw, sem) = refs[:-2], refs[-2:]
    left = jnp.concatenate([pack[2], pack_other[2]], axis=0)
    for j in range(2):
        right = jnp.concatenate([du[2 * info[0] + j], du_other[j]], axis=0)
        dw[j] = tn(left, right).astype(BF)
    store_grad(info, dw, outs, sem, True).wait()


def attention_weight(info, pack, pack_other, side, side_other, *refs):
    outs, (dw, sem) = refs[:-2], refs[-2:]
    left = jnp.concatenate([pack[0], pack_other[0]], axis=0)
    last = jnp.concatenate([pack[1], pack_other[1]], axis=0)
    for j in range(2):
        right = jnp.concatenate([side[2 * info[0] + j], side_other[j]], axis=0)
        if j == 1:
            left = jnp.where(info[0] == 0, left, last)
        dw[j] = tn(left, right).astype(BF)
    store_grad(info, dw, outs, sem, True).wait()


def call(kernel, info, small, parts, grads, outs, scratch, flops, nbytes):
    vmem = pl.BlockSpec(memory_space=pltpu.VMEM)
    hbm = pl.BlockSpec(memory_space=pl.ANY)
    shapes = [jax.ShapeDtypeStruct(s, BF) for s in grads]
    shapes += [jax.ShapeDtypeStruct(s, d) for s, d in outs]
    return pl.pallas_call(
        kernel,
        out_shape=shapes,
        in_specs=[pl.BlockSpec(memory_space=pltpu.SMEM)]
        + [vmem] * len(small)
        + [hbm] * len(parts),
        out_specs=[hbm] * len(grads) + [vmem] * len(outs),
        scratch_shapes=scratch,
        compiler_params=pltpu.CompilerParams(vmem_limit_bytes=VMEM_BYTES),
        cost_estimate=pl.CostEstimate(flops=1, bytes_accessed=1, transcendentals=0),
    )(info, *small, *parts)


class Layer:
    def __init__(self, info, vec, length, width):
        self.info, self.vec = info, vec
        self.length, self.width = length, width
        self.row = ((length, width), F32)
        self.low = ((length, width), BF)
        self.col = ((length, 1), F32)
        self.wide = (4, length, width)
        self.two = ((2, length, width), BF)
        self.half = ((length, width // 2), BF)
        self.size = 2 * length * width * width
        self.stack = pltpu.VMEM((4, width, width), BF)
        self.tall = pltpu.VMEM((4 * width, width), BF)
        self.bytes = 4 * width * width * 2
        self.sem = pltpu.SemaphoreType.DMA
        self.dvec = ((8, width), F32)
        self.other = {}

    def run(self, kernel, parts, small, outs, scratch, mults, grads=()):
        if parts:
            kernel = functools.partial(kernel, len(parts))
        return call(
            kernel, self.info, small, parts, grads, outs, scratch + [self.sem],
            mults * self.size, self.bytes,
        )

    def attention(self, x, parts):
        outs = [((3,) + self.low[0], BF), ((HEADS, self.length, self.length), F32)]
        outs += [((3,) + self.low[0], BF), self.row, self.row, self.col]
        got = self.run(attention_forward, parts, [x, self.vec], outs, [self.stack], 5)
        self.qkv, self.soft, self.pack, self.hidden, self.n1, self.s1 = got
        return self.pack

    def up(self, pack, parts):
        self.act, self.slope = self.run(
            up_forward, parts, [pack, self.vec],
            [((self.length, 4 * self.width), BF), (self.wide, F32)],
            [self.stack], 4,
        )
        return self.act

    def down(self, act, parts):
        out, self.n2, self.s2 = self.run(
            down_forward, parts, [act, self.hidden, self.vec], [self.row, self.row, self.col],
            [self.tall], 4,
        )
        return out

    def down_back(self, first, dy, parts):
        got = self.run(
            functools.partial(down_backward, first), parts,
            [dy, self.n2, self.s2, self.slope, self.vec],
            [self.row, self.half, self.half, (self.wide, BF), self.two, self.dvec],
            [self.tall], 4,
        )
        self.dr, self.dz, dz_give, self.du, du_give, self.dvec_down = got
        return dz_give, du_give

    def up_back(self, parts):
        self.dr1, self.dvec_up = self.run(
            up_backward, parts, [self.du, self.dr, self.n1, self.s1, self.vec],
            [self.row, self.dvec], [self.stack], 4,
        )

    def attention_back(self, dr1, parts):
        self.dx, self.side, give, self.dvec_att = self.run(
            attention_backward, parts, [dr1, self.qkv, self.soft],
            [self.row, (self.wide, BF), self.two, self.dvec], [self.stack], 7,
        )
        return give

    def weight(self, kind, grads, extra=()):
        o = self.other
        stack = pltpu.VMEM((2, self.width, self.width), BF)
        if kind == 2:
            stack = pltpu.VMEM((4 * self.width, self.width // 2), BF)
            small = [self.act, o["act"], self.dz, o["dz"], *extra]
            kernel = functools.partial(down_weight, len(extra) > 0)
        elif kind == 1:
            small = [self.pack, o["pack"], self.du, o["du"]]
            kernel = up_weight
        else:
            small = [self.pack, o["pack"], self.side, o["side"]]
            kernel = attention_weight
        return self.run(kernel, [], small, [], [stack], 4, grads)

    def grad_vec(self):
        d, u, a = self.dvec_down, self.dvec_up, self.dvec_att
        return jnp.concatenate([a[0:2], u[0:3], d[0:7]], axis=0)


def route(move):
    size = lax.axis_size("dp")
    pairs = []
    for s in range(2):
        for d in range(size):
            to_s, to_d = move(s, d)
            pairs.append((s * size + d, to_s * size + to_d))
    return pairs


def send(v, pairs):
    return lax.ppermute(v, ALL, pairs)


def after(v, *others):
    return lax.optimization_barrier((v,) + others)[0]


def cube_routes():
    return (
        route(lambda s, d: (s, d ^ (1 if s == 0 else 2))),
        route(lambda s, d: (s, d ^ (2 if s == 0 else 1))),
    )


def cube_owners(core, me, flat_first):
    slot = jnp.arange(16)
    third = jnp.where(core == 0, 1, 2)

    def table(a, b):
        masks = (a, 8, 4, b) if flat_first else (8, 4, a, b)
        return me ^ sum(((slot >> i) & 1) * m for i, m in enumerate(masks))

    return jnp.concatenate([table(third, 3 - third), table(3 - third, third)]).astype(jnp.int32)


def swap_route():
    return route(lambda s, d: (1 - s, d))


def cube_body(tokens, lengths, cotangent, w_qkv, w_out, w_up, w_down, vectors):
    core = lax.axis_index("section")
    me = lax.axis_index("dp")
    first = core == 0
    _, length, width = tokens.shape
    rows = w_out.shape[1]
    third, last = cube_routes()
    swap = swap_route()
    z_routes = {
        j: route(lambda s, d, m=m: (s, d ^ m)) for j, m in ((1, 8), (2, 4), (3, 12))
    }
    vec_sum_routes = [route(lambda s, d, i=i: (s, d ^ (1 << i))) for i in range(4)]

    def chunks(w):
        return jnp.stack([w[:, j * width : (j + 1) * width] for j in range(w.shape[1] // width)])

    blocks = [None] * 6
    own = [jnp.concatenate([chunks(w_qkv[0]), w_out])]

    def split(p):
        n = own[p].shape[0] // 2
        mine = lax.dynamic_slice_in_dim(own[p], n * core, n, 0)
        other = lax.dynamic_slice_in_dim(own[p], n * (1 - core), n, 0)
        return (mine, other) if n > 1 else (mine[0], other[0])

    def place(p, mine, other):
        blocks[p] = jnp.where(first, mine, other)
        blocks[p + 3] = jnp.where(first, other, mine)

    infos = [
        jnp.concatenate([core[None], lengths[core][None], cube_owners(core, me, flat)])
        for flat in (False, True)
    ]
    infos = [info.astype(jnp.int32) for info in infos]
    layers = [Layer(infos[0], None, length, width) for l in range(2)]

    history = [[], []]
    now = []

    def tie(*values, extra=()):
        deps = history[WINDOW] + list(extra)
        return lax.optimization_barrier(tuple(values) + tuple(deps))[: len(values)]

    gate = []

    slow, older = [[], []], []

    def sends(items, extra=(), long=False, over=False):
        more = [] if long else older if over else slow[0]
        values = tie(*[v for v, _ in items], extra=list(extra) + more)
        gate.extend(values)
        got = [send(v, pairs) for v, (_, pairs) in zip(values, items)]
        (slow[1] if long else now).extend(got)
        return got

    def step_end():
        history[:] = [history[1], list(now)]
        now[:] = []
        gate[:] = []
        older[:] = slow[0]
        slow[:] = [slow[1], []]

    parts = {}
    results = []
    exchange = []

    def forward(p, v):
        l, kind = divmod(p, 3)
        layer = layers[l]
        layer.info = infos[p in FLAT_GATHER]
        (v,) = tie(v, extra=gate)
        if kind == 0:
            v = layer.attention(v, parts[p])
            exchange.append((l, "pack", v))
        elif kind == 1:
            v = layer.up(v, parts[p])
            exchange.append((l, "act", v))
        else:
            v = layer.down(v, parts[p])
            results.append(v)
            v = v.astype(BF)
        now.append(v)
        return v

    rest, swapped = {}, {}
    n = len(blocks)
    halves = [split(0)]
    w_up, w_down, vectors, tokens, cotangent = lax.optimization_barrier(
        (w_up, w_down, vectors, tokens, cotangent, halves[0][1])
    )[:5]
    own.append(chunks(w_up[0]))
    own.append(jnp.stack([w_down[0][:, : width // 2], w_down[0][:, width // 2 :]]))
    halves += [split(1), split(2)]
    x = lax.dynamic_index_in_dim(tokens, core, 0, keepdims=False)
    cot = lax.dynamic_index_in_dim(cotangent, core, 0, keepdims=False)
    vec = jnp.stack([vectors[0], send(vectors[0], swap)])
    vec = jnp.where(first, vec, vec[::-1])
    vec_stages = {
        -1: [(3, z_routes[1]), (2, z_routes[2])],
        0: [(0, vec_sum_routes[0]), (1, vec_sum_routes[1])],
    }
    plan = {}

    def at_step(t, *item):
        plan.setdefault(t, []).append(item)

    for p in range(n):
        at_step(p + 1, "last", p, last)
        if p < DIRECT:
            for j in (1, 2, 3):
                at_step(p - 1, "z", p, z_routes[j])
            at_step(p, "flat", p, third)
        elif p in FLAT_GATHER:
            at_step(FLAT_GATHER[p], "flat", p, third)
            at_step(p - 1, "tall", p, z_routes[1])
            at_step(p, "tall", p, z_routes[2])
        else:
            early = p - 2 if p < 4 else p - 3
            at_step(early, "tall", p, z_routes[1])
            at_step(early + 1, "tall", p, z_routes[2])
            at_step(p, "flat", p, third)
        at_step(min(p + 3, n + 1), "late", p, swap)
        at_step(p + 1, "swapped", p, swap)

    for p in range(2):
        place(p, halves[p][0], send(halves[p][1], swap))
    here = dict(enumerate(blocks))
    joins = []
    for t in range(-1, n + 3):
        flat = [v for _, _, arrays, _ in joins for v in arrays]
        tied = list(tie(*flat)) if flat else []
        for where, q, arrays, join in joins:
            where[q] = join([tied.pop(0) for _ in arrays])
        joins = []
        todo = []
        for name, p, pairs in plan.get(t, []):
            todo.append((name, p, rest[p] if name == "late" else here[p], pairs))
        if t == -1:
            todo.append(("own", 2, halves[2][1], swap))
        for l, name, v in exchange:
            todo.append((name, l, v, swap))
        exchange.clear()
        long = [item for item in todo if item[0] == "last"]
        todo = [item for item in todo if item[0] != "last"]
        got = sends([item[2:] for item in long], long=True) if long else []
        got = got + (sends([item[2:] for item in todo], over=True) if todo else [])
        todo = long + todo
        for (name, q, _, _), v in zip(todo, got):
            if name == "late":
                parts[q] = [here[q], rest[q], swapped[q], v]
        for bit, pairs in vec_stages.get(t, []):
            (v,) = sends([(vec, pairs)], [blocks[0]])
            upper = (me >> bit) & 1 == 1
            vec = jnp.where(upper, jnp.stack([v, vec]), jnp.stack([vec, v]))
        if t == 0:
            vec = vec.transpose(4, 3, 2, 0, 1, 5).reshape(2, -1, width).astype(F32)
            layers[0].vec, layers[1].vec = vec[0], vec[1]
        if t >= 3:
            x = forward(t - 3, x)
        straight = {}
        for (name, q, _, _), v in zip(todo, got):
            if name == "last":
                rest[q] = v
            elif name == "z":
                straight.setdefault(q, [blocks[q]]).append(v)
            elif name == "swapped":
                swapped[q] = v
            elif name == "own":
                place(q, halves[q][0], v)
                here[q], here[q + 3] = blocks[q], blocks[q + 3]
            elif name in ("flat", "tall"):
                one = here[q].shape == blocks[q].shape
                joins.append((here, q, [here[q], v], jnp.stack if one else jnp.concatenate))
            elif name != "late":
                layers[q].other[name] = v
        for q, arrays in straight.items():
            joins.append((here, q, arrays, jnp.stack))
        step_end()

    order = [(1, 2), (1, 1), (1, 0), (0, 1), (0, 0), (0, 2)]
    dxs = {}

    def chain(l, kind):
        layer = layers[l]
        layer.info = infos[3 * l + kind in FLAT_GATHER]
        if kind == 2:
            dy = cot if l == 1 else dxs[1].astype(BF)
            (dy,) = tie(dy, extra=gate)
            dz, du = layer.down_back(l == 0, dy, parts[3 * l + 2])
            layer.other["dz"], layer.other["du"] = send(dz, swap), send(du, swap)
            now.append(layer.dr)
        elif kind == 1:
            (layer.dr,) = tie(layer.dr, extra=gate if l == 0 else ())
            layer.up_back(parts[3 * l + 1])
            now.append(layer.dr1)
        else:
            (dr1,) = tie(layer.dr1, extra=gate)
            layer.other["side"] = send(layer.attention_back(dr1, parts[3 * l]), swap)
            dxs[l] = layer.dx
            now.append(layer.dx)

    def weight(l, kind):
        shape = (8,) + blocks[kind].shape
        extra = ()
        if (l, kind) == order[-1]:
            keep, give = by_layer(layers[0].grad_vec(), layers[1].grad_vec())
            (got,) = sends([(give, swap)])
            entries = (keep + got).reshape(16, 2, -1).astype(BF)
            pad = shape[-1] - entries.shape[-1]
            extra = (jnp.pad(entries, ((0, 0), (0, 14), (0, pad))),)
            shape = (8, shape[1] + 16, shape[2])
        layers[l].info = infos[order.index((l, kind)) in FLAT_SUM]
        give, keep = layers[l].weight(kind, [shape, shape], extra)
        terms.append([keep])
        gives.append(give)
        now.extend([give, keep])

    def by_layer(a, b):
        return jnp.where(first, a, b), jnp.where(first, b, a)

    terms, gives = [], []
    work = [
        [(chain, 1, 2), (weight, 1, 2)],
        [(weight, 1, 1), (chain, 1, 1)],
        [(chain, 1, 0), (weight, 1, 0)],
        [(chain, 0, 2), (weight, 0, 1), (chain, 0, 1)],
        [(chain, 0, 0), (weight, 0, 0)],
        [(weight, 0, 2)],
    ]

    def part(arrays, lo, hi, kind):
        total = arrays[0][lo:hi].astype(F32)
        for v in arrays[1:]:
            total = total + v[lo:hi].astype(F32)
        return total.astype(kind)

    z_low, z_high = z_routes[2], z_routes[1]
    plan = {}
    for q in range(len(order)):
        steps = [(q + 1, last)]
        if q in FLAT_SUM:
            steps += [(q + 2, z_low), (q + 3, z_high), (FLAT_SUM[q], third)]
        else:
            steps += [(q + 2, third), (q + 3, None)]
        left = 16
        for t, pairs in steps:
            plan.setdefault(t, []).append((q, left, pairs))
            left //= 2

    sums = {}
    acts_keep, acts_give = by_layer(*results)
    extra = [("acts", acts_give)]
    kept = {"acts": acts_keep}
    got_extra = {}
    total_vec = None
    for t in range(len(order) + 4):
        todo = []
        for q, left, pairs in plan.get(t, []):
            if left == 16:
                todo.append(("long", q, gives[q], pairs))
                continue
            arrays = tie(*terms[q])
            if pairs is None:
                for j in (1, 2, 3):
                    todo.append(("tall", q, part(arrays, j, j + 1, BF), z_routes[j]))
            else:
                name = "flat" if pairs is third else "tall"
                todo.append((name, q, part(arrays, left // 2, left, BF), pairs))
        for name, v in extra:
            todo.append((name, 0, v, swap))
        extra = []
        long = [item for item in todo if item[0] == "long"]
        todo = [item for item in todo if item[0] != "long"]
        got = sends([item[2:] for item in long], long=True) if long else []
        got = got + (sends([item[2:] for item in todo]) if todo else [])
        todo = long + todo
        for f, l, kind in work[t] if t < len(work) else []:
            f(l, kind)
        step_end()
        for (name, q, _, _), v in zip(todo, got):
            if name in ("flat", "tall", "long"):
                terms[q].append(v)
            else:
                got_extra[name] = v
        if t == 4:
            kept["dx"], give_v = by_layer(dxs[0], dxs[1])
            extra.append(("dx", give_v))
        for q, left, pairs in plan.get(t, []):
            if left > 2 and pairs is not None:
                continue
            sums[order[q]] = part(terms[q], 0, 1, F32)[0]
            l, kind = order[q]
            if (1 - l, kind) not in sums:
                continue
            mine = sums[0, kind]
            if order[-1] == (0, kind):
                n_rows = blocks[kind].shape[0]
                total_vec = mine[n_rows : n_rows + 2, : vectors.shape[1] // 2].reshape(1, -1)
                mine = mine[:n_rows]
            kept[kind], give_v = by_layer(mine, sums[1, kind])
            extra.append((kind, give_v))
        if t == len(order) + 1:
            for name in ("acts", "dx"):
                kept[name], got_extra[name] = tie(kept[name], got_extra[name])

    def joined(name, axis):
        a, b = kept[name], got_extra[name]
        if axis is None:
            return jnp.where(first, jnp.stack([a, b]), jnp.stack([b, a]))
        return jnp.where(first, jnp.concatenate([a, b], axis), jnp.concatenate([b, a], axis))

    acts = joined("acts", None)[None]
    grads_in = joined("dx", None)[None]
    whole = [joined(0, 0), joined(1, 0), joined(2, 1)]

    def side_by_side(stack):
        return jnp.concatenate([stack[j] for j in range(stack.shape[0])], axis=1)[None]

    return (
        acts,
        grads_in,
        side_by_side(whole[0][:3]),
        whole[0][3][None],
        side_by_side(whole[1]),
        whole[2][None],
        total_vec,
    )


def plain_body(tokens, lengths, cotangent, w_qkv, w_out, w_up, w_down, vectors):
    core = lax.axis_index("section")
    first = core == 0
    chains_dev, length, width = tokens.shape
    swap = swap_route()
    size = lax.axis_size("dp")
    rows = w_out.shape[1]

    def gathered(w):
        return lax.all_gather(w, "dp", axis=0, tiled=True)

    def both(v):
        got = send(v, swap)
        return jnp.where(first, v, got), jnp.where(first, got, v)

    def chunks(w):
        return jnp.stack([w[:, j * width : (j + 1) * width] for j in range(w.shape[1] // width)])

    att = jnp.concatenate([chunks(gathered(w_qkv[0])), gathered(w_out[0])[None]])
    up = chunks(gathered(w_up[0]))
    down = gathered(w_down[0])
    vec = gathered(vectors[0]).reshape(-1, width).astype(F32)
    att, up, down, vec = both(att), both(up), both(down), both(vec)
    info = jnp.stack([core, lengths[core]]).astype(jnp.int32)
    layers = [Layer(info, vec[l], length, width) for l in range(2)]
    x = lax.dynamic_index_in_dim(tokens, core, 0, keepdims=False)
    dy = lax.dynamic_index_in_dim(cotangent, core, 0, keepdims=False)
    results = []
    for l in range(2):
        layer = layers[l]
        pack = layer.attention(x, [att[l]])
        act = layer.up(pack, [up[l]])
        layer.other["pack"], layer.other["act"] = send(pack, swap), send(act, swap)
        y = layer.down(act, [down[l]])
        results.append(y)
        x = y.astype(BF)
    stacked, tall = [(2, width, width)], [(4 * width, width // 2)]
    grads = {}
    dxs = {}
    for l in (1, 0):
        layer = layers[l]
        dz, du = layer.down_back(l == 0, dy, [down[l]])
        layer.other["dz"], layer.other["du"] = send(dz, swap), send(du, swap)
        layer.up_back([up[l]])
        layer.other["side"] = send(layer.attention_back(layer.dr1, [att[l]]), swap)
        for kind in range(3):
            (grads[l, kind],) = layer.weight(kind, tall if kind == 2 else stacked)
        dxs[l] = layer.dx
        dy = layer.dx.astype(BF)

    def by_layer(a, b):
        return jnp.where(first, a, b), send(jnp.where(first, b, a), swap)

    def chains(a, b):
        keep, got = by_layer(a, b)
        return jnp.where(first, jnp.stack([keep, got]), jnp.stack([got, keep]))[None]

    def scattered(total):
        dim = total.ndim - 2 if total.ndim > 1 else 0
        return lax.psum_scatter(total, "dp", scatter_dimension=dim, tiled=True).astype(F32)

    def summed(kind, axis):
        keep, got = by_layer(scattered(grads[0, kind]), scattered(grads[1, kind]))
        left, right = jnp.where(first, keep, got), jnp.where(first, got, keep)
        return jnp.concatenate([left, right], axis)

    def side_by_side(stack):
        return jnp.concatenate([stack[j] for j in range(stack.shape[0])], axis=1)[None]

    g_att, g_up, g_down = summed(0, 0), summed(1, 0), summed(2, 1)
    keep, got = by_layer(layers[0].grad_vec(), layers[1].grad_vec())
    g_vec = scattered((keep + got).reshape(-1))
    return (
        chains(*results),
        chains(dxs[0], dxs[1]),
        side_by_side(g_att[:3]),
        g_att[3][None],
        side_by_side(g_up),
        g_down[None],
        g_vec[None],
    )


def solution(mesh):
    placed = (
        P("dp", None, None),
        P("dp"),
        P("dp", None, None),
        P("section", "dp", None),
        P("section", "dp", None),
        P("section", "dp", None),
        P("section", "dp", None),
        P("section", "dp"),
    )
    return jax.shard_map(
        cube_body if mesh.shape["dp"] == 16 else plain_body,
        mesh=mesh,
        in_specs=placed,
        out_specs=(
            P("section", "dp", None, None),
            P("section", "dp", None, None),
            P("section", "dp", None),
            P("section", "dp", None),
            P("section", "dp", None),
            P("section", "dp", None),
            P("section", "dp"),
        ),
        check_vma=False,
    )
```

```python
import functools

import jax
import jax.numpy as jnp
from jax import lax
from jax.experimental import pallas as pl
from jax.experimental.pallas import tpu as pltpu
from jax.sharding import PartitionSpec as P

HEADS = 12
BF = jnp.bfloat16
F32 = jnp.float32
EPS = 1e-06
FILL = -1000000000.0
ROOT_HALF = 0.7071067811865476
INV_ROOT_TWO_PI = 0.3989422804014327
VMEM_BYTES = 24 * 1024 * 1024
ALL = ("section", "dp")
WINDOW = 1
DIRECT = 2
FLAT_GATHER = {3: 0, 5: 3}
FLAT_SUM = {}


def nn(a, b):
    return lax.dot_general(a, b, (((1,), (0,)), ((), ())), preferred_element_type=F32)


def nt(a, b):
    return lax.dot_general(a, b, (((1,), (1,)), ((), ())), preferred_element_type=F32)


def tn(a, b):
    return lax.dot_general(a, b, (((0,), (0,)), ((), ())), preferred_element_type=F32)


def norm(r, gain, shift):
    mean = jnp.mean(r, axis=-1, keepdims=True)
    cent = r - mean
    inv = lax.rsqrt(jnp.mean(cent * cent, axis=-1, keepdims=True) + EPS)
    n = cent * inv
    return n * gain + shift, n, inv


def norm_back(dy, n, inv, gain):
    t = dy * gain
    dr = inv * (
        t - jnp.mean(t, axis=-1, keepdims=True) - n * jnp.mean(t * n, axis=-1, keepdims=True)
    )
    return dr, jnp.sum(dy * n, axis=0, keepdims=True), jnp.sum(dy, axis=0, keepdims=True)


def load_weight(info, parts, dst, sem, stacked):
    if len(parts) == 1:
        copy = pltpu.make_async_copy(parts[0], dst, sem)
        copy.start()
        return copy
    blocks = sum(part.shape[0] for part in parts) // 2
    rows = parts[0].shape[-2]
    slot = 0
    for part in parts:
        for s in range(part.shape[0]):
            half = info[0] if slot < blocks else 1 - info[0]
            at = pl.ds(pl.multiple_of(info[2 + slot] * rows, 16), rows)
            if stacked:
                window = (pl.ds(2 * half, 2), at)
            else:
                cols = part.shape[-1]
                window = (at, pl.ds(pl.multiple_of(half * cols, 128), cols))
            pltpu.make_async_copy(part.at[s], dst.at[window], sem).start()
            slot += 1
    return pltpu.make_async_copy(dst, dst, sem)


def store_grad(info, src, outs, sem, stacked):
    if len(outs) == 1:
        copy = pltpu.make_async_copy(src, outs[0], sem)
        copy.start()
        return copy
    near = outs[1].shape[0]
    rows = outs[0].shape[-2]
    for out, base in ((outs[0], near), (outs[1], 0)):
        for s in range(out.shape[0]):
            at = pl.ds(pl.multiple_of(info[2 + base + s] * rows, 16), rows)
            window = (slice(None), at) if stacked else (at,)
            pltpu.make_async_copy(src.at[window], out.at[s], sem).start()
    return pltpu.make_async_copy(src, src, sem)


def attention_forward(n_w, info, x, vec, *refs):
    parts, refs = refs[:n_w], refs[n_w:]
    qkv, soft, pack, hidden, normed, inv, w, sem = refs
    load_weight(info, parts, w, sem, True).wait()
    xb = x[...]
    length, width = xb.shape
    q = (nn(xb, w[0]) + vec[0:1]).astype(BF)
    k = nn(xb, w[1]).astype(BF)
    v = (nn(xb, w[2]) + vec[1:2]).astype(BF)
    qkv[0] = q
    qkv[1] = k
    qkv[2] = v
    size = width // HEADS
    pair = 2 * size
    low_half = lax.broadcasted_iota(jnp.int32, (length, pair), 1) < size
    valid = lax.broadcasted_iota(jnp.int32, (length, length), 1) < info[1]
    for p in range(HEADS // 2):
        at = slice(p * pair, (p + 1) * pair)
        qp, kp, vp = q[:, at], k[:, at], v[:, at]
        sides = []
        for e in range(2):
            qm = jnp.where(low_half if e == 0 else ~low_half, qp, jnp.zeros_like(qp))
            s = jnp.where(valid, nt(qm, kp) * size ** (-0.5), FILL)
            ex = jnp.exp(s - jnp.max(s, axis=-1, keepdims=True))
            a = ex / jnp.sum(ex, axis=-1, keepdims=True)
            soft[2 * p + e] = a
            sides.append(nn(a.astype(BF), vp))
        pack[1, :, at] = jnp.where(low_half, sides[0], sides[1]).astype(BF)
    pack[0] = xb
    r = xb.astype(F32) + (nn(pack[1], w[3]) + vec[2:3])
    h, normed[...], inv[...] = norm(r, vec[3:4], vec[4:5])
    hidden[...] = h
    pack[2] = h.astype(BF)


def up_forward(n_w, info, pack, vec, *refs):
    parts, refs = refs[:n_w], refs[n_w:]
    act, slope, w, sem = refs
    load_weight(info, parts, w, sem, True).wait()
    hb = pack[2]
    for j in range(4):
        u = nn(hb, w[j]) + vec[8 + j : 9 + j]
        cdf = 0.5 * (1.0 + lax.erf(u * ROOT_HALF))
        act[:, j * u.shape[1] : (j + 1) * u.shape[1]] = (u * cdf).astype(BF)
        slope[j] = cdf + u * INV_ROOT_TWO_PI * jnp.exp(-0.5 * u * u)


def down_forward(n_w, info, act, hidden, vec, *refs):
    parts, refs = refs[:n_w], refs[n_w:]
    out, normed, inv, w, sem = refs
    load_weight(info, parts, w, sem, False).wait()
    r = hidden[...] + (nn(act[...], w[...]) + vec[5:6])
    out[...], normed[...], inv[...] = norm(r, vec[6:7], vec[7:8])


def down_backward(first, n_w, info, dy, normed, inv, slope, vec, *refs):
    parts, refs = refs[:n_w], refs[n_w:]
    dr, dz_keep, dz_give, du, du_give, dvec, w, sem = refs
    load = load_weight(info, parts, w, sem, False)
    g = dy[...].astype(F32)
    if not first:
        rows = lax.broadcasted_iota(jnp.int32, g.shape, 0)
        g = jnp.where(rows < info[1], g, 0.0)
    grad, dgain, dshift = norm_back(g, normed[...], inv[...], vec[6:7])
    dr[...] = grad
    dz = grad.astype(BF)
    dvec[0:1] = jnp.sum(dz.astype(F32), axis=0, keepdims=True)
    dvec[1:2] = dgain
    dvec[2:3] = dshift
    dvec[7:8] = jnp.zeros_like(dshift)
    half = dz.shape[1] // 2
    left, right = dz[:, :half], dz[:, half:]
    on_left = info[0] == 0
    dz_keep[...] = jnp.where(on_left, left, right)
    dz_give[...] = jnp.where(on_left, right, left)
    depth = dz.shape[1]
    load.wait()
    for j in range(4):
        at = slice(j * depth, (j + 1) * depth)
        low = (nt(dz, w[at]) * slope[j]).astype(BF)
        du[j] = low
        dvec[3 + j : 4 + j] = jnp.sum(low.astype(F32), axis=0, keepdims=True)
    for j in range(2):
        du_give[j] = du[2 * (1 - info[0]) + j]


def up_backward(n_w, info, du, dr, normed, inv, vec, *refs):
    parts, refs = refs[:n_w], refs[n_w:]
    dr1, dvec, w, sem = refs
    load_weight(info, parts, w, sem, True).wait()
    dh = dr[...]
    for j in range(4):
        dh += nt(du[j], w[j])
    grad, dgain, dshift = norm_back(dh, normed[...], inv[...], vec[3:4])
    dr1[...] = grad
    dvec[0:1] = jnp.sum(grad.astype(BF).astype(F32), axis=0, keepdims=True)
    dvec[1:2] = dgain
    dvec[2:3] = dshift
    dvec[3:8] = jnp.zeros((5, dshift.shape[1]), F32)


def attention_backward(n_w, info, dr1, qkv, soft, *refs):
    parts, refs = refs[:n_w], refs[n_w:]
    dx, side, side_give, dvec, w, sem = refs
    load = load_weight(info, parts, w, sem, True)
    db = dr1[...].astype(BF)
    load.wait()
    do = nt(db, w[3]).astype(BF)
    length, width = do.shape
    size = width // HEADS
    pair = 2 * size
    scale = size ** (-0.5)
    low_half = lax.broadcasted_iota(jnp.int32, (length, pair), 1) < size
    for p in range(HEADS // 2):
        at = slice(p * pair, (p + 1) * pair)
        qp, kp, vp, dop = qkv[0, :, at], qkv[1, :, at], qkv[2, :, at], do[:, at]
        dqs, dks, dvs = [], [], []
        for e in range(2):
            dom = jnp.where(low_half if e == 0 else ~low_half, dop, jnp.zeros_like(dop))
            a = soft[2 * p + e]
            da = nt(dom, vp)
            ds = (a * (da - jnp.sum(a * da, axis=-1, keepdims=True))).astype(BF)
            dvs.append(tn(a.astype(BF), dop))
            dqs.append(nn(ds, kp))
            dks.append(tn(ds, qp))
        side[0, :, at] = (jnp.where(low_half, dqs[0], dqs[1]) * scale).astype(BF)
        side[1, :, at] = (jnp.where(low_half, dks[0], dks[1]) * scale).astype(BF)
        side[2, :, at] = jnp.where(low_half, dvs[0], dvs[1]).astype(BF)
    side[3] = db
    total = dr1[...]
    for j in range(3):
        total += nt(side[j], w[j])
    dx[...] = total
    dvec[0:1] = jnp.sum(side[0].astype(F32), axis=0, keepdims=True)
    dvec[1:2] = jnp.sum(side[2].astype(F32), axis=0, keepdims=True)
    dvec[2:8] = jnp.zeros((6, width), F32)
    for j in range(2):
        side_give[j] = side[2 * (1 - info[0]) + j]


def down_weight(rows_too, info, act, act_other, dz, dz_other, *refs):
    if rows_too:
        extra, refs = refs[0], refs[1:]
    outs, (dw, sem) = refs[:-2], refs[-2:]
    right = jnp.concatenate([dz[...], dz_other[...]], axis=0)
    depth = dw.shape[0] // 4
    for j in range(4):
        at = slice(j * depth, (j + 1) * depth)
        left = jnp.concatenate([act[:, at], act_other[:, at]], axis=0)
        dw[at] = tn(left, right).astype(BF)
    if not rows_too:
        store_grad(info, dw, outs, sem, False).wait()
        return
    near = outs[1].shape[0]
    rows = dw.shape[0] // (2 * near)
    more = outs[0].shape[-2] - rows
    for out, base in ((outs[0], near), (outs[1], 0)):
        for s in range(out.shape[0]):
            owner = info[2 + base + s]
            at = pl.ds(pl.multiple_of(owner * rows, 16), rows)
            pltpu.make_async_copy(dw.at[at], out.at[s, pl.ds(0, rows)], sem).start()
            pltpu.make_async_copy(extra.at[owner], out.at[s, pl.ds(rows, more)], sem).start()
    pltpu.make_async_copy(dw, dw, sem).wait()
    pltpu.make_async_copy(extra, extra, sem).wait()


def up_weight(info, pack, pack_other, du, du_other, *refs):
    outs, (dw, sem) = refs[:-2], refs[-2:]
    left = jnp.concatenate([pack[2], pack_other[2]], axis=0)
    for j in range(2):
        right = jnp.concatenate([du[2 * info[0] + j], du_other[j]], axis=0)
        dw[j] = tn(left, right).astype(BF)
    store_grad(info, dw, outs, sem, True).wait()


def attention_weight(info, pack, pack_other, side, side_other, *refs):
    outs, (dw, sem) = refs[:-2], refs[-2:]
    left = jnp.concatenate([pack[0], pack_other[0]], axis=0)
    last = jnp.concatenate([pack[1], pack_other[1]], axis=0)
    for j in range(2):
        right = jnp.concatenate([side[2 * info[0] + j], side_other[j]], axis=0)
        if j == 1:
            left = jnp.where(info[0] == 0, left, last)
        dw[j] = tn(left, right).astype(BF)
    store_grad(info, dw, outs, sem, True).wait()


def call(kernel, info, small, parts, grads, outs, scratch, flops, nbytes):
    vmem = pl.BlockSpec(memory_space=pltpu.VMEM)
    hbm = pl.BlockSpec(memory_space=pl.ANY)
    shapes = [jax.ShapeDtypeStruct(s, BF) for s in grads]
    shapes += [jax.ShapeDtypeStruct(s, d) for s, d in outs]
    return pl.pallas_call(
        kernel,
        out_shape=shapes,
        in_specs=[pl.BlockSpec(memory_space=pltpu.SMEM)]
        + [vmem] * len(small)
        + [hbm] * len(parts),
        out_specs=[hbm] * len(grads) + [vmem] * len(outs),
        scratch_shapes=scratch,
        compiler_params=pltpu.CompilerParams(vmem_limit_bytes=VMEM_BYTES),
        cost_estimate=pl.CostEstimate(flops=1, bytes_accessed=1, transcendentals=0),
    )(info, *small, *parts)


class Layer:
    def __init__(self, info, vec, length, width):
        self.info, self.vec = info, vec
        self.length, self.width = length, width
        self.row = ((length, width), F32)
        self.low = ((length, width), BF)
        self.col = ((length, 1), F32)
        self.wide = (4, length, width)
        self.two = ((2, length, width), BF)
        self.half = ((length, width // 2), BF)
        self.size = 2 * length * width * width
        self.stack = pltpu.VMEM((4, width, width), BF)
        self.tall = pltpu.VMEM((4 * width, width), BF)
        self.bytes = 4 * width * width * 2
        self.sem = pltpu.SemaphoreType.DMA
        self.dvec = ((8, width), F32)
        self.other = {}

    def run(self, kernel, parts, small, outs, scratch, mults, grads=()):
        if parts:
            kernel = functools.partial(kernel, len(parts))
        return call(
            kernel, self.info, small, parts, grads, outs, scratch + [self.sem],
            mults * self.size, self.bytes,
        )

    def attention(self, x, parts):
        outs = [((3,) + self.low[0], BF), ((HEADS, self.length, self.length), F32)]
        outs += [((3,) + self.low[0], BF), self.row, self.row, self.col]
        got = self.run(attention_forward, parts, [x, self.vec], outs, [self.stack], 5)
        self.qkv, self.soft, self.pack, self.hidden, self.n1, self.s1 = got
        return self.pack

    def up(self, pack, parts):
        self.act, self.slope = self.run(
            up_forward, parts, [pack, self.vec],
            [((self.length, 4 * self.width), BF), (self.wide, F32)],
            [self.stack], 4,
        )
        return self.act

    def down(self, act, parts):
        out, self.n2, self.s2 = self.run(
            down_forward, parts, [act, self.hidden, self.vec], [self.row, self.row, self.col],
            [self.tall], 4,
        )
        return out

    def down_back(self, first, dy, parts):
        got = self.run(
            functools.partial(down_backward, first), parts,
            [dy, self.n2, self.s2, self.slope, self.vec],
            [self.row, self.half, self.half, (self.wide, BF), self.two, self.dvec],
            [self.tall], 4,
        )
        self.dr, self.dz, dz_give, self.du, du_give, self.dvec_down = got
        return dz_give, du_give

    def up_back(self, parts):
        self.dr1, self.dvec_up = self.run(
            up_backward, parts, [self.du, self.dr, self.n1, self.s1, self.vec],
            [self.row, self.dvec], [self.stack], 4,
        )

    def attention_back(self, dr1, parts):
        self.dx, self.side, give, self.dvec_att = self.run(
            attention_backward, parts, [dr1, self.qkv, self.soft],
            [self.row, (self.wide, BF), self.two, self.dvec], [self.stack], 7,
        )
        return give

    def weight(self, kind, grads, extra=()):
        o = self.other
        stack = pltpu.VMEM((2, self.width, self.width), BF)
        if kind == 2:
            stack = pltpu.VMEM((4 * self.width, self.width // 2), BF)
            small = [self.act, o["act"], self.dz, o["dz"], *extra]
            kernel = functools.partial(down_weight, len(extra) > 0)
        elif kind == 1:
            small = [self.pack, o["pack"], self.du, o["du"]]
            kernel = up_weight
        else:
            small = [self.pack, o["pack"], self.side, o["side"]]
            kernel = attention_weight
        return self.run(kernel, [], small, [], [stack], 4, grads)

    def grad_vec(self):
        d, u, a = self.dvec_down, self.dvec_up, self.dvec_att
        return jnp.concatenate([a[0:2], u[0:3], d[0:7]], axis=0)


def route(move):
    size = lax.axis_size("dp")
    pairs = []
    for s in range(2):
        for d in range(size):
            to_s, to_d = move(s, d)
            pairs.append((s * size + d, to_s * size + to_d))
    return pairs


def send(v, pairs):
    return lax.ppermute(v, ALL, pairs)


def after(v, *others):
    return lax.optimization_barrier((v,) + others)[0]


def cube_routes():
    return (
        route(lambda s, d: (s, d ^ (1 if s == 0 else 2))),
        route(lambda s, d: (s, d ^ (2 if s == 0 else 1))),
    )


def cube_owners(core, me, flat_first):
    slot = jnp.arange(16)
    third = jnp.where(core == 0, 1, 2)

    def table(a, b):
        masks = (a, 8, 4, b) if flat_first else (8, 4, a, b)
        return me ^ sum(((slot >> i) & 1) * m for i, m in enumerate(masks))

    return jnp.concatenate([table(third, 3 - third), table(3 - third, third)]).astype(jnp.int32)


def swap_route():
    return route(lambda s, d: (1 - s, d))


def cube_body(tokens, lengths, cotangent, w_qkv, w_out, w_up, w_down, vectors):
    core = lax.axis_index("section")
    me = lax.axis_index("dp")
    first = core == 0
    _, length, width = tokens.shape
    rows = w_out.shape[1]
    third, last = cube_routes()
    swap = swap_route()
    z_routes = {
        j: route(lambda s, d, m=m: (s, d ^ m)) for j, m in ((1, 8), (2, 4), (3, 12))
    }
    vec_sum_routes = [route(lambda s, d, i=i: (s, d ^ (1 << i))) for i in range(4)]

    def chunks(w):
        return jnp.stack([w[:, j * width : (j + 1) * width] for j in range(w.shape[1] // width)])

    blocks = [None] * 6
    own = [jnp.concatenate([chunks(w_qkv[0]), w_out])]

    def split(p):
        n = own[p].shape[0] // 2
        mine = lax.dynamic_slice_in_dim(own[p], n * core, n, 0)
        other = lax.dynamic_slice_in_dim(own[p], n * (1 - core), n, 0)
        return (mine, other) if n > 1 else (mine[0], other[0])

    def place(p, mine, other):
        blocks[p] = jnp.where(first, mine, other)
        blocks[p + 3] = jnp.where(first, other, mine)

    infos = [
        jnp.concatenate([core[None], lengths[core][None], cube_owners(core, me, flat)])
        for flat in (False, True)
    ]
    infos = [info.astype(jnp.int32) for info in infos]
    layers = [Layer(infos[0], None, length, width) for l in range(2)]

    history = [[], []]
    now = []

    def tie(*values, extra=()):
        deps = history[WINDOW] + list(extra)
        return lax.optimization_barrier(tuple(values) + tuple(deps))[: len(values)]

    gate = []

    slow, older = [[], []], []

    def sends(items, extra=(), long=False, over=False):
        more = [] if long else older if over else slow[0]
        values = tie(*[v for v, _ in items], extra=list(extra) + more)
        gate.extend(values)
        got = [send(v, pairs) for v, (_, pairs) in zip(values, items)]
        (slow[1] if long else now).extend(got)
        return got

    def step_end():
        history[:] = [history[1], list(now)]
        now[:] = []
        gate[:] = []
        older[:] = slow[0]
        slow[:] = [slow[1], []]

    parts = {}
    results = []
    exchange = []

    def forward(p, v):
        l, kind = divmod(p, 3)
        layer = layers[l]
        layer.info = infos[p in FLAT_GATHER]
        (v,) = tie(v, extra=gate)
        if kind == 0:
            v = layer.attention(v, parts[p])
            exchange.append((l, "pack", v))
        elif kind == 1:
            v = layer.up(v, parts[p])
            exchange.append((l, "act", v))
        else:
            v = layer.down(v, parts[p])
            results.append(v)
            v = v.astype(BF)
        now.append(v)
        return v

    rest, swapped = {}, {}
    n = len(blocks)
    halves = [split(0)]
    w_up, w_down, vectors, tokens, cotangent = lax.optimization_barrier(
        (w_up, w_down, vectors, tokens, cotangent, halves[0][1])
    )[:5]
    own.append(chunks(w_up[0]))
    own.append(jnp.stack([w_down[0][:, : width // 2], w_down[0][:, width // 2 :]]))
    halves += [split(1), split(2)]
    x = lax.dynamic_index_in_dim(tokens, core, 0, keepdims=False)
    cot = lax.dynamic_index_in_dim(cotangent, core, 0, keepdims=False)
    vec = jnp.stack([vectors[0], send(vectors[0], swap)])
    vec = jnp.where(first, vec, vec[::-1])
    vec_stages = {
        -1: [(3, z_routes[1]), (2, z_routes[2])],
        0: [(0, vec_sum_routes[0]), (1, vec_sum_routes[1])],
    }
    plan = {}

    def at_step(t, *item):
        plan.setdefault(t, []).append(item)

    for p in range(n):
        at_step(p + 1, "last", p, last)
        if p < DIRECT:
            for j in (1, 2, 3):
                at_step(p - 1, "z", p, z_routes[j])
            at_step(p, "flat", p, third)
        elif p in FLAT_GATHER:
            at_step(FLAT_GATHER[p], "flat", p, third)
            at_step(p - 1, "tall", p, z_routes[1])
            at_step(p, "tall", p, z_routes[2])
        else:
            early = p - 2 if p < 4 else p - 3
            at_step(early, "tall", p, z_routes[1])
            at_step(early + 1, "tall", p, z_routes[2])
            at_step(p, "flat", p, third)
        at_step(min(p + 3, n + 1), "late", p, swap)
        at_step(p + 1, "swapped", p, swap)

    for p in range(2):
        place(p, halves[p][0], send(halves[p][1], swap))
    here = dict(enumerate(blocks))
    joins = []
    for t in range(-1, n + 3):
        flat = [v for _, _, arrays, _ in joins for v in arrays]
        tied = list(tie(*flat)) if flat else []
        for where, q, arrays, join in joins:
            where[q] = join([tied.pop(0) for _ in arrays])
        joins = []
        todo = []
        for name, p, pairs in plan.get(t, []):
            todo.append((name, p, rest[p] if name == "late" else here[p], pairs))
        if t == -1:
            todo.append(("own", 2, halves[2][1], swap))
        for l, name, v in exchange:
            todo.append((name, l, v, swap))
        exchange.clear()
        long = [item for item in todo if item[0] == "last"]
        todo = [item for item in todo if item[0] != "last"]
        got = sends([item[2:] for item in long], long=True) if long else []
        got = got + (sends([item[2:] for item in todo], over=True) if todo else [])
        todo = long + todo
        for (name, q, _, _), v in zip(todo, got):
            if name == "late":
                parts[q] = [here[q], rest[q], swapped[q], v]
        for bit, pairs in vec_stages.get(t, []):
            (v,) = sends([(vec, pairs)], [blocks[0]])
            upper = (me >> bit) & 1 == 1
            vec = jnp.where(upper, jnp.stack([v, vec]), jnp.stack([vec, v]))
        if t == 0:
            vec = vec.transpose(4, 3, 2, 0, 1, 5).reshape(2, -1, width).astype(F32)
            layers[0].vec, layers[1].vec = vec[0], vec[1]
        if t >= 3:
            x = forward(t - 3, x)
        straight = {}
        for (name, q, _, _), v in zip(todo, got):
            if name == "last":
                rest[q] = v
            elif name == "z":
                straight.setdefault(q, [blocks[q]]).append(v)
            elif name == "swapped":
                swapped[q] = v
            elif name == "own":
                place(q, halves[q][0], v)
                here[q], here[q + 3] = blocks[q], blocks[q + 3]
            elif name in ("flat", "tall"):
                one = here[q].shape == blocks[q].shape
                joins.append((here, q, [here[q], v], jnp.stack if one else jnp.concatenate))
            elif name != "late":
                layers[q].other[name] = v
        for q, arrays in straight.items():
            joins.append((here, q, arrays, jnp.stack))
        step_end()

    order = [(1, 2), (1, 1), (1, 0), (0, 1), (0, 0), (0, 2)]
    dxs = {}

    def chain(l, kind):
        layer = layers[l]
        layer.info = infos[3 * l + kind in FLAT_GATHER]
        if kind == 2:
            dy = cot if l == 1 else dxs[1].astype(BF)
            (dy,) = tie(dy, extra=gate)
            dz, du = layer.down_back(l == 0, dy, parts[3 * l + 2])
            layer.other["dz"], layer.other["du"] = send(dz, swap), send(du, swap)
            now.append(layer.dr)
        elif kind == 1:
            (layer.dr,) = tie(layer.dr, extra=gate if l == 0 else ())
            layer.up_back(parts[3 * l + 1])
            now.append(layer.dr1)
        else:
            (dr1,) = tie(layer.dr1, extra=gate)
            layer.other["side"] = send(layer.attention_back(dr1, parts[3 * l]), swap)
            dxs[l] = layer.dx
            now.append(layer.dx)

    def weight(l, kind):
        shape = (8,) + blocks[kind].shape
        extra = ()
        if (l, kind) == order[-1]:
            keep, give = by_layer(layers[0].grad_vec(), layers[1].grad_vec())
            (got,) = sends([(give, swap)])
            entries = (keep + got).reshape(16, 2, -1).astype(BF)
            pad = shape[-1] - entries.shape[-1]
            extra = (jnp.pad(entries, ((0, 0), (0, 14), (0, pad))),)
            shape = (8, shape[1] + 16, shape[2])
        layers[l].info = infos[order.index((l, kind)) in FLAT_SUM]
        give, keep = layers[l].weight(kind, [shape, shape], extra)
        terms.append([keep])
        gives.append(give)
        now.extend([give, keep])

    def by_layer(a, b):
        return jnp.where(first, a, b), jnp.where(first, b, a)

    terms, gives = [], []
    work = [
        [(chain, 1, 2), (weight, 1, 2)],
        [(weight, 1, 1), (chain, 1, 1)],
        [(chain, 1, 0), (weight, 1, 0), (chain, 0, 2)],
        [(weight, 0, 1), (chain, 0, 1)],
        [(chain, 0, 0), (weight, 0, 0)],
        [(weight, 0, 2)],
    ]

    def part(arrays, lo, hi, kind):
        total = arrays[0][lo:hi].astype(F32)
        for v in arrays[1:]:
            total = total + v[lo:hi].astype(F32)
        return total.astype(kind)

    z_low, z_high = z_routes[2], z_routes[1]
    plan = {}
    for q in range(len(order)):
        steps = [(q + 1, last)]
        if q in FLAT_SUM:
            steps += [(q + 2, z_low), (q + 3, z_high), (FLAT_SUM[q], third)]
        else:
            steps += [(q + 2, third), (q + 3, None)]
        left = 16
        for t, pairs in steps:
            plan.setdefault(t, []).append((q, left, pairs))
            left //= 2

    sums = {}
    acts_keep, acts_give = by_layer(*results)
    extra = [("acts", acts_give)]
    kept = {"acts": acts_keep}
    got_extra = {}
    total_vec = None
    for t in range(len(order) + 4):
        todo = []
        for q, left, pairs in plan.get(t, []):
            if left == 16:
                todo.append(("long", q, gives[q], pairs))
                continue
            arrays = tie(*terms[q])
            if pairs is None:
                for j in (1, 2, 3):
                    todo.append(("tall", q, part(arrays, j, j + 1, BF), z_routes[j]))
            else:
                name = "flat" if pairs is third else "tall"
                todo.append((name, q, part(arrays, left // 2, left, BF), pairs))
        for name, v in extra:
            todo.append((name, 0, v, swap))
        extra = []
        long = [item for item in todo if item[0] == "long"]
        todo = [item for item in todo if item[0] != "long"]
        got = sends([item[2:] for item in long], long=True) if long else []
        got = got + (sends([item[2:] for item in todo]) if todo else [])
        todo = long + todo
        for f, l, kind in work[t] if t < len(work) else []:
            f(l, kind)
        step_end()
        for (name, q, _, _), v in zip(todo, got):
            if name in ("flat", "tall", "long"):
                terms[q].append(v)
            else:
                got_extra[name] = v
        if t == 4:
            kept["dx"], give_v = by_layer(dxs[0], dxs[1])
            extra.append(("dx", give_v))
        for q, left, pairs in plan.get(t, []):
            if left > 2 and pairs is not None:
                continue
            sums[order[q]] = part(terms[q], 0, 1, F32)[0]
            l, kind = order[q]
            if (1 - l, kind) not in sums:
                continue
            mine = sums[0, kind]
            if order[-1] == (0, kind):
                n_rows = blocks[kind].shape[0]
                total_vec = mine[n_rows : n_rows + 2, : vectors.shape[1] // 2].reshape(1, -1)
                mine = mine[:n_rows]
            kept[kind], give_v = by_layer(mine, sums[1, kind])
            extra.append((kind, give_v))
        if t == len(order) + 1:
            for name in ("acts", "dx"):
                kept[name], got_extra[name] = tie(kept[name], got_extra[name])

    def joined(name, axis):
        a, b = kept[name], got_extra[name]
        if axis is None:
            return jnp.where(first, jnp.stack([a, b]), jnp.stack([b, a]))
        return jnp.where(first, jnp.concatenate([a, b], axis), jnp.concatenate([b, a], axis))

    acts = joined("acts", None)[None]
    grads_in = joined("dx", None)[None]
    whole = [joined(0, 0), joined(1, 0), joined(2, 1)]

    def side_by_side(stack):
        return jnp.concatenate([stack[j] for j in range(stack.shape[0])], axis=1)[None]

    return (
        acts,
        grads_in,
        side_by_side(whole[0][:3]),
        whole[0][3][None],
        side_by_side(whole[1]),
        whole[2][None],
        total_vec,
    )


def plain_body(tokens, lengths, cotangent, w_qkv, w_out, w_up, w_down, vectors):
    core = lax.axis_index("section")
    first = core == 0
    chains_dev, length, width = tokens.shape
    swap = swap_route()
    size = lax.axis_size("dp")
    rows = w_out.shape[1]

    def gathered(w):
        return lax.all_gather(w, "dp", axis=0, tiled=True)

    def both(v):
        got = send(v, swap)
        return jnp.where(first, v, got), jnp.where(first, got, v)

    def chunks(w):
        return jnp.stack([w[:, j * width : (j + 1) * width] for j in range(w.shape[1] // width)])

    att = jnp.concatenate([chunks(gathered(w_qkv[0])), gathered(w_out[0])[None]])
    up = chunks(gathered(w_up[0]))
    down = gathered(w_down[0])
    vec = gathered(vectors[0]).reshape(-1, width).astype(F32)
    att, up, down, vec = both(att), both(up), both(down), both(vec)
    info = jnp.stack([core, lengths[core]]).astype(jnp.int32)
    layers = [Layer(info, vec[l], length, width) for l in range(2)]
    x = lax.dynamic_index_in_dim(tokens, core, 0, keepdims=False)
    dy = lax.dynamic_index_in_dim(cotangent, core, 0, keepdims=False)
    results = []
    for l in range(2):
        layer = layers[l]
        pack = layer.attention(x, [att[l]])
        act = layer.up(pack, [up[l]])
        layer.other["pack"], layer.other["act"] = send(pack, swap), send(act, swap)
        y = layer.down(act, [down[l]])
        results.append(y)
        x = y.astype(BF)
    stacked, tall = [(2, width, width)], [(4 * width, width // 2)]
    grads = {}
    dxs = {}
    for l in (1, 0):
        layer = layers[l]
        dz, du = layer.down_back(l == 0, dy, [down[l]])
        layer.other["dz"], layer.other["du"] = send(dz, swap), send(du, swap)
        layer.up_back([up[l]])
        layer.other["side"] = send(layer.attention_back(layer.dr1, [att[l]]), swap)
        for kind in range(3):
            (grads[l, kind],) = layer.weight(kind, tall if kind == 2 else stacked)
        dxs[l] = layer.dx
        dy = layer.dx.astype(BF)

    def by_layer(a, b):
        return jnp.where(first, a, b), send(jnp.where(first, b, a), swap)

    def chains(a, b):
        keep, got = by_layer(a, b)
        return jnp.where(first, jnp.stack([keep, got]), jnp.stack([got, keep]))[None]

    def scattered(total):
        dim = total.ndim - 2 if total.ndim > 1 else 0
        return lax.psum_scatter(total, "dp", scatter_dimension=dim, tiled=True).astype(F32)

    def summed(kind, axis):
        keep, got = by_layer(scattered(grads[0, kind]), scattered(grads[1, kind]))
        left, right = jnp.where(first, keep, got), jnp.where(first, got, keep)
        return jnp.concatenate([left, right], axis)

    def side_by_side(stack):
        return jnp.concatenate([stack[j] for j in range(stack.shape[0])], axis=1)[None]

    g_att, g_up, g_down = summed(0, 0), summed(1, 0), summed(2, 1)
    keep, got = by_layer(layers[0].grad_vec(), layers[1].grad_vec())
    g_vec = scattered((keep + got).reshape(-1))
    return (
        chains(*results),
        chains(dxs[0], dxs[1]),
        side_by_side(g_att[:3]),
        g_att[3][None],
        side_by_side(g_up),
        g_down[None],
        g_vec[None],
    )


def solution(mesh):
    placed = (
        P("dp", None, None),
        P("dp"),
        P("dp", None, None),
        P("section", "dp", None),
        P("section", "dp", None),
        P("section", "dp", None),
        P("section", "dp", None),
        P("section", "dp"),
    )
    return jax.shard_map(
        cube_body if mesh.shape["dp"] == 16 else plain_body,
        mesh=mesh,
        in_specs=placed,
        out_specs=(
            P("section", "dp", None, None),
            P("section", "dp", None, None),
            P("section", "dp", None),
            P("section", "dp", None),
            P("section", "dp", None),
            P("section", "dp", None),
            P("section", "dp"),
        ),
        check_vma=False,
    )
```

```python
import functools

import jax
import jax.numpy as jnp
from jax import lax
from jax.experimental import pallas as pl
from jax.experimental.pallas import tpu as pltpu
from jax.sharding import PartitionSpec as P

HEADS = 12
BF = jnp.bfloat16
F32 = jnp.float32
EPS = 1e-06
FILL = -1000000000.0
ROOT_HALF = 0.7071067811865476
INV_ROOT_TWO_PI = 0.3989422804014327
VMEM_BYTES = 24 * 1024 * 1024
ALL = ("section", "dp")
WINDOW = 1
DIRECT = 2
FLAT_GATHER = {5: 3}
FLAT_SUM = {}


def nn(a, b):
    return lax.dot_general(a, b, (((1,), (0,)), ((), ())), preferred_element_type=F32)


def nt(a, b):
    return lax.dot_general(a, b, (((1,), (1,)), ((), ())), preferred_element_type=F32)


def tn(a, b):
    return lax.dot_general(a, b, (((0,), (0,)), ((), ())), preferred_element_type=F32)


def norm(r, gain, shift):
    mean = jnp.mean(r, axis=-1, keepdims=True)
    cent = r - mean
    inv = lax.rsqrt(jnp.mean(cent * cent, axis=-1, keepdims=True) + EPS)
    n = cent * inv
    return n * gain + shift, n, inv


def norm_back(dy, n, inv, gain):
    t = dy * gain
    dr = inv * (
        t - jnp.mean(t, axis=-1, keepdims=True) - n * jnp.mean(t * n, axis=-1, keepdims=True)
    )
    return dr, jnp.sum(dy * n, axis=0, keepdims=True), jnp.sum(dy, axis=0, keepdims=True)


def load_weight(info, parts, dst, sem, stacked):
    if len(parts) == 1:
        copy = pltpu.make_async_copy(parts[0], dst, sem)
        copy.start()
        return copy
    blocks = sum(part.shape[0] for part in parts) // 2
    rows = parts[0].shape[-2]
    slot = 0
    for part in parts:
        for s in range(part.shape[0]):
            half = info[0] if slot < blocks else 1 - info[0]
            at = pl.ds(pl.multiple_of(info[2 + slot] * rows, 16), rows)
            if stacked:
                window = (pl.ds(2 * half, 2), at)
            else:
                cols = part.shape[-1]
                window = (at, pl.ds(pl.multiple_of(half * cols, 128), cols))
            pltpu.make_async_copy(part.at[s], dst.at[window], sem).start()
            slot += 1
    return pltpu.make_async_copy(dst, dst, sem)


def store_grad(info, src, outs, sem, stacked):
    if len(outs) == 1:
        copy = pltpu.make_async_copy(src, outs[0], sem)
        copy.start()
        return copy
    near = outs[1].shape[0]
    rows = outs[0].shape[-2]
    for out, base in ((outs[0], near), (outs[1], 0)):
        for s in range(out.shape[0]):
            at = pl.ds(pl.multiple_of(info[2 + base + s] * rows, 16), rows)
            window = (slice(None), at) if stacked else (at,)
            pltpu.make_async_copy(src.at[window], out.at[s], sem).start()
    return pltpu.make_async_copy(src, src, sem)


def attention_forward(n_w, info, x, vec, *refs):
    parts, refs = refs[:n_w], refs[n_w:]
    qkv, soft, pack, hidden, normed, inv, w, sem = refs
    load_weight(info, parts, w, sem, True).wait()
    xb = x[...]
    length, width = xb.shape
    q = (nn(xb, w[0]) + vec[0:1]).astype(BF)
    k = nn(xb, w[1]).astype(BF)
    v = (nn(xb, w[2]) + vec[1:2]).astype(BF)
    qkv[0] = q
    qkv[1] = k
    qkv[2] = v
    size = width // HEADS
    pair = 2 * size
    low_half = lax.broadcasted_iota(jnp.int32, (length, pair), 1) < size
    valid = lax.broadcasted_iota(jnp.int32, (length, length), 1) < info[1]
    for p in range(HEADS // 2):
        at = slice(p * pair, (p + 1) * pair)
        qp, kp, vp = q[:, at], k[:, at], v[:, at]
        sides = []
        for e in range(2):
            qm = jnp.where(low_half if e == 0 else ~low_half, qp, jnp.zeros_like(qp))
            s = jnp.where(valid, nt(qm, kp) * size ** (-0.5), FILL)
            ex = jnp.exp(s - jnp.max(s, axis=-1, keepdims=True))
            a = ex / jnp.sum(ex, axis=-1, keepdims=True)
            soft[2 * p + e] = a
            sides.append(nn(a.astype(BF), vp))
        pack[1, :, at] = jnp.where(low_half, sides[0], sides[1]).astype(BF)
    pack[0] = xb
    r = xb.astype(F32) + (nn(pack[1], w[3]) + vec[2:3])
    h, normed[...], inv[...] = norm(r, vec[3:4], vec[4:5])
    hidden[...] = h
    pack[2] = h.astype(BF)


def up_forward(n_w, info, pack, vec, *refs):
    parts, refs = refs[:n_w], refs[n_w:]
    act, slope, w, sem = refs
    load_weight(info, parts, w, sem, True).wait()
    hb = pack[2]
    for j in range(4):
        u = nn(hb, w[j]) + vec[8 + j : 9 + j]
        cdf = 0.5 * (1.0 + lax.erf(u * ROOT_HALF))
        act[:, j * u.shape[1] : (j + 1) * u.shape[1]] = (u * cdf).astype(BF)
        slope[j] = cdf + u * INV_ROOT_TWO_PI * jnp.exp(-0.5 * u * u)


def down_forward(n_w, info, act, hidden, vec, *refs):
    parts, refs = refs[:n_w], refs[n_w:]
    out, normed, inv, w, sem = refs
    load_weight(info, parts, w, sem, False).wait()
    r = hidden[...] + (nn(act[...], w[...]) + vec[5:6])
    out[...], normed[...], inv[...] = norm(r, vec[6:7], vec[7:8])


def down_backward(first, n_w, info, dy, normed, inv, slope, vec, *refs):
    parts, refs = refs[:n_w], refs[n_w:]
    dr, dz_keep, dz_give, du, du_give, dvec, w, sem = refs
    load = load_weight(info, parts, w, sem, False)
    g = dy[...].astype(F32)
    if not first:
        rows = lax.broadcasted_iota(jnp.int32, g.shape, 0)
        g = jnp.where(rows < info[1], g, 0.0)
    grad, dgain, dshift = norm_back(g, normed[...], inv[...], vec[6:7])
    dr[...] = grad
    dz = grad.astype(BF)
    dvec[0:1] = jnp.sum(dz.astype(F32), axis=0, keepdims=True)
    dvec[1:2] = dgain
    dvec[2:3] = dshift
    dvec[7:8] = jnp.zeros_like(dshift)
    half = dz.shape[1] // 2
    left, right = dz[:, :half], dz[:, half:]
    on_left = info[0] == 0
    dz_keep[...] = jnp.where(on_left, left, right)
    dz_give[...] = jnp.where(on_left, right, left)
    depth = dz.shape[1]
    load.wait()
    for j in range(4):
        at = slice(j * depth, (j + 1) * depth)
        low = (nt(dz, w[at]) * slope[j]).astype(BF)
        du[j] = low
        dvec[3 + j : 4 + j] = jnp.sum(low.astype(F32), axis=0, keepdims=True)
    for j in range(2):
        du_give[j] = du[2 * (1 - info[0]) + j]


def up_backward(n_w, info, du, dr, normed, inv, vec, *refs):
    parts, refs = refs[:n_w], refs[n_w:]
    dr1, dvec, w, sem = refs
    load_weight(info, parts, w, sem, True).wait()
    dh = dr[...]
    for j in range(4):
        dh += nt(du[j], w[j])
    grad, dgain, dshift = norm_back(dh, normed[...], inv[...], vec[3:4])
    dr1[...] = grad
    dvec[0:1] = jnp.sum(grad.astype(BF).astype(F32), axis=0, keepdims=True)
    dvec[1:2] = dgain
    dvec[2:3] = dshift
    dvec[3:8] = jnp.zeros((5, dshift.shape[1]), F32)


def attention_backward(n_w, info, dr1, qkv, soft, *refs):
    parts, refs = refs[:n_w], refs[n_w:]
    dx, side, side_give, dvec, w, sem = refs
    load = load_weight(info, parts, w, sem, True)
    db = dr1[...].astype(BF)
    load.wait()
    do = nt(db, w[3]).astype(BF)
    length, width = do.shape
    size = width // HEADS
    pair = 2 * size
    scale = size ** (-0.5)
    low_half = lax.broadcasted_iota(jnp.int32, (length, pair), 1) < size
    for p in range(HEADS // 2):
        at = slice(p * pair, (p + 1) * pair)
        qp, kp, vp, dop = qkv[0, :, at], qkv[1, :, at], qkv[2, :, at], do[:, at]
        dqs, dks, dvs = [], [], []
        for e in range(2):
            dom = jnp.where(low_half if e == 0 else ~low_half, dop, jnp.zeros_like(dop))
            a = soft[2 * p + e]
            da = nt(dom, vp)
            ds = (a * (da - jnp.sum(a * da, axis=-1, keepdims=True))).astype(BF)
            dvs.append(tn(a.astype(BF), dop))
            dqs.append(nn(ds, kp))
            dks.append(tn(ds, qp))
        side[0, :, at] = (jnp.where(low_half, dqs[0], dqs[1]) * scale).astype(BF)
        side[1, :, at] = (jnp.where(low_half, dks[0], dks[1]) * scale).astype(BF)
        side[2, :, at] = jnp.where(low_half, dvs[0], dvs[1]).astype(BF)
    side[3] = db
    total = dr1[...]
    for j in range(3):
        total += nt(side[j], w[j])
    dx[...] = total
    dvec[0:1] = jnp.sum(side[0].astype(F32), axis=0, keepdims=True)
    dvec[1:2] = jnp.sum(side[2].astype(F32), axis=0, keepdims=True)
    dvec[2:8] = jnp.zeros((6, width), F32)
    for j in range(2):
        side_give[j] = side[2 * (1 - info[0]) + j]


def down_weight(rows_too, info, act, act_other, dz, dz_other, *refs):
    if rows_too:
        extra, refs = refs[0], refs[1:]
    outs, (dw, sem) = refs[:-2], refs[-2:]
    right = jnp.concatenate([dz[...], dz_other[...]], axis=0)
    depth = dw.shape[0] // 4
    for j in range(4):
        at = slice(j * depth, (j + 1) * depth)
        left = jnp.concatenate([act[:, at], act_other[:, at]], axis=0)
        dw[at] = tn(left, right).astype(BF)
    if not rows_too:
        store_grad(info, dw, outs, sem, False).wait()
        return
    near = outs[1].shape[0]
    rows = dw.shape[0] // (2 * near)
    more = outs[0].shape[-2] - rows
    for out, base in ((outs[0], near), (outs[1], 0)):
        for s in range(out.shape[0]):
            owner = info[2 + base + s]
            at = pl.ds(pl.multiple_of(owner * rows, 16), rows)
            pltpu.make_async_copy(dw.at[at], out.at[s, pl.ds(0, rows)], sem).start()
            pltpu.make_async_copy(extra.at[owner], out.at[s, pl.ds(rows, more)], sem).start()
    pltpu.make_async_copy(dw, dw, sem).wait()
    pltpu.make_async_copy(extra, extra, sem).wait()


def up_weight(info, pack, pack_other, du, du_other, *refs):
    outs, (dw, sem) = refs[:-2], refs[-2:]
    left = jnp.concatenate([pack[2], pack_other[2]], axis=0)
    for j in range(2):
        right = jnp.concatenate([du[2 * info[0] + j], du_other[j]], axis=0)
        dw[j] = tn(left, right).astype(BF)
    store_grad(info, dw, outs, sem, True).wait()


def attention_weight(info, pack, pack_other, side, side_other, *refs):
    outs, (dw, sem) = refs[:-2], refs[-2:]
    left = jnp.concatenate([pack[0], pack_other[0]], axis=0)
    last = jnp.concatenate([pack[1], pack_other[1]], axis=0)
    for j in range(2):
        right = jnp.concatenate([side[2 * info[0] + j], side_other[j]], axis=0)
        if j == 1:
            left = jnp.where(info[0] == 0, left, last)
        dw[j] = tn(left, right).astype(BF)
    store_grad(info, dw, outs, sem, True).wait()


def call(kernel, info, small, parts, grads, outs, scratch, flops, nbytes):
    vmem = pl.BlockSpec(memory_space=pltpu.VMEM)
    hbm = pl.BlockSpec(memory_space=pl.ANY)
    shapes = [jax.ShapeDtypeStruct(s, BF) for s in grads]
    shapes += [jax.ShapeDtypeStruct(s, d) for s, d in outs]
    return pl.pallas_call(
        kernel,
        out_shape=shapes,
        in_specs=[pl.BlockSpec(memory_space=pltpu.SMEM)]
        + [vmem] * len(small)
        + [hbm] * len(parts),
        out_specs=[hbm] * len(grads) + [vmem] * len(outs),
        scratch_shapes=scratch,
        compiler_params=pltpu.CompilerParams(vmem_limit_bytes=VMEM_BYTES),
        cost_estimate=pl.CostEstimate(flops=1, bytes_accessed=1, transcendentals=0),
    )(info, *small, *parts)


class Layer:
    def __init__(self, info, vec, length, width):
        self.info, self.vec = info, vec
        self.length, self.width = length, width
        self.row = ((length, width), F32)
        self.low = ((length, width), BF)
        self.col = ((length, 1), F32)
        self.wide = (4, length, width)
        self.two = ((2, length, width), BF)
        self.half = ((length, width // 2), BF)
        self.size = 2 * length * width * width
        self.stack = pltpu.VMEM((4, width, width), BF)
        self.tall = pltpu.VMEM((4 * width, width), BF)
        self.bytes = 4 * width * width * 2
        self.sem = pltpu.SemaphoreType.DMA
        self.dvec = ((8, width), F32)
        self.other = {}

    def run(self, kernel, parts, small, outs, scratch, mults, grads=()):
        if parts:
            kernel = functools.partial(kernel, len(parts))
        return call(
            kernel, self.info, small, parts, grads, outs, scratch + [self.sem],
            mults * self.size, self.bytes,
        )

    def attention(self, x, parts):
        outs = [((3,) + self.low[0], BF), ((HEADS, self.length, self.length), F32)]
        outs += [((3,) + self.low[0], BF), self.row, self.row, self.col]
        got = self.run(attention_forward, parts, [x, self.vec], outs, [self.stack], 5)
        self.qkv, self.soft, self.pack, self.hidden, self.n1, self.s1 = got
        return self.pack

    def up(self, pack, parts):
        self.act, self.slope = self.run(
            up_forward, parts, [pack, self.vec],
            [((self.length, 4 * self.width), BF), (self.wide, F32)],
            [self.stack], 4,
        )
        return self.act

    def down(self, act, parts):
        out, self.n2, self.s2 = self.run(
            down_forward, parts, [act, self.hidden, self.vec], [self.row, self.row, self.col],
            [self.tall], 4,
        )
        return out

    def down_back(self, first, dy, parts):
        got = self.run(
            functools.partial(down_backward, first), parts,
            [dy, self.n2, self.s2, self.slope, self.vec],
            [self.row, self.half, self.half, (self.wide, BF), self.two, self.dvec],
            [self.tall], 4,
        )
        self.dr, self.dz, dz_give, self.du, du_give, self.dvec_down = got
        return dz_give, du_give

    def up_back(self, parts):
        self.dr1, self.dvec_up = self.run(
            up_backward, parts, [self.du, self.dr, self.n1, self.s1, self.vec],
            [self.row, self.dvec], [self.stack], 4,
        )

    def attention_back(self, dr1, parts):
        self.dx, self.side, give, self.dvec_att = self.run(
            attention_backward, parts, [dr1, self.qkv, self.soft],
            [self.row, (self.wide, BF), self.two, self.dvec], [self.stack], 7,
        )
        return give

    def weight(self, kind, grads, extra=()):
        o = self.other
        stack = pltpu.VMEM((2, self.width, self.width), BF)
        if kind == 2:
            stack = pltpu.VMEM((4 * self.width, self.width // 2), BF)
            small = [self.act, o["act"], self.dz, o["dz"], *extra]
            kernel = functools.partial(down_weight, len(extra) > 0)
        elif kind == 1:
            small = [self.pack, o["pack"], self.du, o["du"]]
            kernel = up_weight
        else:
            small = [self.pack, o["pack"], self.side, o["side"]]
            kernel = attention_weight
        return self.run(kernel, [], small, [], [stack], 4, grads)

    def grad_vec(self):
        d, u, a = self.dvec_down, self.dvec_up, self.dvec_att
        return jnp.concatenate([a[0:2], u[0:3], d[0:7]], axis=0)


def route(move):
    size = lax.axis_size("dp")
    pairs = []
    for s in range(2):
        for d in range(size):
            to_s, to_d = move(s, d)
            pairs.append((s * size + d, to_s * size + to_d))
    return pairs


def send(v, pairs):
    return lax.ppermute(v, ALL, pairs)


def after(v, *others):
    return lax.optimization_barrier((v,) + others)[0]


def cube_routes():
    return (
        route(lambda s, d: (s, d ^ (1 if s == 0 else 2))),
        route(lambda s, d: (s, d ^ (2 if s == 0 else 1))),
    )


def cube_owners(core, me, flat_first):
    slot = jnp.arange(16)
    third = jnp.where(core == 0, 1, 2)

    def table(a, b):
        masks = (a, 8, 4, b) if flat_first else (8, 4, a, b)
        return me ^ sum(((slot >> i) & 1) * m for i, m in enumerate(masks))

    return jnp.concatenate([table(third, 3 - third), table(3 - third, third)]).astype(jnp.int32)


def swap_route():
    return route(lambda s, d: (1 - s, d))


def cube_body(tokens, lengths, cotangent, w_qkv, w_out, w_up, w_down, vectors):
    core = lax.axis_index("section")
    me = lax.axis_index("dp")
    first = core == 0
    _, length, width = tokens.shape
    rows = w_out.shape[1]
    third, last = cube_routes()
    swap = swap_route()
    z_routes = {
        j: route(lambda s, d, m=m: (s, d ^ m)) for j, m in ((1, 8), (2, 4), (3, 12))
    }
    vec_sum_routes = [route(lambda s, d, i=i: (s, d ^ (1 << i))) for i in range(4)]

    def chunks(w):
        return jnp.stack([w[:, j * width : (j + 1) * width] for j in range(w.shape[1] // width)])

    blocks = [None] * 6
    own = [jnp.concatenate([chunks(w_qkv[0]), w_out])]

    def split(p):
        n = own[p].shape[0] // 2
        mine = lax.dynamic_slice_in_dim(own[p], n * core, n, 0)
        other = lax.dynamic_slice_in_dim(own[p], n * (1 - core), n, 0)
        return (mine, other) if n > 1 else (mine[0], other[0])

    def place(p, mine, other):
        blocks[p] = jnp.where(first, mine, other)
        blocks[p + 3] = jnp.where(first, other, mine)

    infos = [
        jnp.concatenate([core[None], lengths[core][None], cube_owners(core, me, flat)])
        for flat in (False, True)
    ]
    infos = [info.astype(jnp.int32) for info in infos]
    layers = [Layer(infos[0], None, length, width) for l in range(2)]

    history = [[], []]
    now = []

    def tie(*values, extra=()):
        deps = history[WINDOW] + list(extra)
        return lax.optimization_barrier(tuple(values) + tuple(deps))[: len(values)]

    gate = []

    slow, older = [[], []], []

    def sends(items, extra=(), long=False, over=False):
        more = [] if long else older if over else slow[0]
        values = tie(*[v for v, _ in items], extra=list(extra) + more)
        gate.extend(values)
        got = [send(v, pairs) for v, (_, pairs) in zip(values, items)]
        (slow[1] if long else now).extend(got)
        return got

    def step_end():
        history[:] = [history[1], list(now)]
        now[:] = []
        gate[:] = []
        older[:] = slow[0]
        slow[:] = [slow[1], []]

    parts = {}
    results = []
    exchange = []

    def forward(p, v):
        l, kind = divmod(p, 3)
        layer = layers[l]
        layer.info = infos[p in FLAT_GATHER]
        (v,) = tie(v, extra=gate)
        if kind == 0:
            v = layer.attention(v, parts[p])
            exchange.append((l, "pack", v))
        elif kind == 1:
            v = layer.up(v, parts[p])
            exchange.append((l, "act", v))
        else:
            v = layer.down(v, parts[p])
            results.append(v)
            v = v.astype(BF)
        now.append(v)
        return v

    rest, swapped = {}, {}
    n = len(blocks)
    halves = [split(0)]
    w_up, w_down, vectors, tokens, cotangent = lax.optimization_barrier(
        (w_up, w_down, vectors, tokens, cotangent, halves[0][1])
    )[:5]
    own.append(chunks(w_up[0]))
    own.append(jnp.stack([w_down[0][:, : width // 2], w_down[0][:, width // 2 :]]))
    halves += [split(1), split(2)]
    x = lax.dynamic_index_in_dim(tokens, core, 0, keepdims=False)
    cot = lax.dynamic_index_in_dim(cotangent, core, 0, keepdims=False)
    vec = jnp.stack([vectors[0], send(vectors[0], swap)])
    vec = jnp.where(first, vec, vec[::-1])
    vec_stages = {
        -1: [(3, z_routes[1]), (2, z_routes[2])],
        0: [(0, vec_sum_routes[0]), (1, vec_sum_routes[1])],
    }
    plan = {}

    def at_step(t, *item):
        plan.setdefault(t, []).append(item)

    for p in range(n):
        at_step(p + 1, "last", p, last)
        if p < DIRECT:
            for j in (1, 2, 3):
                at_step(p - 1, "z", p, z_routes[j])
            at_step(p, "flat", p, third)
        elif p in FLAT_GATHER:
            at_step(FLAT_GATHER[p], "flat", p, third)
            at_step(p - 1, "tall", p, z_routes[1])
            at_step(p, "tall", p, z_routes[2])
        else:
            early = p - 2 if p < 4 else p - 3
            at_step(early, "tall", p, z_routes[1])
            at_step(early + 1, "tall", p, z_routes[2])
            at_step(p, "flat", p, third)
        at_step(min(p + 3, n + 1), "late", p, swap)
        at_step(p + 1, "swapped", p, swap)

    for p in range(2):
        place(p, halves[p][0], send(halves[p][1], swap))
    here = dict(enumerate(blocks))
    joins = []
    for t in range(-1, n + 3):
        flat = [v for _, _, arrays, _ in joins for v in arrays]
        tied = list(tie(*flat)) if flat else []
        for where, q, arrays, join in joins:
            where[q] = join([tied.pop(0) for _ in arrays])
        joins = []
        todo = []
        for name, p, pairs in plan.get(t, []):
            todo.append((name, p, rest[p] if name == "late" else here[p], pairs))
        if t == -1:
            todo.append(("own", 2, halves[2][1], swap))
        for l, name, v in exchange:
            todo.append((name, l, v, swap))
        exchange.clear()
        long = [item for item in todo if item[0] == "last"]
        todo = [item for item in todo if item[0] != "last"]
        got = sends([item[2:] for item in long], long=True) if long else []
        got = got + (sends([item[2:] for item in todo], over=True) if todo else [])
        todo = long + todo
        for (name, q, _, _), v in zip(todo, got):
            if name == "late":
                parts[q] = [here[q], rest[q], swapped[q], v]
        for bit, pairs in vec_stages.get(t, []):
            (v,) = sends([(vec, pairs)], [blocks[0]])
            upper = (me >> bit) & 1 == 1
            vec = jnp.where(upper, jnp.stack([v, vec]), jnp.stack([vec, v]))
        if t == 0:
            vec = vec.transpose(4, 3, 2, 0, 1, 5).reshape(2, -1, width).astype(F32)
            layers[0].vec, layers[1].vec = vec[0], vec[1]
        if t >= 3:
            x = forward(t - 3, x)
        straight = {}
        for (name, q, _, _), v in zip(todo, got):
            if name == "last":
                rest[q] = v
            elif name == "z":
                straight.setdefault(q, [blocks[q]]).append(v)
            elif name == "swapped":
                swapped[q] = v
            elif name == "own":
                place(q, halves[q][0], v)
                here[q], here[q + 3] = blocks[q], blocks[q + 3]
            elif name in ("flat", "tall"):
                one = here[q].shape == blocks[q].shape
                joins.append((here, q, [here[q], v], jnp.stack if one else jnp.concatenate))
            elif name != "late":
                layers[q].other[name] = v
        for q, arrays in straight.items():
            joins.append((here, q, arrays, jnp.stack))
        step_end()

    order = [(1, 2), (1, 1), (1, 0), (0, 1), (0, 0), (0, 2)]
    dxs = {}

    def chain(l, kind):
        layer = layers[l]
        layer.info = infos[3 * l + kind in FLAT_GATHER]
        if kind == 2:
            dy = cot if l == 1 else dxs[1].astype(BF)
            (dy,) = tie(dy, extra=gate)
            dz, du = layer.down_back(l == 0, dy, parts[3 * l + 2])
            layer.other["dz"], layer.other["du"] = send(dz, swap), send(du, swap)
            now.append(layer.dr)
        elif kind == 1:
            (layer.dr,) = tie(layer.dr, extra=gate if l == 0 else ())
            layer.up_back(parts[3 * l + 1])
            now.append(layer.dr1)
        else:
            (dr1,) = tie(layer.dr1, extra=gate)
            layer.other["side"] = send(layer.attention_back(dr1, parts[3 * l]), swap)
            dxs[l] = layer.dx
            now.append(layer.dx)

    def weight(l, kind):
        shape = (8,) + blocks[kind].shape
        extra = ()
        if (l, kind) == order[-1]:
            keep, give = by_layer(layers[0].grad_vec(), layers[1].grad_vec())
            (got,) = sends([(give, swap)])
            entries = (keep + got).reshape(16, 2, -1).astype(BF)
            pad = shape[-1] - entries.shape[-1]
            extra = (jnp.pad(entries, ((0, 0), (0, 14), (0, pad))),)
            shape = (8, shape[1] + 16, shape[2])
        layers[l].info = infos[order.index((l, kind)) in FLAT_SUM]
        give, keep = layers[l].weight(kind, [shape, shape], extra)
        terms.append([keep])
        gives.append(give)
        now.extend([give, keep])

    def by_layer(a, b):
        return jnp.where(first, a, b), jnp.where(first, b, a)

    terms, gives = [], []
    work = [
        [(chain, 1, 2), (weight, 1, 2)],
        [(weight, 1, 1), (chain, 1, 1)],
        [(chain, 1, 0), (weight, 1, 0)],
        [(chain, 0, 2), (weight, 0, 1), (chain, 0, 1)],
        [(chain, 0, 0), (weight, 0, 0)],
        [(weight, 0, 2)],
    ]

    def part(arrays, lo, hi, kind):
        total = arrays[0][lo:hi].astype(F32)
        for v in arrays[1:]:
            total = total + v[lo:hi].astype(F32)
        return total.astype(kind)

    z_low, z_high = z_routes[2], z_routes[1]
    plan = {}
    for q in range(len(order)):
        steps = [(q + 1, last)]
        if q in FLAT_SUM:
            steps += [(q + 2, z_low), (q + 3, z_high), (FLAT_SUM[q], third)]
        else:
            steps += [(q + 2, third), (q + 3, None)]
        left = 16
        for t, pairs in steps:
            plan.setdefault(t, []).append((q, left, pairs))
            left //= 2

    sums = {}
    acts_keep, acts_give = by_layer(*results)
    extra = [("acts", acts_give)]
    kept = {"acts": acts_keep}
    got_extra = {}
    total_vec = None
    for t in range(len(order) + 4):
        todo = []
        for q, left, pairs in plan.get(t, []):
            if left == 16:
                todo.append(("long", q, gives[q], pairs))
                continue
            arrays = tie(*terms[q])
            if pairs is None:
                for j in (1, 2, 3):
                    todo.append(("tall", q, part(arrays, j, j + 1, BF), z_routes[j]))
            else:
                name = "flat" if pairs is third else "tall"
                todo.append((name, q, part(arrays, left // 2, left, BF), pairs))
        for name, v in extra:
            todo.append((name, 0, v, swap))
        extra = []
        long = [item for item in todo if item[0] == "long"]
        todo = [item for item in todo if item[0] != "long"]
        got = sends([item[2:] for item in long], long=True) if long else []
        got = got + (sends([item[2:] for item in todo]) if todo else [])
        todo = long + todo
        for f, l, kind in work[t] if t < len(work) else []:
            f(l, kind)
        step_end()
        for (name, q, _, _), v in zip(todo, got):
            if name in ("flat", "tall", "long"):
                terms[q].append(v)
            else:
                got_extra[name] = v
        if t == 4:
            kept["dx"], give_v = by_layer(dxs[0], dxs[1])
            extra.append(("dx", give_v))
        for q, left, pairs in plan.get(t, []):
            if left > 2 and pairs is not None:
                continue
            sums[order[q]] = part(terms[q], 0, 1, F32)[0]
            l, kind = order[q]
            if (1 - l, kind) not in sums:
                continue
            mine = sums[0, kind]
            if order[-1] == (0, kind):
                n_rows = blocks[kind].shape[0]
                total_vec = mine[n_rows : n_rows + 2, : vectors.shape[1] // 2].reshape(1, -1)
                mine = mine[:n_rows]
            kept[kind], give_v = by_layer(mine, sums[1, kind])
            extra.append((kind, give_v))
        if t == len(order) + 1:
            for name in ("acts", "dx"):
                kept[name], got_extra[name] = tie(kept[name], got_extra[name])

    def joined(name, axis):
        a, b = kept[name], got_extra[name]
        if axis is None:
            return jnp.where(first, jnp.stack([a, b]), jnp.stack([b, a]))
        return jnp.where(first, jnp.concatenate([a, b], axis), jnp.concatenate([b, a], axis))

    acts = joined("acts", None)[None]
    grads_in = joined("dx", None)[None]
    whole = [joined(0, 0), joined(1, 0), joined(2, 1)]

    def side_by_side(stack):
        return jnp.concatenate([stack[j] for j in range(stack.shape[0])], axis=1)[None]

    return (
        acts,
        grads_in,
        side_by_side(whole[0][:3]),
        whole[0][3][None],
        side_by_side(whole[1]),
        whole[2][None],
        total_vec,
    )


def plain_body(tokens, lengths, cotangent, w_qkv, w_out, w_up, w_down, vectors):
    core = lax.axis_index("section")
    first = core == 0
    chains_dev, length, width = tokens.shape
    swap = swap_route()
    size = lax.axis_size("dp")
    rows = w_out.shape[1]

    def gathered(w):
        return lax.all_gather(w, "dp", axis=0, tiled=True)

    def both(v):
        got = send(v, swap)
        return jnp.where(first, v, got), jnp.where(first, got, v)

    def chunks(w):
        return jnp.stack([w[:, j * width : (j + 1) * width] for j in range(w.shape[1] // width)])

    att = jnp.concatenate([chunks(gathered(w_qkv[0])), gathered(w_out[0])[None]])
    up = chunks(gathered(w_up[0]))
    down = gathered(w_down[0])
    vec = gathered(vectors[0]).reshape(-1, width).astype(F32)
    att, up, down, vec = both(att), both(up), both(down), both(vec)
    info = jnp.stack([core, lengths[core]]).astype(jnp.int32)
    layers = [Layer(info, vec[l], length, width) for l in range(2)]
    x = lax.dynamic_index_in_dim(tokens, core, 0, keepdims=False)
    dy = lax.dynamic_index_in_dim(cotangent, core, 0, keepdims=False)
    results = []
    for l in range(2):
        layer = layers[l]
        pack = layer.attention(x, [att[l]])
        act = layer.up(pack, [up[l]])
        layer.other["pack"], layer.other["act"] = send(pack, swap), send(act, swap)
        y = layer.down(act, [down[l]])
        results.append(y)
        x = y.astype(BF)
    stacked, tall = [(2, width, width)], [(4 * width, width // 2)]
    grads = {}
    dxs = {}
    for l in (1, 0):
        layer = layers[l]
        dz, du = layer.down_back(l == 0, dy, [down[l]])
        layer.other["dz"], layer.other["du"] = send(dz, swap), send(du, swap)
        layer.up_back([up[l]])
        layer.other["side"] = send(layer.attention_back(layer.dr1, [att[l]]), swap)
        for kind in range(3):
            (grads[l, kind],) = layer.weight(kind, tall if kind == 2 else stacked)
        dxs[l] = layer.dx
        dy = layer.dx.astype(BF)

    def by_layer(a, b):
        return jnp.where(first, a, b), send(jnp.where(first, b, a), swap)

    def chains(a, b):
        keep, got = by_layer(a, b)
        return jnp.where(first, jnp.stack([keep, got]), jnp.stack([got, keep]))[None]

    def scattered(total):
        dim = total.ndim - 2 if total.ndim > 1 else 0
        return lax.psum_scatter(total, "dp", scatter_dimension=dim, tiled=True).astype(F32)

    def summed(kind, axis):
        keep, got = by_layer(scattered(grads[0, kind]), scattered(grads[1, kind]))
        left, right = jnp.where(first, keep, got), jnp.where(first, got, keep)
        return jnp.concatenate([left, right], axis)

    def side_by_side(stack):
        return jnp.concatenate([stack[j] for j in range(stack.shape[0])], axis=1)[None]

    g_att, g_up, g_down = summed(0, 0), summed(1, 0), summed(2, 1)
    keep, got = by_layer(layers[0].grad_vec(), layers[1].grad_vec())
    g_vec = scattered((keep + got).reshape(-1))
    return (
        chains(*results),
        chains(dxs[0], dxs[1]),
        side_by_side(g_att[:3]),
        g_att[3][None],
        side_by_side(g_up),
        g_down[None],
        g_vec[None],
    )


def solution(mesh):
    placed = (
        P("dp", None, None),
        P("dp"),
        P("dp", None, None),
        P("section", "dp", None),
        P("section", "dp", None),
        P("section", "dp", None),
        P("section", "dp", None),
        P("section", "dp"),
    )
    return jax.shard_map(
        cube_body if mesh.shape["dp"] == 16 else plain_body,
        mesh=mesh,
        in_specs=placed,
        out_specs=(
            P("section", "dp", None, None),
            P("section", "dp", None, None),
            P("section", "dp", None),
            P("section", "dp", None),
            P("section", "dp", None),
            P("section", "dp", None),
            P("section", "dp"),
        ),
        check_vma=False,
    )
```
